128 devices in a mesh: frames: 32 (over z, x, core), rows: 4 (over y).
Axes of the slice: x: 4, y: 4, z: 4, core: 2. Of those that a mesh axis runs over, the one named last changes fastest.
Arguments:
- latents: bfloat16 [128, 32, 18, 1280], P('frames', 'rows')
- first_gain: float32 [1280], replicated, may hold values from 0.1 to 1.9
- first_shift: float32 [1280], replicated, may hold values from -3 to 3
- spatial_kernel: bfloat16 [3, 3, 1280, 1280], P(None, None, 'frames'), may hold values from -0.0546875 to 0.0546875
- spatial_bias: float32 [1280], replicated, may hold values from -2 to 2
- second_gain: float32 [1280], replicated, may hold values from 0.1 to 1.9
- second_shift: float32 [1280], replicated, may hold values from -3 to 3
- temporal_kernel: bfloat16 [3, 1280, 1280], replicated, may hold values from -0.09375 to 0.09375
- temporal_bias: float32 [1280], replicated, may hold values from -2 to 2
- frame_slot: int32 [100], replicated, may hold values from 0 to 127, as said below
Outputs:
- block_output: bfloat16 [128, 32, 18, 1280], P('frames', 'rows')
The draws below stay inside these ranges and needn't reach their ends.
Inputs may be any that keep to these rules, and one draw needn't show every extreme that they name: `frame_slot`: the 100 entries are distinct; device i of frames holds slots i * 4 to (i + 1) * 4 - 1; in every draw all 4 slots of some device are used, and slots 0 and 127 are used.
All inputs are finite; a program needn't handle non-finite values.
Results may differ from the reference program's by a relative error of at most 0.0018.
The reference program's roundings to bfloat16 on the way (of `frames_in`, `hidden_one`, `spatial`, `hidden_two` and `mixed`) count: a program that leaves them out, or rounds other values in their place, can miss the bound.
Values may be sent and summed in bfloat16 or wider, within the bound.
A program may use at most 320 MiB of HBM per device.

```python
import jax
import jax.numpy as jnp
from jax import lax

C = 1280
FRAMES = 25
GROUPS = 32
LROWS = 32
LCOLS = 18
VIDEOS = 4
TOTAL = 100
FSLOT = 4
SLOTS = 128


def draw_latents(key, part):
    key = jax.random.fold_in(key, 11)
    base_key, channel_key, slot_key = jax.random.split(key, 3)
    array_shape = (SLOTS, LROWS, LCOLS, C)
    channel_scale = jnp.exp(jax.random.uniform(channel_key, (C,), jnp.float32, 0.0, 2.3)) / 3.0
    slot_scale = jnp.exp(jax.random.uniform(slot_key, (SLOTS, 1, 1, 1), jnp.float32, -0.7, 0.7))
    values = jax.random.normal(base_key, array_shape, jnp.float32) * channel_scale * slot_scale
    return values.astype(jnp.bfloat16)


def draw_frame_slot(key, part):
    key = jax.random.fold_in(key, 23)
    order_key, device_key = jax.random.split(key)
    shuffled = jax.random.permutation(order_key, SLOTS).astype(jnp.int32)
    chosen_device = jax.random.randint(device_key, (), 0, SLOTS // FSLOT, dtype=jnp.int32)
    position = jnp.arange(SLOTS, dtype=jnp.int32)
    forced = ((shuffled == 0) | (shuffled == SLOTS - 1)).astype(jnp.int32)
    filled_device = (shuffled // FSLOT == chosen_device).astype(jnp.int32)
    priority = position - SLOTS * forced - 2 * SLOTS * filled_device
    ranked = jnp.argsort(priority, stable=True)
    return shuffled[ranked][:TOTAL]


def block_scale(stream_key, shape, cuts, least, high):
    level = 1.0
    for axis_at, blocks in cuts:
        heights = jax.random.uniform(jax.random.fold_in(jax.random.fold_in(stream_key, 6), axis_at), (blocks,), jnp.float32, least / len(cuts), high / len(cuts))
        level = level * jnp.repeat(jnp.exp(heights), shape[axis_at] // blocks).reshape((-1,) + (1,) * (len(shape) - 1 - axis_at))
    return level


def noise(own_key, dims, width, most, cuts=(), kind=jnp.bfloat16):
    entries = width * jax.random.normal(own_key, dims, jnp.float32)
    if cuts:
        entries = entries * block_scale(own_key, dims, cuts, -0.22, 0.18)
    return jnp.clip(entries, -most, most).astype(kind)


def setup_inputs(seed: int = 0) -> dict:
    splits = jax.random.split(jax.random.key(seed), 11)
    latents = draw_latents(jax.random.fold_in(splits[10], 71), 0)
    first_gain = jnp.clip(1.0 + 0.18 * jax.random.normal(splits[1], (C,), jnp.float32), 0.1, 1.9)
    first_shift = noise(splits[2], (C,), 0.5, 3.0, (), jnp.float32)
    spatial_kernel = noise(splits[3], (3, 3, C, C), (9 * C) ** -0.5, 0.0546875, ((2, 32),))
    spatial_bias = noise(splits[4], (C,), 0.3, 2.0, (), jnp.float32)
    second_gain = jnp.clip(1.0 + 0.18 * jax.random.normal(splits[5], (C,), jnp.float32), 0.1, 1.9)
    second_shift = noise(splits[6], (C,), 0.5, 3.0, (), jnp.float32)
    temporal_kernel = noise(splits[7], (3, C, C), (3 * C) ** -0.5, 0.09375)
    temporal_bias = noise(splits[8], (C,), 0.3, 2.0, (), jnp.float32)
    frame_slot = draw_frame_slot(jax.random.fold_in(splits[10], 71), 0)
    return {"latents": latents, "first_gain": first_gain, "first_shift": first_shift, "spatial_kernel": spatial_kernel, "spatial_bias": spatial_bias, "second_gain": second_gain, "second_shift": second_shift, "temporal_kernel": temporal_kernel, "temporal_bias": temporal_bias, "frame_slot": frame_slot}


norm_epsilon = 1e-06

def norm_silu(values, gain, shift):
    full_shape = values.shape
    grouped = values.reshape((full_shape[0], -1, GROUPS, full_shape[-1] // GROUPS))
    average = lax.optimization_barrier(jnp.mean(grouped, axis=(1, 3), keepdims=True))
    squares = lax.optimization_barrier(jnp.mean(grouped * grouped, axis=(1, 3), keepdims=True))
    scaled = (grouped - average) * lax.rsqrt(squares - average * average + norm_epsilon)
    return jax.nn.silu(scaled.reshape(full_shape) * gain + shift).astype(jnp.bfloat16)

def reference(latents, first_gain, first_shift, spatial_kernel, spatial_bias, second_gain, second_shift, temporal_kernel, temporal_bias, frame_slot):
    frames_in = latents[frame_slot]
    hidden_one = norm_silu(frames_in.astype(jnp.float32), first_gain, first_shift)
    padded = jnp.pad(hidden_one, ((0, 0), (1, 1), (1, 1), (0, 0)))
    summed = jnp.zeros((TOTAL * LROWS * LCOLS, C), jnp.float32)
    for row_tap in range(3):
        for col_tap in range(3):
            window = padded[:, row_tap:row_tap + LROWS, col_tap:col_tap + LCOLS, :].reshape(-1, C)
            summed = summed + jnp.dot(window, spatial_kernel[row_tap, col_tap], preferred_element_type=jnp.float32)
    spatial = (frames_in.astype(jnp.float32) + summed.reshape(frames_in.shape) + spatial_bias).astype(jnp.bfloat16)
    clips = spatial.reshape(VIDEOS, FRAMES, LROWS * LCOLS, C)
    hidden_two = norm_silu(clips.astype(jnp.float32), second_gain, second_shift)
    extended = jnp.pad(hidden_two, ((0, 0), (1, 1), (0, 0), (0, 0)))
    temporal = jnp.zeros((TOTAL * LROWS * LCOLS, C), jnp.float32)
    for frame_tap in range(3):
        window = extended[:, frame_tap:frame_tap + FRAMES].reshape(-1, C)
        temporal = temporal + jnp.dot(window, temporal_kernel[frame_tap], preferred_element_type=jnp.float32)
    mixed = (clips.astype(jnp.float32) + temporal.reshape(clips.shape) + temporal_bias).astype(jnp.bfloat16)
    placed = jnp.zeros((SLOTS, LROWS, LCOLS, C), jnp.bfloat16)
    return placed.at[frame_slot].set(mixed.reshape(TOTAL, LROWS, LCOLS, C))
```

```python
import jax
import jax.numpy as jnp
from jax import lax
from jax.experimental import pallas as pl
from jax.experimental.pallas import tpu as pltpu
from jax.sharding import PartitionSpec as P

FRAMES = 25
GROUPS = 32
EPS = 1e-06
MESH = pl.DeviceIdType.MESH
C = 1280
LANES = 10
STAGES = 5
PITCH = 24
KINDS = 24


def group_indicator(tile):
    channel = lax.broadcasted_iota(jnp.int32, (128, 128), 0) + tile * 128
    first = lax.broadcasted_iota(jnp.int32, (128, 128), 1) * 40
    return jnp.where((channel >= first) & (channel < first + 40), 1.0, 0.0)


def group_indicator_t(tile):
    channel = lax.broadcasted_iota(jnp.int32, (128, 128), 1) + tile * 128
    first = lax.broadcasted_iota(jnp.int32, (128, 128), 0) * 40
    return jnp.where((channel >= first) & (channel < first + 40), 1.0, 0.0)


def exact_dot(a, b):
    return jnp.dot(a, b, preferred_element_type=jnp.float32, precision=lax.Precision.HIGHEST)


def spatial_kernel_body(
    lat,
    gain,
    shift,
    wk,
    bias,
    out,
    G,
    X,
    F,
    R,
    halo,
    RM,
    acc,
    pieces,
    stats,
    scales,
    send,
    recv,
    piece_send,
    piece_recv,
    piece_own,
    small_send,
    small_recv,
    lat_sem,
):
    fr = lax.axis_index("frames")
    y = lax.axis_index("rows")
    core = lax.rem(fr, 2)
    chip = lax.div(fr, 2)
    x = lax.rem(chip, 4)
    z = lax.div(chip, 4)
    u = x + core * (z - x)
    w = z + core * (x - z)
    par = lax.rem(y, 2)

    def wrap(v):
        return lax.rem(v + 4, 4)

    def same_core(u_, w_):
        return (((w_ + core * (u_ - w_)) * 4) + u_ + core * (w_ - u_)) * 2 + core

    u_up = {"frames": same_core(wrap(u + 1), w)}
    u_dn = {"frames": same_core(wrap(u - 1), w)}
    w_up = {"frames": same_core(u, wrap(w + 1))}
    w_dn = {"frames": same_core(u, wrap(w - 1))}
    sib = {"frames": fr + 1 - 2 * core}
    y_up = {"rows": wrap(y + 1)}
    y_dn = {"rows": wrap(y - 1)}
    y_op = {"rows": wrap(y + 2)}
    barrier = pltpu.get_barrier_semaphore()
    for peer in (u_up, u_dn, w_up, w_dn, sib, y_up, y_dn, y_op):
        pl.semaphore_signal(barrier, inc=1, device_id=peer, device_id_type=MESH)
    pl.semaphore_wait(barrier, 8)

    plane_tap = 3 * par

    def piece_copy(s):
        return pltpu.make_async_remote_copy(
            src_ref=wk.at[pl.ds(plane_tap, 6), :, pl.ds(pl.multiple_of(256 * s + 128 * (1 - core), 128), 128)],
            dst_ref=pieces.at[s, core],
            send_sem=piece_send.at[s],
            recv_sem=piece_recv.at[s],
            device_id=sib,
            device_id_type=MESH,
        )

    def piece_arrived(s):
        return pltpu.make_async_remote_copy(
            src_ref=pieces.at[s, 1 - core],
            dst_ref=pieces.at[s, 1 - core],
            send_sem=piece_send.at[s],
            recv_sem=piece_recv.at[s],
            device_id=sib,
            device_id_type=MESH,
        )

    def piece_local(s):
        return pltpu.make_async_copy(
            wk.at[pl.ds(plane_tap, 6), :, pl.ds(pl.multiple_of(256 * s + 128 * core, 128), 128)],
            pieces.at[s, core],
            piece_own.at[s],
        )

    for s in range(STAGES):
        piece_copy(s).start()
        piece_local(s).start()
    lat_copy = pltpu.make_async_copy(lat, R, lat_sem)
    lat_copy.start()

    def small(src, dst, k, target):
        return pltpu.make_async_remote_copy(
            src_ref=src,
            dst_ref=dst,
            send_sem=small_send.at[k],
            recv_sem=small_recv.at[k],
            device_id=target,
            device_id_type=MESH,
        )

    small(lat.at[:, 7], halo.at[0], 0, y_up).start()
    small(lat.at[:, 0], halo.at[1], 1, y_dn).start()

    def region(q, row, u0, count, tap, taps):
        return G.at[q, row, pl.ds(u0, count), pl.ds(tap, taps)]

    def mover(k, s, ref, target):
        return pltpu.make_async_remote_copy(
            src_ref=ref,
            dst_ref=ref,
            send_sem=send.at[s, k],
            recv_sem=recv.at[s, k],
            device_id=target,
            device_id_type=MESH,
        )

    rows = [w, wrap(w - 1), wrap(w + 1), wrap(w + 2)]
    sib_rows = [u, wrap(u - 1), wrap(u + 1), wrap(u + 2)]
    out_tap = 6 * par
    in_tap = 6 * (1 - par)
    pending = []

    def go(k, s, ref, target):
        copy = mover(k, s, ref, target)
        copy.start()
        pending.append(copy)

    def arrived(k, s, ref, source):
        mover(k, s, ref, source).wait_recv()

    def spread(i, s):
        q = 2 * s + core
        go(8 + 2 * i, s, region(q, rows[i], 0, 2, out_tap, 3), y_up)
        go(9 + 2 * i, s, region(q, rows[i], 2, 2, out_tap, 3), y_dn)
        go(16 + i, s, region(q, rows[i], 0, 4, plane_tap, 6), sib)

    def event0(s):
        piece_local(s).wait()
        piece_arrived(s).wait_recv()
        q = 2 * s + core

        def one(t, carry):
            both = jnp.concatenate(
                [pieces[s, 0, t].astype(jnp.float32), pieces[s, 1, t].astype(jnp.float32)], axis=0
            )
            G[q, w, u, plane_tap + t] = both.astype(jnp.bfloat16)
            return carry

        lax.fori_loop(0, 6, one, 0)
        unit = region(q, w, u, 1, plane_tap, 6)
        go(0, s, unit, u_up)
        go(1, s, unit, u_dn)

    def event1(s):
        q = 2 * s + core
        um, up = wrap(u - 1), wrap(u + 1)
        arrived(0, s, region(q, w, um, 1, plane_tap, 6), u_dn)
        go(2, s, region(q, w, um, 1, plane_tap, 3), u_up)
        arrived(1, s, region(q, w, up, 1, plane_tap, 6), u_up)
        go(3, s, region(q, w, up, 1, plane_tap + 3, 3), u_dn)

    def event2(s):
        q = 2 * s + core
        uo = wrap(u + 2)
        arrived(2, s, region(q, w, uo, 1, plane_tap, 3), u_dn)
        arrived(3, s, region(q, w, uo, 1, plane_tap + 3, 3), u_up)
        unit = region(q, w, 0, 4, plane_tap, 6)
        go(4, s, unit, w_up)
        go(5, s, unit, w_dn)
        spread(0, s)

    def event3(s):
        q = 2 * s + core
        arrived(4, s, region(q, rows[1], 0, 4, plane_tap, 6), w_dn)
        go(6, s, region(q, rows[1], 0, 2, plane_tap, 6), w_up)
        arrived(5, s, region(q, rows[2], 0, 4, plane_tap, 6), w_up)
        go(7, s, region(q, rows[2], 2, 2, plane_tap, 6), w_dn)
        spread(1, s)
        spread(2, s)

    def event4(s):
        q = 2 * s + core
        arrived(6, s, region(q, rows[3], 0, 2, plane_tap, 6), w_dn)
        arrived(7, s, region(q, rows[3], 2, 2, plane_tap, 6), w_up)
        spread(3, s)
        for i in range(3):
            from_y(i, s)

    def from_y(i, s):
        q = 2 * s + core
        arrived(8 + 2 * i, s, region(q, rows[i], 0, 2, in_tap, 3), y_dn)
        arrived(9 + 2 * i, s, region(q, rows[i], 2, 2, in_tap, 3), y_up)
        go(20 + i, s, region(q, rows[i], 0, 4, in_tap, 3), sib)

    def event5(s):
        from_y(3, s)
        q = 2 * s + 1 - core
        for i in range(4):
            arrived(16 + i, s, region(q, sib_rows[i], 0, 4, plane_tap, 6), sib)
            arrived(20 + i, s, region(q, sib_rows[i], 0, 4, in_tap, 3), sib)

    def conv(s):
        acc[...] = jnp.zeros_like(acc)

        def one(a, carry):
            for b in range(3):
                t = a * 3 + b
                even = G[2 * s, :, :, t].reshape(C, 128)
                odd = jnp.concatenate(
                    [G[2 * s + 1, i, j, t] for j in range(4) for i in range(4)], axis=0
                )
                kernel = jnp.concatenate([even, odd], axis=1)
                window = X[a, :, b * 16 : b * 16 + 288, :].reshape(576, C)
                acc[...] += jnp.dot(window, kernel, preferred_element_type=jnp.float32)
            return carry

        lax.fori_loop(0, 3, one, 0)
        cols = slice(256 * s, 256 * s + 256)
        base = RM[:, :, cols].reshape(576, 256).astype(jnp.float32)
        out[:, :, cols] = (
            (base + acc[...] + bias[:, cols]).astype(jnp.bfloat16).reshape(2, 288, 256)
        )

    def raw_rows():
        lat_copy.wait()

        def one(r, carry):
            for s in range(4):
                start = pl.multiple_of(((r + 1) * 4 + s) * PITCH, 8)
                for l in range(LANES):
                    F[l, pl.ds(start, 18), :] = R[s, r, :, l * 128 : l * 128 + 128].astype(
                        jnp.float32
                    )
            return carry

        lax.fori_loop(0, 8, one, 0)

        def sums(l, carry):
            total, square = [], []
            for s in range(4):
                a = jnp.zeros((18, 128), jnp.float32)
                b = jnp.zeros((18, 128), jnp.float32)
                for r in range(8):
                    v = F[l, ((r + 1) * 4 + s) * PITCH : ((r + 1) * 4 + s) * PITCH + 18, :]
                    a = a + v
                    b = b + v * v
                total.append(jnp.sum(a, axis=0, keepdims=True))
                square.append(jnp.sum(b, axis=0, keepdims=True))
            stats[y, l] = jnp.concatenate(total + square, axis=0)
            return carry

        lax.fori_loop(0, LANES, sums, 0)
        for k, peer in ((2, y_up), (3, y_dn), (4, y_op)):
            small(stats.at[y], stats.at[y], k, peer).start()

    def residual_rows():
        def one(c, carry):
            for l in range(LANES):
                for h in range(2):
                    v = F[l, pl.ds(4 * (4 * h + 1) * PITCH + c, 16, stride=PITCH), :]
                    RM[h, pl.ds(pl.multiple_of(c * 16, 16), 16), l * 128 : l * 128 + 128] = (
                        v.astype(jnp.bfloat16)
                    )
            return carry

        lax.fori_loop(0, 18, one, 0)

    def hidden_rows():
        small(lat.at[:, 7], halo.at[0], 0, y_up).wait_recv()
        small(lat.at[:, 0], halo.at[1], 1, y_dn).wait_recv()
        for side, r in ((0, 0), (1, 9)):
            for s in range(4):
                start = (r * 4 + s) * PITCH
                for l in range(LANES):
                    F[l, start : start + 18, :] = halo[
                        side, s, :, l * 128 : l * 128 + 128
                    ].astype(jnp.float32)
        small(stats.at[wrap(y - 1)], stats.at[wrap(y - 1)], 2, y_up).wait_recv()
        small(stats.at[wrap(y + 1)], stats.at[wrap(y + 1)], 3, y_dn).wait_recv()
        small(stats.at[wrap(y + 2)], stats.at[wrap(y + 2)], 4, y_op).wait_recv()
        grouped = jnp.zeros((8, 128), jnp.float32)
        for l in range(LANES):
            total = (stats[0, l] + stats[1, l]) + (stats[2, l] + stats[3, l])
            grouped = grouped + exact_dot(total, group_indicator(l))
        grouped = grouped * (1.0 / 23040.0)
        mean = grouped[0:4]
        rate = lax.rsqrt(grouped[4:8] - mean * mean + EPS)
        both = jnp.concatenate([rate, mean * rate], axis=0)
        for l in range(LANES):
            wide = exact_dot(both, group_indicator_t(l))
            g = gain[:, l * 128 : l * 128 + 128]
            b = shift[:, l * 128 : l * 128 + 128]
            scales[l] = jnp.concatenate([wide[0:4] * g, b - wide[4:8] * g], axis=0)

        def one(r, carry):
            inside = jnp.logical_and(
                jnp.logical_or(r > 0, y > 0), jnp.logical_or(r < 9, y < 3)
            )
            keep = jnp.where(inside, 1.0, 0.0)
            for s in range(4):
                start = pl.multiple_of((r * 4 + s) * PITCH, 8)
                for l in range(LANES):
                    v = F[l, pl.ds(start, PITCH), :] * scales[l, s : s + 1] + scales[
                        l, 4 + s : 5 + s
                    ]
                    v = v * (1.0 / (1.0 + jnp.exp(-v)))
                    F[l, pl.ds(start, PITCH), :] = jnp.where(keep > 0.5, v, 0.0)
            return carry

        lax.fori_loop(0, 10, one, 0)

    def window_rows():
        zero = jnp.zeros((16, C), jnp.bfloat16)
        for a in range(3):
            for h in range(2):
                X[a, h, 0:16, :] = zero
                X[a, h, 304:320, :] = zero

        def one(c, carry):
            for l in range(LANES):
                for h in range(2):
                    for a in range(3):
                        v = F[l, pl.ds(4 * (4 * h + a) * PITCH + c, 16, stride=PITCH), :]
                        X[
                            a,
                            h,
                            pl.ds(pl.multiple_of(c * 16 + 16, 16), 16),
                            l * 128 : l * 128 + 128,
                        ] = v.astype(jnp.bfloat16)
            return carry

        lax.fori_loop(0, 18, one, 0)

    for s in range(STAGES):
        event0(s)
    raw_rows()
    event1(0)
    event1(1)
    residual_rows()
    event2(0)
    event1(2)
    hidden_rows()
    event3(0)
    event2(1)
    event1(3)
    window_rows()
    event4(0)
    event3(1)
    event2(2)
    event1(4)
    event4(1)
    event3(2)
    event2(3)
    event5(0)
    conv(0)
    event4(2)
    event3(3)
    event2(4)
    event5(1)
    conv(1)
    event4(3)
    event3(4)
    event5(2)
    conv(2)
    event4(4)
    event5(3)
    conv(3)
    event5(4)
    conv(4)
    for copy in pending:
        copy.wait_send()
    for s in range(STAGES):
        piece_copy(s).wait_send()
    small(lat.at[:, 7], halo.at[0], 0, y_up).wait_send()
    small(lat.at[:, 0], halo.at[1], 1, y_dn).wait_send()
    for k, peer in ((2, y_up), (3, y_dn), (4, y_op)):
        small(stats.at[y], stats.at[y], k, peer).wait_send()


def spatial_section(latents, gain, shift, kernel, bias):
    vmem = pl.BlockSpec(memory_space=pltpu.VMEM)
    anywhere = pl.BlockSpec(memory_space=pl.ANY)
    dma = pltpu.SemaphoreType.DMA
    return pl.pallas_call(
        spatial_kernel_body,
        out_shape=jax.ShapeDtypeStruct((2, 288, C), jnp.bfloat16),
        in_specs=[anywhere, vmem, vmem, anywhere, vmem],
        out_specs=vmem,
        scratch_shapes=[
            pltpu.VMEM((10, 4, 4, 9, 80, 128), jnp.bfloat16),
            pltpu.VMEM((3, 2, 320, C), jnp.bfloat16),
            pltpu.VMEM((LANES, 40 * PITCH, 128), jnp.float32),
            pltpu.VMEM((4, 8, 18, C), jnp.bfloat16),
            pltpu.VMEM((2, 4, 18, C), jnp.bfloat16),
            pltpu.VMEM((2, 288, C), jnp.bfloat16),
            pltpu.VMEM((576, 256), jnp.float32),
            pltpu.VMEM((STAGES, 2, 6, 40, 128), jnp.bfloat16),
            pltpu.VMEM((4, LANES, 8, 128), jnp.float32),
            pltpu.VMEM((LANES, 8, 128), jnp.float32),
            dma((STAGES, KINDS)),
            dma((STAGES, KINDS)),
            dma((STAGES,)),
            dma((STAGES,)),
            dma((STAGES,)),
            dma((5,)),
            dma((5,)),
            dma,
        ],
        compiler_params=pltpu.CompilerParams(
            collective_id=0, has_side_effects=True, vmem_limit_bytes=60 * 1024 * 1024
        ),
        cost_estimate=pl.CostEstimate(
            flops=2 * 576 * 9 * C * C, bytes_accessed=40_000_000, transcendentals=2_000_000
        ),
        name="spatial",
    )(latents, gain[None], shift[None], kernel.reshape(9, 40, C), bias[None])


def body(
    latents,
    first_gain,
    first_shift,
    spatial_kernel,
    spatial_bias,
    second_gain,
    second_shift,
    temporal_kernel,
    temporal_bias,
    frame_slot,
):
    videos = 4
    frame_total = 100
    group_width = 40
    pixel_slots = 5
    spatial = spatial_section(latents, first_gain, first_shift, spatial_kernel, spatial_bias)
    flat = spatial.reshape(144, 4, C)
    flat = jnp.pad(flat, ((0, 16), (0, 0), (0, 0)))
    outgoing = flat.reshape(32, 5, 4, C)
    arrived = lax.all_to_all(outgoing, "frames", split_axis=0, concat_axis=0, tiled=True)
    arrived = arrived.transpose(0, 2, 1, 3).reshape(128, 5, C)
    ordered = arrived[frame_slot].reshape(videos, FRAMES, pixel_slots, C)
    ordered_values = ordered.astype(jnp.float32)
    grouped = ordered_values.reshape(videos, FRAMES * pixel_slots, GROUPS, group_width)
    clip_sum, clip_square = lax.psum(
        (jnp.sum(grouped, axis=(1, 3)), jnp.sum(grouped * grouped, axis=(1, 3))), ("frames", "rows")
    )
    clip_entries = FRAMES * 576 * group_width
    clip_average = (clip_sum / clip_entries)[:, None, :, None]
    clip_squares = (clip_square / clip_entries)[:, None, :, None]
    clip_scaled = (grouped - clip_average) * lax.rsqrt(
        clip_squares - clip_average * clip_average + EPS
    )
    hidden_two = jax.nn.silu(
        clip_scaled.reshape(ordered.shape) * second_gain + second_shift
    ).astype(jnp.bfloat16)
    extended_two = jnp.pad(hidden_two, ((0, 0), (1, 1), (0, 0), (0, 0)))
    temporal = jnp.zeros((videos * FRAMES * pixel_slots, C), jnp.float32)
    for frame_tap in range(3):
        window = extended_two[:, frame_tap : frame_tap + FRAMES].reshape(-1, C)
        temporal = temporal + jnp.dot(
            window, temporal_kernel[frame_tap], preferred_element_type=jnp.float32
        )
    mixed = (ordered_values + temporal.reshape(ordered.shape) + temporal_bias).astype(jnp.bfloat16)
    placed = jnp.zeros((128, pixel_slots, C), jnp.bfloat16)
    placed = placed.at[frame_slot].set(mixed.reshape(frame_total, pixel_slots, C))
    returned = lax.all_to_all(
        placed.reshape(32, 4, pixel_slots, C), "frames", split_axis=0, concat_axis=0, tiled=True
    )
    result = returned.transpose(0, 2, 1, 3).reshape(160, 4, C)[:144]
    result = result.reshape(2, 18, 4, 4, C).transpose(3, 0, 2, 1, 4)
    return result.reshape(latents.shape)


def solution(mesh):
    in_specs = (
        P("frames", "rows", None, None),
        P(),
        P(),
        P(None, None, "frames", None),
        P(),
        P(),
        P(),
        P(),
        P(),
        P(),
    )
    out_specs = P("frames", "rows", None, None)
    return jax.shard_map(body, mesh=mesh, in_specs=in_specs, out_specs=out_specs, check_vma=False)
```

```python
import jax
import jax.numpy as jnp
from jax import lax
from jax.experimental import pallas as pl
from jax.experimental.pallas import tpu as pltpu
from jax.sharding import PartitionSpec as P

EPS = 1e-06
MESH = pl.DeviceIdType.MESH
C = 1280
LANES = 10
STAGES = 5
PITCH = 24
KINDS = 24


def group_indicator(tile):
    channel = lax.broadcasted_iota(jnp.int32, (128, 128), 0) + tile * 128
    first = lax.broadcasted_iota(jnp.int32, (128, 128), 1) * 40
    return jnp.where((channel >= first) & (channel < first + 40), 1.0, 0.0)


def group_indicator_t(tile):
    channel = lax.broadcasted_iota(jnp.int32, (128, 128), 1) + tile * 128
    first = lax.broadcasted_iota(jnp.int32, (128, 128), 0) * 40
    return jnp.where((channel >= first) & (channel < first + 40), 1.0, 0.0)


def exact_dot(a, b):
    return jnp.dot(a, b, preferred_element_type=jnp.float32, precision=lax.Precision.HIGHEST)


def iota(shape, dim):
    return lax.broadcasted_iota(jnp.int32, shape, dim)


def flag(mask):
    return jnp.where(mask, 1.0, 0.0).astype(jnp.bfloat16)


def by_slot(total, square):
    a = (total[0:4] + total[4:8]) + (total[8:12] + total[12:16])
    b = (square[0:4] + square[4:8]) + (square[8:12] + square[12:16])
    return jnp.concatenate([a, b], axis=0)


def slot_vectors(slots, padded):
    padded[...] = jnp.full((1, 128), -1, jnp.int32)
    padded[:, 0:100] = slots[...]
    row = padded[...].astype(jnp.float32)
    wide = jnp.broadcast_to(row, (128, 128))
    diagonal = jnp.where(iota((128, 128), 0) == iota((128, 128), 1), wide, 0.0)
    return row, jnp.sum(diagonal, axis=1, keepdims=True)


def greet_plane(barrier, fr):
    def one(i, carry):
        pl.semaphore_signal(
            barrier, inc=1, device_id={"frames": lax.rem(fr + i, 32)}, device_id_type=MESH
        )
        return carry

    lax.fori_loop(1, 32, one, 0)


def spatial_kernel_body(
    lat,
    gain,
    shift,
    wk,
    bias,
    slots,
    A,
    AX,
    clip,
    G,
    X,
    F,
    R,
    halo,
    RM,
    S,
    EX,
    acc,
    pieces,
    stats,
    scales,
    slot_sums,
    slot_sent,
    slot_all,
    clip_all,
    slot_pad,
    send,
    recv,
    piece_send,
    piece_recv,
    piece_own,
    small_send,
    small_recv,
    lat_sem,
    a2a_send,
    a2a_recv,
    a2a_own,
):
    fr = lax.axis_index("frames")
    y = lax.axis_index("rows")
    core = lax.rem(fr, 2)
    chip = lax.div(fr, 2)
    x = lax.rem(chip, 4)
    z = lax.div(chip, 4)
    u = x + core * (z - x)
    w = z + core * (x - z)
    par = lax.rem(y, 2)

    def wrap(v):
        return lax.rem(v + 4, 4)

    def same_core(u_, w_):
        return (((w_ + core * (u_ - w_)) * 4) + u_ + core * (w_ - u_)) * 2 + core

    u_up = {"frames": same_core(wrap(u + 1), w)}
    u_dn = {"frames": same_core(wrap(u - 1), w)}
    w_up = {"frames": same_core(u, wrap(w + 1))}
    w_dn = {"frames": same_core(u, wrap(w - 1))}
    sib = {"frames": fr + 1 - 2 * core}
    y_up = {"rows": wrap(y + 1)}
    y_dn = {"rows": wrap(y - 1)}
    y_op = {"rows": wrap(y + 2)}
    barrier = pltpu.get_barrier_semaphore()
    for peer in (y_up, y_dn, y_op):
        pl.semaphore_signal(barrier, inc=1, device_id=peer, device_id_type=MESH)
    greet_plane(barrier, fr)
    pl.semaphore_wait(barrier, 34)

    plane_tap = 3 * par

    def piece_copy(s):
        return pltpu.make_async_remote_copy(
            src_ref=wk.at[pl.ds(plane_tap, 6), :, pl.ds(pl.multiple_of(256 * s + 128 * (1 - core), 128), 128)],
            dst_ref=pieces.at[s, core],
            send_sem=piece_send.at[s],
            recv_sem=piece_recv.at[s],
            device_id=sib,
            device_id_type=MESH,
        )

    def piece_arrived(s):
        return pltpu.make_async_remote_copy(
            src_ref=pieces.at[s, 1 - core],
            dst_ref=pieces.at[s, 1 - core],
            send_sem=piece_send.at[s],
            recv_sem=piece_recv.at[s],
            device_id=sib,
            device_id_type=MESH,
        )

    def piece_local(s):
        return pltpu.make_async_copy(
            wk.at[pl.ds(plane_tap, 6), :, pl.ds(pl.multiple_of(256 * s + 128 * core, 128), 128)],
            pieces.at[s, core],
            piece_own.at[s],
        )

    for s in range(STAGES):
        piece_copy(s).start()
        piece_local(s).start()
    lat_copy = pltpu.make_async_copy(lat, R, lat_sem)
    lat_copy.start()

    def small(src, dst, k, target):
        return pltpu.make_async_remote_copy(
            src_ref=src,
            dst_ref=dst,
            send_sem=small_send.at[k],
            recv_sem=small_recv.at[k],
            device_id=target,
            device_id_type=MESH,
        )

    small(lat.at[:, 7], halo.at[0], 0, y_up).start()
    small(lat.at[:, 0], halo.at[1], 1, y_dn).start()

    def region(q, row, u0, count, tap, taps):
        return G.at[q, row, pl.ds(u0, count), pl.ds(tap, taps)]

    def mover(k, s, ref, target):
        return pltpu.make_async_remote_copy(
            src_ref=ref,
            dst_ref=ref,
            send_sem=send.at[s, k],
            recv_sem=recv.at[s, k],
            device_id=target,
            device_id_type=MESH,
        )

    rows = [w, wrap(w - 1), wrap(w + 1), wrap(w + 2)]
    sib_rows = [u, wrap(u - 1), wrap(u + 1), wrap(u + 2)]
    out_tap = 6 * par
    in_tap = 6 * (1 - par)
    pending = []

    def go(k, s, ref, target):
        copy = mover(k, s, ref, target)
        copy.start()
        pending.append(copy)

    def arrived(k, s, ref, source):
        mover(k, s, ref, source).wait_recv()

    def spread(i, s):
        q = 2 * s + core
        go(8 + 2 * i, s, region(q, rows[i], 0, 2, out_tap, 3), y_up)
        go(9 + 2 * i, s, region(q, rows[i], 2, 2, out_tap, 3), y_dn)
        go(16 + i, s, region(q, rows[i], 0, 4, plane_tap, 6), sib)

    def event0(s):
        piece_local(s).wait()
        piece_arrived(s).wait_recv()
        q = 2 * s + core

        def one(t, carry):
            both = jnp.concatenate(
                [pieces[s, 0, t].astype(jnp.float32), pieces[s, 1, t].astype(jnp.float32)], axis=0
            )
            G[q, w, u, plane_tap + t] = both.astype(jnp.bfloat16)
            return carry

        lax.fori_loop(0, 6, one, 0)
        unit = region(q, w, u, 1, plane_tap, 6)
        go(0, s, unit, u_up)
        go(1, s, unit, u_dn)

    def event1(s):
        q = 2 * s + core
        um, up = wrap(u - 1), wrap(u + 1)
        arrived(0, s, region(q, w, um, 1, plane_tap, 6), u_dn)
        go(2, s, region(q, w, um, 1, plane_tap, 3), u_up)
        arrived(1, s, region(q, w, up, 1, plane_tap, 6), u_up)
        go(3, s, region(q, w, up, 1, plane_tap + 3, 3), u_dn)

    def event2(s):
        q = 2 * s + core
        uo = wrap(u + 2)
        arrived(2, s, region(q, w, uo, 1, plane_tap, 3), u_dn)
        arrived(3, s, region(q, w, uo, 1, plane_tap + 3, 3), u_up)
        unit = region(q, w, 0, 4, plane_tap, 6)
        go(4, s, unit, w_up)
        go(5, s, unit, w_dn)
        spread(0, s)

    def event3(s):
        q = 2 * s + core
        arrived(4, s, region(q, rows[1], 0, 4, plane_tap, 6), w_dn)
        go(6, s, region(q, rows[1], 0, 2, plane_tap, 6), w_up)
        arrived(5, s, region(q, rows[2], 0, 4, plane_tap, 6), w_up)
        go(7, s, region(q, rows[2], 2, 2, plane_tap, 6), w_dn)
        spread(1, s)
        spread(2, s)

    def event4(s):
        q = 2 * s + core
        arrived(6, s, region(q, rows[3], 0, 2, plane_tap, 6), w_dn)
        arrived(7, s, region(q, rows[3], 2, 2, plane_tap, 6), w_up)
        spread(3, s)
        for i in range(3):
            from_y(i, s)

    def from_y(i, s):
        q = 2 * s + core
        arrived(8 + 2 * i, s, region(q, rows[i], 0, 2, in_tap, 3), y_dn)
        arrived(9 + 2 * i, s, region(q, rows[i], 2, 2, in_tap, 3), y_up)
        go(20 + i, s, region(q, rows[i], 0, 4, in_tap, 3), sib)

    def event5(s):
        from_y(3, s)
        q = 2 * s + 1 - core
        for i in range(4):
            arrived(16 + i, s, region(q, sib_rows[i], 0, 4, plane_tap, 6), sib)
            arrived(20 + i, s, region(q, sib_rows[i], 0, 4, in_tap, 3), sib)

    def conv(s):
        acc[...] = jnp.zeros_like(acc)

        def one(a, carry):
            for b in range(3):
                t = a * 3 + b
                even = G[2 * s, :, :, t].reshape(C, 128)
                odd = jnp.concatenate(
                    [G[2 * s + 1, i, j, t] for j in range(4) for i in range(4)], axis=0
                )
                kernel = jnp.concatenate([even, odd], axis=1)
                window = X[a, :, b * 16 : b * 16 + 288, :].reshape(576, C)
                acc[...] += jnp.dot(window, kernel, preferred_element_type=jnp.float32)
            return carry

        lax.fori_loop(0, 3, one, 0)
        cols = slice(256 * s, 256 * s + 256)
        base = RM[:, :, cols].reshape(576, 256).astype(jnp.float32)
        value = base + acc[...] + bias[:, cols]
        value = jnp.where(jnp.abs(value) < 3.3e38, value, 0.0).astype(jnp.bfloat16)
        S[:, :, cols] = value.reshape(36, 16, 256)
        value = value.astype(jnp.float32).reshape(36, 16, 256)
        total = jnp.sum(value, axis=0)
        square = jnp.sum(value * value, axis=0)
        slot_sums[2 * s] = by_slot(total[:, 0:128], square[:, 0:128])
        slot_sums[2 * s + 1] = by_slot(total[:, 128:256], square[:, 128:256])

    def send_tiles(k, lo, hi):
        def one(i, carry):
            d = lax.rem(fr + i, 32)
            pltpu.make_async_remote_copy(
                src_ref=S.at[d, :, lo:hi],
                dst_ref=A.at[fr, :, lo:hi],
                send_sem=a2a_send.at[k],
                recv_sem=a2a_recv.at[k],
                device_id={"frames": d},
                device_id_type=MESH,
            ).start()
            return carry

        lax.fori_loop(1, 32, one, 0)
        pltpu.make_async_copy(S.at[fr, :, lo:hi], A.at[fr, :, lo:hi], a2a_own.at[k]).start()

    def wait_tiles(k, lo, hi):
        pltpu.make_async_copy(S.at[fr, :, lo:hi], A.at[fr, :, lo:hi], a2a_own.at[k]).wait()
        wait_all(S.at[0:31, :, lo:hi], A.at[0:31, :, lo:hi], k)

    def wait_all(src, dst, k):
        both = pltpu.make_async_remote_copy(
            src_ref=src,
            dst_ref=dst,
            send_sem=a2a_send.at[k],
            recv_sem=a2a_recv.at[k],
            device_id=sib,
            device_id_type=MESH,
        )
        both.wait_send()
        both.wait_recv()

    def send_extra():
        for t in range(4):
            for l in range(LANES):
                part = S[32 + t, :, l * 128 : l * 128 + 128].astype(jnp.float32)
                stacks[t][l] = part
        for t in range(4):
            for r in range(4):
                for m in range(3):
                    picked = [
                        stacks[t][l][4 * r : 4 * r + 4]
                        if l < LANES
                        else jnp.zeros((4, 128), jnp.float32)
                        for l in range(4 * m, 4 * m + 4)
                    ]
                    EX[4 * t + r, m] = jnp.concatenate(picked, axis=0).astype(jnp.bfloat16)

        def one(i, carry):
            d = lax.rem(fr + i, 32)
            pltpu.make_async_remote_copy(
                src_ref=EX.at[lax.div(d, 2)],
                dst_ref=AX.at[fr],
                send_sem=a2a_send.at[3],
                recv_sem=a2a_recv.at[3],
                device_id={"frames": d},
                device_id_type=MESH,
            ).start()
            return carry

        lax.fori_loop(1, 32, one, 0)
        pltpu.make_async_copy(EX.at[chip], AX.at[fr], a2a_own.at[3]).start()

    def send_sums():
        grouped = jnp.zeros((8, 128), jnp.float32)
        for l in range(LANES):
            grouped = grouped + exact_dot(slot_sums[l], group_indicator(l))
        grouped = jnp.minimum(jnp.maximum(grouped, -3e38), 3e38)
        slot_sent[...] = grouped
        slot_all[fr] = grouped

        def one(i, carry):
            d = lax.rem(fr + i, 32)
            pltpu.make_async_remote_copy(
                src_ref=slot_sent,
                dst_ref=slot_all.at[fr],
                send_sem=a2a_send.at[4],
                recv_sem=a2a_recv.at[4],
                device_id={"frames": d},
                device_id_type=MESH,
            ).start()
            return carry

        lax.fori_loop(1, 32, one, 0)

    def clip_copy(k, peer):
        return small(clip_all.at[y], clip_all.at[y], k, peer)

    def clip_sums():
        wait_all(slot_all.at[0:31], slot_all.at[0:31], 4)
        row, col = slot_vectors(slots, slot_pad)
        kind = lax.shift_right_logical(iota((8, 128), 0), 2)
        video = jnp.bitwise_and(iota((8, 128), 0), 3) * 25
        j = iota((8, 128), 1)
        pick = flag((j >= video) & (j < video + 25))
        entry = iota((128, 256), 1)
        slot_of = lax.shift_right_logical(entry, 3) * 4 + jnp.bitwise_and(entry, 3)
        match = flag(col == slot_of.astype(jnp.float32))
        pick = jnp.dot(pick, match, preferred_element_type=jnp.float32)
        same = jnp.bitwise_and(lax.shift_right_logical(iota((8, 256), 1), 2), 1) == (
            lax.shift_right_logical(iota((8, 256), 0), 2)
        )
        pick = jnp.where(same, pick, 0.0)
        clip_all[y] = exact_dot(pick, slot_all[...].reshape(256, 128))
        for k, peer in ((5, y_up), (6, y_dn), (7, y_op)):
            clip_copy(k, peer).start()
        for k, o, peer in ((5, 3, y_up), (6, 1, y_dn), (7, 2, y_op)):
            source = clip_all.at[wrap(y + o)]
            small(source, source, k, peer).wait_recv()
        clip[...] = (clip_all[0] + clip_all[1]) + (clip_all[2] + clip_all[3])

    stacks = [[None] * LANES for _ in range(4)]

    def raw_rows():
        lat_copy.wait()

        def one(r, carry):
            for s in range(4):
                start = pl.multiple_of(((r + 1) * 4 + s) * PITCH, 8)
                for l in range(LANES):
                    F[l, pl.ds(start, 18), :] = R[s, r, :, l * 128 : l * 128 + 128].astype(
                        jnp.float32
                    )
            return carry

        lax.fori_loop(0, 8, one, 0)

        def sums(l, carry):
            total, square = [], []
            for s in range(4):
                a = jnp.zeros((18, 128), jnp.float32)
                b = jnp.zeros((18, 128), jnp.float32)
                for r in range(8):
                    v = F[l, ((r + 1) * 4 + s) * PITCH : ((r + 1) * 4 + s) * PITCH + 18, :]
                    a = a + v
                    b = b + v * v
                total.append(jnp.sum(a, axis=0, keepdims=True))
                square.append(jnp.sum(b, axis=0, keepdims=True))
            stats[y, l] = jnp.concatenate(total + square, axis=0)
            return carry

        lax.fori_loop(0, LANES, sums, 0)
        for k, peer in ((2, y_up), (3, y_dn), (4, y_op)):
            small(stats.at[y], stats.at[y], k, peer).start()

    def residual_rows():
        def one(c, carry):
            for l in range(LANES):
                for h in range(2):
                    v = F[l, pl.ds(4 * (4 * h + 1) * PITCH + c, 16, stride=PITCH), :]
                    RM[h, pl.ds(pl.multiple_of(c * 16, 16), 16), l * 128 : l * 128 + 128] = (
                        v.astype(jnp.bfloat16)
                    )
            return carry

        lax.fori_loop(0, 18, one, 0)

    def hidden_rows():
        small(lat.at[:, 7], halo.at[0], 0, y_up).wait_recv()
        small(lat.at[:, 0], halo.at[1], 1, y_dn).wait_recv()
        for side, r in ((0, 0), (1, 9)):
            for s in range(4):
                start = (r * 4 + s) * PITCH
                for l in range(LANES):
                    F[l, start : start + 18, :] = halo[
                        side, s, :, l * 128 : l * 128 + 128
                    ].astype(jnp.float32)
        small(stats.at[wrap(y - 1)], stats.at[wrap(y - 1)], 2, y_up).wait_recv()
        small(stats.at[wrap(y + 1)], stats.at[wrap(y + 1)], 3, y_dn).wait_recv()
        small(stats.at[wrap(y + 2)], stats.at[wrap(y + 2)], 4, y_op).wait_recv()
        grouped = jnp.zeros((8, 128), jnp.float32)
        for l in range(LANES):
            total = (stats[0, l] + stats[1, l]) + (stats[2, l] + stats[3, l])
            grouped = grouped + exact_dot(total, group_indicator(l))
        grouped = grouped * (1.0 / 23040.0)
        mean = grouped[0:4]
        rate = lax.rsqrt(grouped[4:8] - mean * mean + EPS)
        both = jnp.concatenate([rate, mean * rate], axis=0)
        for l in range(LANES):
            wide = exact_dot(both, group_indicator_t(l))
            g = gain[:, l * 128 : l * 128 + 128]
            b = shift[:, l * 128 : l * 128 + 128]
            scales[l] = jnp.concatenate([wide[0:4] * g, b - wide[4:8] * g], axis=0)

        def one(r, carry):
            inside = jnp.logical_and(
                jnp.logical_or(r > 0, y > 0), jnp.logical_or(r < 9, y < 3)
            )
            keep = jnp.where(inside, 1.0, 0.0)
            for s in range(4):
                start = pl.multiple_of((r * 4 + s) * PITCH, 8)
                for l in range(LANES):
                    v = F[l, pl.ds(start, PITCH), :] * scales[l, s : s + 1] + scales[
                        l, 4 + s : 5 + s
                    ]
                    v = v * (1.0 / (1.0 + jnp.exp(-v)))
                    F[l, pl.ds(start, PITCH), :] = jnp.where(keep > 0.5, v, 0.0)
            return carry

        lax.fori_loop(0, 10, one, 0)

    def window_rows():
        zero = jnp.zeros((16, C), jnp.bfloat16)
        for a in range(3):
            for h in range(2):
                X[a, h, 0:16, :] = zero
                X[a, h, 304:320, :] = zero

        def one(c, carry):
            for l in range(LANES):
                for h in range(2):
                    for a in range(3):
                        v = F[l, pl.ds(4 * (4 * h + a) * PITCH + c, 16, stride=PITCH), :]
                        X[
                            a,
                            h,
                            pl.ds(pl.multiple_of(c * 16 + 16, 16), 16),
                            l * 128 : l * 128 + 128,
                        ] = v.astype(jnp.bfloat16)
            return carry

        lax.fori_loop(0, 18, one, 0)

    for s in range(STAGES):
        event0(s)
    raw_rows()
    event1(0)
    event1(1)
    residual_rows()
    event2(0)
    event1(2)
    hidden_rows()
    event3(0)
    event2(1)
    event1(3)
    window_rows()
    event4(0)
    event3(1)
    event2(2)
    event1(4)
    event4(1)
    event3(2)
    event2(3)
    event5(0)
    conv(0)
    event4(2)
    event3(3)
    event2(4)
    event5(1)
    conv(1)
    send_tiles(0, 0, 512)
    event4(3)
    event3(4)
    event5(2)
    conv(2)
    event4(4)
    event5(3)
    conv(3)
    send_tiles(1, 512, 1024)
    event5(4)
    conv(4)
    send_sums()
    send_tiles(2, 1024, 1280)
    send_extra()
    clip_sums()
    wait_tiles(0, 0, 512)
    wait_tiles(1, 512, 1024)
    wait_tiles(2, 1024, 1280)
    pltpu.make_async_copy(EX.at[chip], AX.at[fr], a2a_own.at[3]).wait()
    rest = pltpu.make_async_remote_copy(
        src_ref=AX.at[0:31],
        dst_ref=AX.at[0:31],
        send_sem=a2a_send.at[3],
        recv_sem=a2a_recv.at[3],
        device_id=sib,
        device_id_type=MESH,
    )
    rest.wait_send()
    rest.wait_recv()
    for k, peer in ((5, y_up), (6, y_dn), (7, y_op)):
        clip_copy(k, peer).wait_send()
    for copy in pending:
        copy.wait_send()
    for s in range(STAGES):
        piece_copy(s).wait_send()
    small(lat.at[:, 7], halo.at[0], 0, y_up).wait_send()
    small(lat.at[:, 0], halo.at[1], 1, y_dn).wait_send()
    for k, peer in ((2, y_up), (3, y_dn), (4, y_op)):
        small(stats.at[y], stats.at[y], k, peer).wait_send()


def spatial_section(latents, gain, shift, kernel, bias, slots):
    vmem = pl.BlockSpec(memory_space=pltpu.VMEM)
    anywhere = pl.BlockSpec(memory_space=pl.ANY)
    dma = pltpu.SemaphoreType.DMA
    return pl.pallas_call(
        spatial_kernel_body,
        out_shape=(
            jax.ShapeDtypeStruct((32, 16, C), jnp.bfloat16),
            jax.ShapeDtypeStruct((32, 3, 16, 128), jnp.bfloat16),
            jax.ShapeDtypeStruct((8, 128), jnp.float32),
        ),
        in_specs=[anywhere, vmem, vmem, anywhere, vmem, vmem],
        out_specs=(vmem, vmem, vmem),
        scratch_shapes=[
            pltpu.VMEM((10, 4, 4, 9, 80, 128), jnp.bfloat16),
            pltpu.VMEM((3, 2, 320, C), jnp.bfloat16),
            pltpu.VMEM((LANES, 40 * PITCH, 128), jnp.float32),
            pltpu.VMEM((4, 8, 18, C), jnp.bfloat16),
            pltpu.VMEM((2, 4, 18, C), jnp.bfloat16),
            pltpu.VMEM((2, 288, C), jnp.bfloat16),
            pltpu.VMEM((36, 16, C), jnp.bfloat16),
            pltpu.VMEM((16, 3, 16, 128), jnp.bfloat16),
            pltpu.VMEM((576, 256), jnp.float32),
            pltpu.VMEM((STAGES, 2, 6, 40, 128), jnp.bfloat16),
            pltpu.VMEM((4, LANES, 8, 128), jnp.float32),
            pltpu.VMEM((LANES, 8, 128), jnp.float32),
            pltpu.VMEM((LANES, 8, 128), jnp.float32),
            pltpu.VMEM((8, 128), jnp.float32),
            pltpu.VMEM((32, 8, 128), jnp.float32),
            pltpu.VMEM((4, 8, 128), jnp.float32),
            pltpu.VMEM((1, 128), jnp.int32),
            dma((STAGES, KINDS)),
            dma((STAGES, KINDS)),
            dma((STAGES,)),
            dma((STAGES,)),
            dma((STAGES,)),
            dma((8,)),
            dma((8,)),
            dma,
            dma((5,)),
            dma((5,)),
            dma((4,)),
        ],
        compiler_params=pltpu.CompilerParams(
            collective_id=0, has_side_effects=True, vmem_limit_bytes=60 * 1024 * 1024
        ),
        cost_estimate=pl.CostEstimate(
            flops=2 * 576 * 9 * C * C, bytes_accessed=40_000_000, transcendentals=2_000_000
        ),
        name="spatial",
    )(latents, gain[None], shift[None], kernel.reshape(9, 40, C), bias[None], slots[None])


def temporal_kernel_body(
    A,
    AX,
    clip,
    slots,
    wt,
    gain,
    shift,
    bias,
    O,
    W,
    H,
    RF,
    HE,
    RE,
    OM,
    OX,
    BX,
    back,
    back_extra,
    scale_rows,
    slot_pad,
    w_sem,
    send,
    recv,
    own,
):
    fr = lax.axis_index("frames")
    core = lax.rem(fr, 2)
    sib = {"frames": fr + 1 - 2 * core}
    loads = [
        pltpu.make_async_copy(
            wt.at[:, :, 256 * n : 256 * n + 256], W.at[:, :, 256 * n : 256 * n + 256], w_sem.at[n]
        )
        for n in range(5)
    ]
    for load in loads:
        load.start()
    barrier = pltpu.get_barrier_semaphore()
    greet_plane(barrier, fr)

    row, col = slot_vectors(slots, slot_pad)

    def entry_slot(entry):
        return lax.shift_right_logical(entry, 4) * 4 + jnp.bitwise_and(entry, 3)

    def entry_pixel(entry):
        return jnp.bitwise_and(lax.shift_right_logical(entry, 2), 3)

    match = flag(col == entry_slot(iota((128, 512), 1)).astype(jnp.float32))
    match_t = flag(entry_slot(iota((512, 128), 0)).astype(jnp.float32) == row)

    def frame_number(line, shift_bits):
        frame = lax.shift_right_logical(line, shift_bits)
        video = jnp.bitwise_and(lax.shift_right_logical(line, shift_bits - 2), 3)
        return video * 25 + frame

    def real(line, count):
        return line < count

    line = iota((400, 128), 0)
    which = flag(frame_number(line, 4) == iota((400, 128), 1))
    pick = jnp.dot(which, match, preferred_element_type=jnp.float32)
    pixel = jnp.bitwise_and(iota((400, 512), 0), 3)
    pick = jnp.where(pixel == entry_pixel(iota((400, 512), 1)), pick, 0.0).astype(jnp.bfloat16)
    line_t = iota((128, 400), 1)
    which_t = flag(frame_number(line_t, 4) == iota((128, 400), 0))
    pick_t = jnp.dot(match_t, which_t, preferred_element_type=jnp.float32)
    pixel_t = jnp.bitwise_and(iota((512, 400), 1), 3)
    back[...] = jnp.where(pixel_t == entry_pixel(iota((512, 400), 0)), pick_t, 0.0).astype(
        jnp.bfloat16
    )
    line = iota((112, 128), 0)
    which = flag((frame_number(line, 2) == iota((112, 128), 1)) & (line < 100))
    extra = jnp.dot(which, match, preferred_element_type=jnp.float32)
    extra_pixel = entry_pixel(iota((112, 512), 1))
    line_t = iota((128, 112), 1)
    which_t = flag((frame_number(line_t, 2) == iota((128, 112), 0)) & (line_t < 100))
    extra_t = jnp.dot(match_t, which_t, preferred_element_type=jnp.float32)
    extra_pixel_t = entry_pixel(iota((512, 112), 0))
    for i in range(4):
        back_extra[i] = jnp.where(extra_pixel_t == i, extra_t, 0.0).astype(jnp.bfloat16)
    for n in range(5):
        cols = slice(256 * n, 256 * n + 256)
        RF[:, cols] = jnp.dot(
            pick, A[:, :, cols].reshape(512, 256), preferred_element_type=jnp.float32
        ).astype(jnp.bfloat16)
    for i in range(4):
        picked = jnp.where(extra_pixel == i, extra, 0.0).astype(jnp.bfloat16)
        for m in range(3):
            l = 4 * m + i
            if l < LANES:
                RE[:, l * 128 : l * 128 + 128] = jnp.dot(
                    picked, AX[:, m].reshape(512, 128), preferred_element_type=jnp.float32
                ).astype(jnp.bfloat16)

    grouped = clip[...] * (1.0 / 576000.0)
    mean = grouped[0:4]
    rate = lax.rsqrt(grouped[4:8] - mean * mean + EPS)
    both = jnp.concatenate([rate, mean * rate], axis=0)
    HE[0:8, :] = jnp.zeros((8, C), jnp.float32)
    HE[104:128, :] = jnp.zeros((24, C), jnp.float32)
    H[0] = jnp.zeros((16, C), jnp.bfloat16)
    H[26] = jnp.zeros((16, C), jnp.bfloat16)
    for l in range(LANES):
        cols = slice(l * 128, l * 128 + 128)
        wide = exact_dot(both, group_indicator_t(l))
        a = wide[0:4] * gain[:, cols]
        b = shift[:, cols] - wide[4:8] * gain[:, cols]
        for o, part in ((0, a), (16, b)):
            scale_rows[o : o + 16, cols] = jnp.concatenate(
                [jnp.broadcast_to(part[v : v + 1], (4, 128)) for v in range(4)], axis=0
            )
        a8 = jnp.concatenate([a, a], axis=0)
        b8 = jnp.concatenate([b, b], axis=0)
        raw = RE[:, cols].astype(jnp.float32).reshape(14, 8, 128)
        v = raw * a8[None] + b8[None]
        v = (v * (1.0 / (1.0 + jnp.exp(-v)))).reshape(112, 128)
        HE[8:108, cols] = v[0:100]

    def one(f, carry):
        for l in range(LANES):
            cols = slice(l * 128, l * 128 + 128)
            v = RF[pl.ds(pl.multiple_of(f * 16, 16), 16), cols].astype(jnp.float32)
            v = v * scale_rows[0:16, cols] + scale_rows[16:32, cols]
            v = v * (1.0 / (1.0 + jnp.exp(-v)))
            H[f + 1, :, cols] = v.astype(jnp.bfloat16)
        return carry

    lax.fori_loop(0, 25, one, 0)
    pl.semaphore_wait(barrier, 31)

    def spread(src, dst, k):
        def one(i, carry):
            d = lax.rem(fr + i, 32)
            pltpu.make_async_remote_copy(
                src_ref=src(d),
                dst_ref=dst(fr),
                send_sem=send.at[k],
                recv_sem=recv.at[k],
                device_id={"frames": d},
                device_id_type=MESH,
            ).start()
            return carry

        lax.fori_loop(1, 32, one, 0)
        pltpu.make_async_copy(src(fr), dst(fr), own.at[k]).start()

    def collect(src, dst, k):
        pltpu.make_async_copy(src(fr), dst(fr), own.at[k]).wait()
        whole = pltpu.make_async_remote_copy(
            src_ref=src(slice(0, 31)),
            dst_ref=dst(slice(0, 31)),
            send_sem=send.at[k],
            recv_sem=recv.at[k],
            device_id=sib,
            device_id_type=MESH,
        )
        whole.wait_send()
        whole.wait_recv()

    def chunk(n):
        cols = slice(256 * n, 256 * n + 256)
        return (lambda d: OM.at[d, :, cols]), (lambda d: O.at[d, :, cols])

    for n in range(5):
        cols = slice(256 * n, 256 * n + 256)
        loads[n].wait()
        total = RF[:, cols].astype(jnp.float32) + bias[:, cols]
        for k in range(3):
            total = total + jnp.dot(
                H[k : k + 25].reshape(400, C), W[k, :, cols], preferred_element_type=jnp.float32
            )
        placed = jnp.dot(back[...], total.astype(jnp.bfloat16), preferred_element_type=jnp.float32)
        OM[:, :, cols] = placed.astype(jnp.bfloat16).reshape(32, 16, 256)
        spread(*chunk(n), n)
    half = pl.multiple_of(core * 640, 128)
    total = RE[:, pl.ds(half, 640)].astype(jnp.float32) + bias[:, pl.ds(half, 640)]
    for k in range(3):
        window = HE[4 + 4 * k : 116 + 4 * k, :].astype(jnp.bfloat16)
        total = total + jnp.dot(
            window, W[k, :, pl.ds(half, 640)], preferred_element_type=jnp.float32
        )
    mixed = total.astype(jnp.bfloat16)
    for m in range(2):
        placed = jnp.zeros((512, 128), jnp.float32)
        for i in range(4):
            l = 4 * m + i
            if l < 5:
                placed = placed + jnp.dot(
                    back_extra[i],
                    mixed[:, l * 128 : l * 128 + 128],
                    preferred_element_type=jnp.float32,
                )
        OX[:, m] = placed.astype(jnp.bfloat16).reshape(32, 16, 128)
    spread((lambda d: OX.at[d]), (lambda d: BX.at[d]), 5)
    collect((lambda d: OX.at[d]), (lambda d: BX.at[d]), 5)
    for t in range(4):
        for l in range(LANES):
            k, m, i = l // 5, (l % 5) // 4, (l % 5) % 4
            part = [
                BX[2 * (4 * t + r) + k, m].astype(jnp.float32)[4 * i : 4 * i + 4] for r in range(4)
            ]
            O[32 + t, :, l * 128 : l * 128 + 128] = jnp.concatenate(part, axis=0).astype(
                jnp.bfloat16
            )
    for n in range(5):
        collect(*chunk(n), n)


def temporal_section(A, AX, clip, slots, kernel, gain, shift, bias):
    vmem = pl.BlockSpec(memory_space=pltpu.VMEM)
    anywhere = pl.BlockSpec(memory_space=pl.ANY)
    dma = pltpu.SemaphoreType.DMA
    return pl.pallas_call(
        temporal_kernel_body,
        out_shape=jax.ShapeDtypeStruct((36, 16, C), jnp.bfloat16),
        in_specs=[vmem, vmem, vmem, vmem, anywhere, vmem, vmem, vmem],
        out_specs=vmem,
        scratch_shapes=[
            pltpu.VMEM((3, C, C), jnp.bfloat16),
            pltpu.VMEM((27, 16, C), jnp.bfloat16),
            pltpu.VMEM((400, C), jnp.bfloat16),
            pltpu.VMEM((128, C), jnp.float32),
            pltpu.VMEM((112, C), jnp.bfloat16),
            pltpu.VMEM((32, 16, C), jnp.bfloat16),
            pltpu.VMEM((32, 2, 16, 128), jnp.bfloat16),
            pltpu.VMEM((32, 2, 16, 128), jnp.bfloat16),
            pltpu.VMEM((512, 400), jnp.bfloat16),
            pltpu.VMEM((4, 512, 112), jnp.bfloat16),
            pltpu.VMEM((32, C), jnp.float32),
            pltpu.VMEM((1, 128), jnp.int32),
            dma((5,)),
            dma((6,)),
            dma((6,)),
            dma((6,)),
        ],
        compiler_params=pltpu.CompilerParams(
            collective_id=1, has_side_effects=True, vmem_limit_bytes=56 * 1024 * 1024
        ),
        cost_estimate=pl.CostEstimate(
            flops=2 * 500 * 3 * C * C, bytes_accessed=14_000_000, transcendentals=1_000_000
        ),
        name="temporal",
    )(A, AX, clip, slots[None], kernel, gain[None], shift[None], bias[None])


def body(
    latents,
    first_gain,
    first_shift,
    spatial_kernel,
    spatial_bias,
    second_gain,
    second_shift,
    temporal_kernel,
    temporal_bias,
    frame_slot,
):
    main, extra, clip = spatial_section(
        latents, first_gain, first_shift, spatial_kernel, spatial_bias, frame_slot
    )
    tiles = temporal_section(
        main, extra, clip, frame_slot, temporal_kernel, second_gain, second_shift, temporal_bias
    )
    result = tiles.reshape(2, 18, 4, 4, C).transpose(3, 0, 2, 1, 4)
    return result.reshape(latents.shape)


def solution(mesh):
    in_specs = (
        P("frames", "rows", None, None),
        P(),
        P(),
        P(None, None, "frames", None),
        P(),
        P(),
        P(),
        P(),
        P(),
        P(),
    )
    out_specs = P("frames", "rows", None, None)
    return jax.shard_map(body, mesh=mesh, in_specs=in_specs, out_specs=out_specs, check_vma=False)
```

```python
import jax
import jax.numpy as jnp
from jax import lax
from jax.experimental import pallas as pl
from jax.experimental.pallas import tpu as pltpu
from jax.sharding import PartitionSpec as P

EPS = 1e-06
MESH = pl.DeviceIdType.MESH
C = 1280
LANES = 10
STAGES = 5
KINDS = 24


def member(shape, channel_dim):
    channel = iota(shape, channel_dim)
    first = iota(shape, 1 - channel_dim) * 40
    return flag((channel >= first) & (channel < first + 40))


def exact_dot(a, b):
    rows = a.shape[0]
    high = a.astype(jnp.bfloat16)
    rest = a - high.astype(jnp.float32)
    middle = rest.astype(jnp.bfloat16)
    low = (rest - middle.astype(jnp.float32)).astype(jnp.bfloat16)
    parts = jnp.concatenate([high.astype(jnp.float32), middle.astype(jnp.float32), low.astype(jnp.float32)], axis=0)
    out = jnp.dot(parts.astype(jnp.bfloat16), b, preferred_element_type=jnp.float32)
    return (out[2 * rows :] + out[rows : 2 * rows]) + out[0:rows]


def exact_pick(pick, b):
    pick = pick.astype(jnp.bfloat16)
    high = b.astype(jnp.bfloat16)
    rest = b - high.astype(jnp.float32)
    middle = rest.astype(jnp.bfloat16)
    low = (rest - middle.astype(jnp.float32)).astype(jnp.bfloat16)
    out = jnp.dot(
        pick, jnp.concatenate([high, middle, low], axis=1), preferred_element_type=jnp.float32
    )
    return (out[:, 256:384] + out[:, 128:256]) + out[:, 0:128]


def to_groups(tiles):
    return exact_dot(jnp.concatenate(tiles, axis=1), member((C, 128), 0))


def to_channels(groups):
    return exact_dot(groups, member((128, C), 1))


def iota(shape, dim):
    return lax.broadcasted_iota(jnp.int32, shape, dim)


def flag(mask):
    return jnp.where(mask, 1.0, 0.0).astype(jnp.bfloat16)


def by_slot(total, square):
    a = (total[0:4] + total[4:8]) + (total[8:12] + total[12:16])
    b = (square[0:4] + square[4:8]) + (square[8:12] + square[12:16])
    return jnp.concatenate([a, b], axis=0)


def slot_vectors(slots, padded):
    padded[...] = jnp.full((1, 128), -1, jnp.int32)
    padded[:, 0:100] = slots[...]
    row = padded[...].astype(jnp.float32)
    wide = jnp.broadcast_to(row, (128, 128))
    diagonal = jnp.where(iota((128, 128), 0) == iota((128, 128), 1), wide, 0.0)
    return row, jnp.sum(diagonal, axis=1, keepdims=True)


def greet_plane(barrier, fr):
    def one(i, carry):
        pl.semaphore_signal(
            barrier, inc=1, device_id={"frames": lax.rem(fr + i, 32)}, device_id_type=MESH
        )
        return carry

    lax.fori_loop(1, 32, one, 0)


def spatial_kernel_body(
    lat,
    gain,
    shift,
    wk,
    bias,
    slots,
    A,
    AX,
    clip,
    G,
    X,
    F,
    R,
    edge_out,
    edge_in,
    RM,
    S,
    EX,
    acc,
    pieces,
    stats,
    scales,
    slot_sums,
    slot_sent,
    slot_all,
    clip_all,
    slot_pad,
    send,
    recv,
    piece_send,
    piece_recv,
    piece_own,
    small_send,
    small_recv,
    lat_sem,
    a2a_send,
    a2a_recv,
    a2a_own,
):
    fr = lax.axis_index("frames")
    y = lax.axis_index("rows")
    core = lax.rem(fr, 2)
    chip = lax.div(fr, 2)
    x = lax.rem(chip, 4)
    z = lax.div(chip, 4)
    u = x + core * (z - x)
    w = z + core * (x - z)
    part = lax.rem(y, 2)

    def wrap(v):
        return lax.rem(v + 4, 4)

    def same_core(u_, w_):
        return (((w_ + core * (u_ - w_)) * 4) + u_ + core * (w_ - u_)) * 2 + core

    u_up = {"frames": same_core(wrap(u + 1), w)}
    u_dn = {"frames": same_core(wrap(u - 1), w)}
    w_up = {"frames": same_core(u, wrap(w + 1))}
    w_dn = {"frames": same_core(u, wrap(w - 1))}
    sib = {"frames": fr + 1 - 2 * core}
    y_up = {"rows": wrap(y + 1)}
    y_dn = {"rows": wrap(y - 1)}
    y_op = {"rows": wrap(y + 2)}
    barrier = pltpu.get_barrier_semaphore()
    for peer in (y_up, y_dn, y_op):
        pl.semaphore_signal(barrier, inc=1, device_id=peer, device_id_type=MESH)
    greet_plane(barrier, fr)
    lat_copy = pltpu.make_async_copy(lat, R, lat_sem)
    lat_copy.start()

    plane_tap = 3 * part

    def piece_cols(s, c):
        return pl.ds(pl.multiple_of(256 * s + 128 * c, 128), 128)

    def piece_copy(s):
        return pltpu.make_async_remote_copy(
            src_ref=wk.at[pl.ds(plane_tap, 6), :, piece_cols(s, 1 - core)],
            dst_ref=pieces.at[s, core],
            send_sem=piece_send.at[s],
            recv_sem=piece_recv.at[s],
            device_id=sib,
            device_id_type=MESH,
        )

    def piece_arrived(s):
        return pltpu.make_async_remote_copy(
            src_ref=pieces.at[s, 1 - core],
            dst_ref=pieces.at[s, 1 - core],
            send_sem=piece_send.at[s],
            recv_sem=piece_recv.at[s],
            device_id=sib,
            device_id_type=MESH,
        )

    def piece_local(s):
        return pltpu.make_async_copy(
            wk.at[pl.ds(plane_tap, 6), :, piece_cols(s, core)], pieces.at[s, core], piece_own.at[s]
        )

    for s in range(STAGES):
        piece_local(s).start()
    pl.semaphore_wait(barrier, 34)
    for s in range(STAGES):
        piece_copy(s).start()

    def small(src, dst, k, target):
        return pltpu.make_async_remote_copy(
            src_ref=src,
            dst_ref=dst,
            send_sem=small_send.at[k],
            recv_sem=small_recv.at[k],
            device_id=target,
            device_id_type=MESH,
        )

    def region(q, row, u0, count, tap, taps):
        return G.at[q, row, pl.ds(u0, count), pl.ds(tap, taps)]

    def mover(k, s, ref, target):
        return pltpu.make_async_remote_copy(
            src_ref=ref,
            dst_ref=ref,
            send_sem=send.at[s, k],
            recv_sem=recv.at[s, k],
            device_id=target,
            device_id_type=MESH,
        )

    rows = [w, wrap(w - 1), wrap(w + 1), wrap(w + 2)]
    sib_rows = [u, wrap(u - 1), wrap(u + 1), wrap(u + 2)]
    out_tap = 6 * part
    in_tap = 6 * (1 - part)
    pending = []

    def go(k, s, ref, target):
        copy = mover(k, s, ref, target)
        copy.start()
        pending.append(copy)

    def arrived(k, s, ref, source):
        mover(k, s, ref, source).wait_recv()

    def spread(i, s):
        q = 2 * s + core
        go(8 + 2 * i, s, region(q, rows[i], 0, 2, out_tap, 3), y_up)
        go(9 + 2 * i, s, region(q, rows[i], 2, 2, out_tap, 3), y_dn)
        go(16 + i, s, region(q, rows[i], 0, 4, plane_tap, 6), sib)

    def event0(s):
        piece_local(s).wait()
        piece_arrived(s).wait_recv()
        q = 2 * s + core

        def one(t, carry):
            both = jnp.concatenate(
                [pieces[s, 0, t].astype(jnp.float32), pieces[s, 1, t].astype(jnp.float32)], axis=0
            )
            G[q, w, u, plane_tap + t] = both.astype(jnp.bfloat16)
            return carry

        lax.fori_loop(0, 6, one, 0)
        unit = region(q, w, u, 1, plane_tap, 6)
        go(0, s, unit, u_up)
        go(1, s, unit, u_dn)

    def event1(s):
        q = 2 * s + core
        um, up = wrap(u - 1), wrap(u + 1)
        arrived(0, s, region(q, w, um, 1, plane_tap, 6), u_dn)
        go(2, s, region(q, w, um, 1, plane_tap, 3), u_up)
        arrived(1, s, region(q, w, up, 1, plane_tap, 6), u_up)
        go(3, s, region(q, w, up, 1, plane_tap + 3, 3), u_dn)

    def event2(s):
        q = 2 * s + core
        uo = wrap(u + 2)
        arrived(2, s, region(q, w, uo, 1, plane_tap, 3), u_dn)
        arrived(3, s, region(q, w, uo, 1, plane_tap + 3, 3), u_up)
        unit = region(q, w, 0, 4, plane_tap, 6)
        go(4, s, unit, w_up)
        go(5, s, unit, w_dn)
        spread(0, s)

    def event3(s):
        q = 2 * s + core
        arrived(4, s, region(q, rows[1], 0, 4, plane_tap, 6), w_dn)
        go(6, s, region(q, rows[1], 0, 2, plane_tap, 6), w_up)
        arrived(5, s, region(q, rows[2], 0, 4, plane_tap, 6), w_up)
        go(7, s, region(q, rows[2], 2, 2, plane_tap, 6), w_dn)
        spread(1, s)
        spread(2, s)

    def event4(s):
        q = 2 * s + core
        arrived(6, s, region(q, rows[3], 0, 2, plane_tap, 6), w_dn)
        arrived(7, s, region(q, rows[3], 2, 2, plane_tap, 6), w_up)
        spread(3, s)
        for i in range(3):
            from_y(i, s)

    def from_y(i, s):
        q = 2 * s + core
        arrived(8 + 2 * i, s, region(q, rows[i], 0, 2, in_tap, 3), y_dn)
        arrived(9 + 2 * i, s, region(q, rows[i], 2, 2, in_tap, 3), y_up)
        go(20 + i, s, region(q, rows[i], 0, 4, in_tap, 3), sib)

    def event5(s):
        from_y(3, s)
        q = 2 * s + 1 - core
        for i in range(4):
            arrived(16 + i, s, region(q, sib_rows[i], 0, 4, plane_tap, 6), sib)
            arrived(20 + i, s, region(q, sib_rows[i], 0, 4, in_tap, 3), sib)

    def conv(s):
        def one(a, carry):
            for b in range(3):
                t = a * 3 + b
                even = G[2 * s, :, :, t].reshape(C, 128)
                odd = jnp.concatenate(
                    [G[2 * s + 1, i, j, t] for j in range(4) for i in range(4)], axis=0
                )
                kernel = jnp.concatenate([even, odd], axis=1)
                window = X[a, :, b * 16 : b * 16 + 288, :].reshape(576, C)
                acc[...] += jnp.dot(window, kernel, preferred_element_type=jnp.float32)
            return carry

        acc[...] = jnp.zeros_like(acc)
        lax.fori_loop(0, 3, one, 0)
        for n in range(2):
            q = 2 * s + n
            base = RM[:, q].reshape(576, 128).astype(jnp.float32)
            value = base + acc[:, 128 * n : 128 * n + 128]
            value = value + bias[q * 128 : q * 128 + 128].reshape(1, 128)
            value = jnp.where(jnp.abs(value) < 3.3e38, value, 0.0).astype(jnp.bfloat16)
            S[:, q] = value.reshape(36, 16, 128)

    def each_peer(start):
        def one(i, carry):
            start(lax.rem(fr + i, 32))
            return carry

        lax.fori_loop(1, 32, one, 0)

    def finish(s):
        span = slice(2 * s, 2 * s + 2)
        each_peer(
            lambda d: pltpu.make_async_remote_copy(
                src_ref=S.at[d, span],
                dst_ref=A.at[fr, span],
                send_sem=a2a_send.at[s],
                recv_sem=a2a_recv.at[s],
                device_id={"frames": d},
                device_id_type=MESH,
            ).start()
        )
        pltpu.make_async_copy(S.at[fr, span], A.at[fr, span], a2a_own.at[s]).start()
        if s in (1, 3, 4):
            send_extra(s // 2)
        for q in range(2 * s, 2 * s + 2):
            value = S[:, q].astype(jnp.float32)
            slot_sums[q] = by_slot(jnp.sum(value, axis=0), jnp.sum(value * value, axis=0))

    def wait_tiles(s):
        span = slice(2 * s, 2 * s + 2)
        pltpu.make_async_copy(S.at[fr, span], A.at[fr, span], a2a_own.at[s]).wait()
        wait_all(S.at[0:31, span], A.at[0:31, span], s)

    def wait_all(src, dst, k):
        both = pltpu.make_async_remote_copy(
            src_ref=src,
            dst_ref=dst,
            send_sem=a2a_send.at[k],
            recv_sem=a2a_recv.at[k],
            device_id=sib,
            device_id_type=MESH,
        )
        both.wait_send()
        both.wait_recv()

    def send_extra(m):
        for t in range(4):
            lanes = [S[32 + t, q].astype(jnp.float32) for q in range(4 * m, min(4 * m + 4, LANES))]
            for r in range(4):
                picked = [v[4 * r : 4 * r + 4] for v in lanes]
                picked += [jnp.zeros((4, 128), jnp.float32)] * (4 - len(lanes))
                EX[4 * t + r, m] = jnp.concatenate(picked, axis=0).astype(jnp.bfloat16)
        each_peer(
            lambda d: pltpu.make_async_remote_copy(
                src_ref=EX.at[lax.div(d, 2), m],
                dst_ref=AX.at[fr, m],
                send_sem=a2a_send.at[5 + m],
                recv_sem=a2a_recv.at[5 + m],
                device_id={"frames": d},
                device_id_type=MESH,
            ).start()
        )
        pltpu.make_async_copy(EX.at[chip, m], AX.at[fr, m], a2a_own.at[5 + m]).start()

    def wait_extra(m):
        pltpu.make_async_copy(EX.at[chip, m], AX.at[fr, m], a2a_own.at[5 + m]).wait()
        wait_all(AX.at[0:31, m], AX.at[0:31, m], 5 + m)

    def send_sums():
        grouped = to_groups([slot_sums[l] for l in range(LANES)])
        grouped = jnp.minimum(jnp.maximum(grouped, -3e38), 3e38)
        slot_sent[...] = grouped
        slot_all[fr] = grouped

        each_peer(
            lambda d: pltpu.make_async_remote_copy(
                src_ref=slot_sent,
                dst_ref=slot_all.at[fr],
                send_sem=a2a_send.at[8],
                recv_sem=a2a_recv.at[8],
                device_id={"frames": d},
                device_id_type=MESH,
            ).start()
        )

    def clip_sums():
        wait_all(slot_all.at[0:31], slot_all.at[0:31], 8)
        row, col = slot_vectors(slots, slot_pad)
        kind = lax.shift_right_logical(iota((8, 128), 0), 2)
        video = jnp.bitwise_and(iota((8, 128), 0), 3) * 25
        j = iota((8, 128), 1)
        pick = flag((j >= video) & (j < video + 25))
        entry = iota((128, 256), 1)
        slot_of = lax.shift_right_logical(entry, 3) * 4 + jnp.bitwise_and(entry, 3)
        match = flag(col == slot_of.astype(jnp.float32))
        pick = jnp.dot(pick, match, preferred_element_type=jnp.float32)
        same = jnp.bitwise_and(lax.shift_right_logical(iota((8, 256), 1), 2), 1) == (
            lax.shift_right_logical(iota((8, 256), 0), 2)
        )
        pick = jnp.where(same, pick, 0.0)
        clip_all[y] = exact_pick(pick, slot_all[...].reshape(256, 128))
        for k, peer in ((5, y_up), (6, y_dn), (7, y_op)):
            small(clip_all.at[y], clip_all.at[y], k, peer).start()
        for k, o, peer in ((5, 3, y_up), (6, 1, y_dn), (7, 2, y_op)):
            source = clip_all.at[wrap(y + o)]
            small(source, source, k, peer).wait_recv()
        clip[...] = (clip_all[0] + clip_all[1]) + (clip_all[2] + clip_all[3])

    def own_rows():
        lat_copy.wait()

        def fill(c, carry):
            for s in range(4):
                for l in range(LANES):
                    F[l, c, pl.ds(4 + s, 8, stride=4), :] = R[
                        s, c, :, l * 128 : l * 128 + 128
                    ].astype(jnp.float32)
            return carry

        lax.fori_loop(0, 18, fill, 0)

        def edges(l, carry):
            edge_out[0, l] = F[l, :, 32:36, :].astype(jnp.bfloat16)
            edge_out[1, l] = F[l, :, 4:8, :].astype(jnp.bfloat16)
            return carry

        lax.fori_loop(0, LANES, edges, 0)
        small(edge_out.at[0], edge_in.at[0], 0, y_up).start()
        small(edge_out.at[1], edge_in.at[1], 1, y_dn).start()

        def sums(l, carry):
            cols = pl.ds(pl.multiple_of(l * 128, 128), 128)
            total, square = [], []
            for s in range(4):
                a = jnp.zeros((8, 128), jnp.float32)
                b = jnp.zeros((8, 128), jnp.float32)
                for c in range(18):
                    v = R[s, c, :, cols].astype(jnp.float32)
                    a = a + v
                    b = b + v * v
                total.append(jnp.sum(a, axis=0, keepdims=True))
                square.append(jnp.sum(b, axis=0, keepdims=True))
            stats[y, l] = jnp.concatenate(total + square, axis=0)
            return carry

        lax.fori_loop(0, LANES, sums, 0)
        for k, peer in ((2, y_up), (3, y_dn), (4, y_op)):
            small(stats.at[y], stats.at[y], k, peer).start()

    def norm_scales():
        for k, o, peer in ((2, 3, y_up), (3, 1, y_dn), (4, 2, y_op)):
            source = stats.at[wrap(y + o)]
            small(source, source, k, peer).wait_recv()
        grouped = to_groups(
            [(stats[0, l] + stats[1, l]) + (stats[2, l] + stats[3, l]) for l in range(LANES)]
        )
        grouped = grouped * (1.0 / 23040.0)
        mean = grouped[0:4]
        rate = lax.rsqrt(grouped[4:8] - mean * mean + EPS)
        both = jnp.concatenate([rate, mean * rate], axis=0)
        channels = to_channels(both)
        for l in range(LANES):
            wide = channels[:, l * 128 : l * 128 + 128]
            g = gain[l * 128 : l * 128 + 128].reshape(1, 128)
            b = shift[l * 128 : l * 128 + 128].reshape(1, 128)
            up = wide[0:4] * g
            down = b - wide[4:8] * g
            scales[l] = jnp.concatenate([up, up, down, down], axis=0)

    def edge_rows():
        small(edge_out.at[0], edge_in.at[0], 0, y_up).wait_recv()
        small(edge_out.at[1], edge_in.at[1], 1, y_dn).wait_recv()

        def one(l, carry):
            F[l, :, 0:4, :] = edge_in[0, l].astype(jnp.float32)
            F[l, :, 36:40, :] = edge_in[1, l].astype(jnp.float32)
            return carry

        lax.fori_loop(0, LANES, one, 0)

    def window_rows():
        first = jnp.where(y == 0, 4, 0)
        last = jnp.where(y == 3, 36, 40)

        def one(c, carry):
            line = iota((40, 128), 0)
            inside = (line >= first) & (line < last)
            at = pl.ds(pl.multiple_of(c * 16 + 16, 16), 16)
            here_at = pl.ds(pl.multiple_of(c * 16, 16), 16)
            for l in range(LANES):
                raw = F[l, c]
                for h in range(2):
                    RM[h, l, here_at, :] = raw[16 * h + 4 : 16 * h + 20].astype(jnp.bfloat16)
                v = raw.reshape(5, 8, 128) * scales[l, 0:8][None] + scales[l, 8:16][None]
                v = (v * (1.0 / (1.0 + jnp.exp(-v)))).reshape(40, 128)
                v = jnp.where(inside, v, 0.0)
                for h in range(2):
                    for a in range(3):
                        X[a, h, at, l * 128 : l * 128 + 128] = v[
                            16 * h + 4 * a : 16 * h + 4 * a + 16
                        ].astype(jnp.bfloat16)
            return carry

        lax.fori_loop(0, 18, one, 0)

    for s in range(STAGES):
        event0(s)
    zero = jnp.zeros((16, C), jnp.bfloat16)
    for a in range(3):
        for h in range(2):
            X[a, h, 0:16, :] = zero
            X[a, h, 304:320, :] = zero
    event1(0)
    event1(1)
    event2(0)
    own_rows()
    event1(2)
    event2(1)
    event3(0)
    event1(3)
    norm_scales()
    edge_rows()
    event2(2)
    event3(1)
    event4(0)
    event1(4)
    window_rows()
    event2(3)
    event3(2)
    event4(1)
    event5(0)
    conv(0)
    finish(0)
    event2(4)
    event3(3)
    event4(2)
    event5(1)
    conv(1)
    finish(1)
    event3(4)
    event4(3)
    event5(2)
    conv(2)
    finish(2)
    event4(4)
    event5(3)
    conv(3)
    finish(3)
    event5(4)
    conv(4)
    finish(4)
    send_sums()
    clip_sums()
    for s in range(STAGES):
        wait_tiles(s)
    for m in range(3):
        wait_extra(m)
    for copy in pending:
        copy.wait_send()
    for s in range(STAGES):
        piece_copy(s).wait_send()
    small(edge_out.at[0], edge_in.at[0], 0, y_up).wait_send()
    small(edge_out.at[1], edge_in.at[1], 1, y_dn).wait_send()
    for k, peer in ((2, y_up), (3, y_dn), (4, y_op)):
        small(stats.at[y], stats.at[y], k, peer).wait_send()
    for k, peer in ((5, y_up), (6, y_dn), (7, y_op)):
        small(clip_all.at[y], clip_all.at[y], k, peer).wait_send()


def spatial_section(latents, gain, shift, kernel, bias, slots):
    vmem = pl.BlockSpec(memory_space=pltpu.VMEM)
    anywhere = pl.BlockSpec(memory_space=pl.ANY)
    dma = pltpu.SemaphoreType.DMA
    return pl.pallas_call(
        spatial_kernel_body,
        out_shape=(
            jax.ShapeDtypeStruct((32, LANES, 16, 128), jnp.bfloat16),
            jax.ShapeDtypeStruct((32, 3, 16, 128), jnp.bfloat16),
            jax.ShapeDtypeStruct((8, 128), jnp.float32),
        ),
        in_specs=[anywhere, vmem, vmem, anywhere, vmem, vmem],
        out_specs=(vmem, vmem, vmem),
        scratch_shapes=[
            pltpu.VMEM((2 * STAGES, 4, 4, 9, 80, 128), jnp.bfloat16),
            pltpu.VMEM((3, 2, 320, C), jnp.bfloat16),
            pltpu.VMEM((LANES, 18, 40, 128), jnp.float32),
            pltpu.VMEM((4, 18, 8, C), jnp.bfloat16),
            pltpu.VMEM((2, LANES, 18, 4, 128), jnp.bfloat16),
            pltpu.VMEM((2, LANES, 18, 4, 128), jnp.bfloat16),
            pltpu.VMEM((2, LANES, 288, 128), jnp.bfloat16),
            pltpu.VMEM((36, LANES, 16, 128), jnp.bfloat16),
            pltpu.VMEM((16, 3, 16, 128), jnp.bfloat16),
            pltpu.VMEM((576, 256), jnp.float32),
            pltpu.VMEM((STAGES, 2, 6, 40, 128), jnp.bfloat16),
            pltpu.VMEM((4, LANES, 8, 128), jnp.float32),
            pltpu.VMEM((LANES, 16, 128), jnp.float32),
            pltpu.VMEM((LANES, 8, 128), jnp.float32),
            pltpu.VMEM((8, 128), jnp.float32),
            pltpu.VMEM((32, 8, 128), jnp.float32),
            pltpu.VMEM((4, 8, 128), jnp.float32),
            pltpu.VMEM((1, 128), jnp.int32),
            dma((STAGES, KINDS)),
            dma((STAGES, KINDS)),
            dma((STAGES,)),
            dma((STAGES,)),
            dma((STAGES,)),
            dma((8,)),
            dma((8,)),
            dma,
            dma((9,)),
            dma((9,)),
            dma((8,)),
        ],
        compiler_params=pltpu.CompilerParams(
            collective_id=0, has_side_effects=True, vmem_limit_bytes=60 * 1024 * 1024
        ),
        cost_estimate=pl.CostEstimate(
            flops=2 * 576 * 9 * C * C, bytes_accessed=40_000_000, transcendentals=2_000_000
        ),
        name="spatial",
    )(
        latents.transpose(0, 2, 1, 3), gain, shift, kernel.reshape(9, 40, C), bias, slots[None]
    )


def temporal_kernel_body(
    A,
    AX,
    clip,
    slots,
    wt,
    gain,
    shift,
    bias,
    O,
    W,
    H,
    RF,
    HE,
    RE,
    OM,
    OX,
    BX,
    back,
    back_extra,
    scale_rows,
    slot_pad,
    w_sem,
    send,
    recv,
    own,
):
    fr = lax.axis_index("frames")
    core = lax.rem(fr, 2)
    sib = {"frames": fr + 1 - 2 * core}
    loads = [
        pltpu.make_async_copy(
            wt.at[:, :, 256 * n : 256 * n + 256], W.at[:, :, 256 * n : 256 * n + 256], w_sem.at[n]
        )
        for n in range(5)
    ]
    for load in loads:
        load.start()
    barrier = pltpu.get_barrier_semaphore()
    greet_plane(barrier, fr)

    row, col = slot_vectors(slots, slot_pad)

    def entry_slot(entry):
        return lax.shift_right_logical(entry, 4) * 4 + jnp.bitwise_and(entry, 3)

    def entry_pixel(entry):
        return jnp.bitwise_and(lax.shift_right_logical(entry, 2), 3)

    match = flag(col == entry_slot(iota((128, 512), 1)).astype(jnp.float32))
    match_t = flag(entry_slot(iota((512, 128), 0)).astype(jnp.float32) == row)

    def frame_number(line, shift_bits):
        frame = lax.shift_right_logical(line, shift_bits)
        video = jnp.bitwise_and(lax.shift_right_logical(line, shift_bits - 2), 3)
        return video * 25 + frame

    def real(line, count):
        return line < count

    line = iota((400, 128), 0)
    which = flag(frame_number(line, 4) == iota((400, 128), 1))
    pick = jnp.dot(which, match, preferred_element_type=jnp.float32)
    pixel = jnp.bitwise_and(iota((400, 512), 0), 3)
    pick = jnp.where(pixel == entry_pixel(iota((400, 512), 1)), pick, 0.0).astype(jnp.bfloat16)
    line_t = iota((128, 400), 1)
    which_t = flag(frame_number(line_t, 4) == iota((128, 400), 0))
    pick_t = jnp.dot(match_t, which_t, preferred_element_type=jnp.float32)
    pixel_t = jnp.bitwise_and(iota((512, 400), 1), 3)
    back[...] = jnp.where(pixel_t == entry_pixel(iota((512, 400), 0)), pick_t, 0.0).astype(
        jnp.bfloat16
    )
    line = iota((112, 128), 0)
    which = flag((frame_number(line, 2) == iota((112, 128), 1)) & (line < 100))
    extra = jnp.dot(which, match, preferred_element_type=jnp.float32)
    extra_pixel = entry_pixel(iota((112, 512), 1))
    line_t = iota((128, 112), 1)
    which_t = flag((frame_number(line_t, 2) == iota((128, 112), 0)) & (line_t < 100))
    extra_t = jnp.dot(match_t, which_t, preferred_element_type=jnp.float32)
    extra_pixel_t = entry_pixel(iota((512, 112), 0))
    for i in range(4):
        back_extra[i] = jnp.where(extra_pixel_t == i, extra_t, 0.0).astype(jnp.bfloat16)
    for n in range(5):
        both = jnp.concatenate(
            [A[:, 2 * n].reshape(512, 128), A[:, 2 * n + 1].reshape(512, 128)], axis=1
        )
        both = jnp.dot(pick, both, preferred_element_type=jnp.float32).astype(jnp.bfloat16)
        RF[:, n * 256 : n * 256 + 256] = both
    for i in range(4):
        picked = jnp.where(extra_pixel == i, extra, 0.0).astype(jnp.bfloat16)
        for m in range(3):
            if 4 * m + i < LANES:
                l = 4 * m + i
                RE[:, l * 128 : l * 128 + 128] = jnp.dot(
                    picked, AX[:, m].reshape(512, 128), preferred_element_type=jnp.float32
                ).astype(jnp.bfloat16)

    grouped = clip[...] * (1.0 / 576000.0)
    mean = grouped[0:4]
    rate = lax.rsqrt(grouped[4:8] - mean * mean + EPS)
    both = jnp.concatenate([rate, mean * rate], axis=0)
    HE[0:8, :] = jnp.zeros((8, C), jnp.float32)
    HE[104:128, :] = jnp.zeros((24, C), jnp.float32)
    H[0] = jnp.zeros((16, C), jnp.bfloat16)
    H[26] = jnp.zeros((16, C), jnp.bfloat16)
    channels = to_channels(both)
    for l in range(LANES):
        cols = slice(l * 128, l * 128 + 128)
        wide = channels[:, cols]
        a = wide[0:4] * gain[cols].reshape(1, 128)
        b = shift[cols].reshape(1, 128) - wide[4:8] * gain[cols].reshape(1, 128)
        for o, part in ((0, a), (16, b)):
            scale_rows[o : o + 16, cols] = jnp.concatenate(
                [jnp.broadcast_to(part[v : v + 1], (4, 128)) for v in range(4)], axis=0
            )
        a8 = jnp.concatenate([a, a], axis=0)
        b8 = jnp.concatenate([b, b], axis=0)
        raw = RE[:, cols].astype(jnp.float32).reshape(14, 8, 128)
        v = raw * a8[None] + b8[None]
        v = (v * (1.0 / (1.0 + jnp.exp(-v)))).reshape(112, 128)
        HE[8:108, cols] = v[0:100]

    def one(f, carry):
        for l in range(LANES):
            cols = slice(l * 128, l * 128 + 128)
            v = RF[pl.ds(pl.multiple_of(f * 16, 16), 16), cols].astype(jnp.float32)
            v = v * scale_rows[0:16, cols] + scale_rows[16:32, cols]
            v = v * (1.0 / (1.0 + jnp.exp(-v)))
            H[f + 1, :, cols] = v.astype(jnp.bfloat16)
        return carry

    lax.fori_loop(0, 25, one, 0)
    pl.semaphore_wait(barrier, 31)

    def spread(src, dst, k):
        def one(i, carry):
            d = lax.rem(fr + i, 32)
            pltpu.make_async_remote_copy(
                src_ref=src(d),
                dst_ref=dst(fr),
                send_sem=send.at[k],
                recv_sem=recv.at[k],
                device_id={"frames": d},
                device_id_type=MESH,
            ).start()
            return carry

        lax.fori_loop(1, 32, one, 0)
        pltpu.make_async_copy(src(fr), dst(fr), own.at[k]).start()

    def collect(src, dst, k):
        pltpu.make_async_copy(src(fr), dst(fr), own.at[k]).wait()
        whole = pltpu.make_async_remote_copy(
            src_ref=src(slice(0, 31)),
            dst_ref=dst(slice(0, 31)),
            send_sem=send.at[k],
            recv_sem=recv.at[k],
            device_id=sib,
            device_id_type=MESH,
        )
        whole.wait_send()
        whole.wait_recv()

    def chunk(n):
        cols = slice(256 * n, 256 * n + 256)
        return (lambda d: OM.at[d, :, cols]), (lambda d: O.at[d, :, cols])

    for n in range(5):
        cols = slice(256 * n, 256 * n + 256)
        loads[n].wait()
        total = RF[:, cols].astype(jnp.float32) + bias[cols].reshape(1, 256)
        for k in range(3):
            total = total + jnp.dot(
                H[k : k + 25].reshape(400, C), W[k, :, cols], preferred_element_type=jnp.float32
            )
        placed = jnp.dot(back[...], total.astype(jnp.bfloat16), preferred_element_type=jnp.float32)
        OM[:, :, cols] = placed.astype(jnp.bfloat16).reshape(32, 16, 256)
        spread(*chunk(n), n)
    half = pl.multiple_of(core * 640, 128)
    total = RE[:, pl.ds(half, 640)].astype(jnp.float32) + bias[pl.ds(half, 640)].reshape(1, 640)
    for k in range(3):
        window = HE[4 + 4 * k : 116 + 4 * k, :].astype(jnp.bfloat16)
        total = total + jnp.dot(
            window, W[k, :, pl.ds(half, 640)], preferred_element_type=jnp.float32
        )
    mixed = total.astype(jnp.bfloat16)
    for m in range(2):
        placed = jnp.zeros((512, 128), jnp.float32)
        for i in range(4):
            l = 4 * m + i
            if l < 5:
                placed = placed + jnp.dot(
                    back_extra[i],
                    mixed[:, l * 128 : l * 128 + 128],
                    preferred_element_type=jnp.float32,
                )
        OX[:, m] = placed.astype(jnp.bfloat16).reshape(32, 16, 128)
    spread((lambda d: OX.at[d]), (lambda d: BX.at[d]), 5)
    collect((lambda d: OX.at[d]), (lambda d: BX.at[d]), 5)
    for t in range(4):
        for l in range(LANES):
            k, m, i = l // 5, (l % 5) // 4, (l % 5) % 4
            part = [
                BX[2 * (4 * t + r) + k, m].astype(jnp.float32)[4 * i : 4 * i + 4] for r in range(4)
            ]
            O[32 + t, :, l * 128 : l * 128 + 128] = jnp.concatenate(part, axis=0).astype(
                jnp.bfloat16
            )
    for n in range(5):
        collect(*chunk(n), n)


def temporal_section(A, AX, clip, slots, kernel, gain, shift, bias):
    vmem = pl.BlockSpec(memory_space=pltpu.VMEM)
    anywhere = pl.BlockSpec(memory_space=pl.ANY)
    dma = pltpu.SemaphoreType.DMA
    return pl.pallas_call(
        temporal_kernel_body,
        out_shape=jax.ShapeDtypeStruct((36, 16, C), jnp.bfloat16),
        in_specs=[vmem, vmem, vmem, vmem, anywhere, vmem, vmem, vmem],
        out_specs=vmem,
        scratch_shapes=[
            pltpu.VMEM((3, C, C), jnp.bfloat16),
            pltpu.VMEM((27, 16, C), jnp.bfloat16),
            pltpu.VMEM((400, C), jnp.bfloat16),
            pltpu.VMEM((128, C), jnp.float32),
            pltpu.VMEM((112, C), jnp.bfloat16),
            pltpu.VMEM((32, 16, C), jnp.bfloat16),
            pltpu.VMEM((32, 2, 16, 128), jnp.bfloat16),
            pltpu.VMEM((32, 2, 16, 128), jnp.bfloat16),
            pltpu.VMEM((512, 400), jnp.bfloat16),
            pltpu.VMEM((4, 512, 112), jnp.bfloat16),
            pltpu.VMEM((32, C), jnp.float32),
            pltpu.VMEM((1, 128), jnp.int32),
            dma((5,)),
            dma((6,)),
            dma((6,)),
            dma((6,)),
        ],
        compiler_params=pltpu.CompilerParams(
            collective_id=1, has_side_effects=True, vmem_limit_bytes=56 * 1024 * 1024
        ),
        cost_estimate=pl.CostEstimate(
            flops=2 * 500 * 3 * C * C, bytes_accessed=14_000_000, transcendentals=1_000_000
        ),
        name="temporal",
    )(A, AX, clip, slots[None], kernel, gain, shift, bias)


def body(
    latents,
    first_gain,
    first_shift,
    spatial_kernel,
    spatial_bias,
    second_gain,
    second_shift,
    temporal_kernel,
    temporal_bias,
    frame_slot,
):
    main, extra, clip = spatial_section(
        latents, first_gain, first_shift, spatial_kernel, spatial_bias, frame_slot
    )
    tiles = temporal_section(
        main, extra, clip, frame_slot, temporal_kernel, second_gain, second_shift, temporal_bias
    )
    result = tiles.reshape(2, 18, 4, 4, C).transpose(3, 0, 2, 1, 4)
    return result.reshape(latents.shape)


def solution(mesh):
    in_specs = (
        P("frames", "rows", None, None),
        P(),
        P(),
        P(None, None, "frames", None),
        P(),
        P(),
        P(),
        P(),
        P(),
        P(),
    )
    out_specs = P("frames", "rows", None, None)
    return jax.shard_map(body, mesh=mesh, in_specs=in_specs, out_specs=out_specs, check_vma=False)
```

```python
import jax
import jax.numpy as jnp
from jax import lax
from jax.experimental import pallas as pl
from jax.experimental.pallas import tpu as pltpu
from jax.sharding import PartitionSpec as P

EPS = 1e-06
MESH = pl.DeviceIdType.MESH
C = 1280
LANES = 10
STAGES = 5
KINDS = 24


def member(shape, channel_dim):
    channel = iota(shape, channel_dim)
    first = iota(shape, 1 - channel_dim) * 40
    return flag((channel >= first) & (channel < first + 40))


def exact_dot(a, b):
    rows = a.shape[0]
    high = a.astype(jnp.bfloat16)
    rest = a - high.astype(jnp.float32)
    middle = rest.astype(jnp.bfloat16)
    low = (rest - middle.astype(jnp.float32)).astype(jnp.bfloat16)
    parts = jnp.concatenate([high.astype(jnp.float32), middle.astype(jnp.float32), low.astype(jnp.float32)], axis=0)
    out = jnp.dot(parts.astype(jnp.bfloat16), b, preferred_element_type=jnp.float32)
    return (out[2 * rows :] + out[rows : 2 * rows]) + out[0:rows]


def exact_pick(pick, b):
    high = b.astype(jnp.bfloat16)
    rest = b - high.astype(jnp.float32)
    middle = rest.astype(jnp.bfloat16)
    low = (rest - middle.astype(jnp.float32)).astype(jnp.bfloat16)
    out = jnp.dot(
        pick, jnp.concatenate([high, middle, low], axis=1), preferred_element_type=jnp.float32
    )
    return (out[:, 256:384] + out[:, 128:256]) + out[:, 0:128]


def to_groups(tiles, groups_of):
    return exact_dot(jnp.concatenate(tiles, axis=1), groups_of)


def to_channels(groups):
    return exact_dot(groups, member((128, C), 1))


def iota(shape, dim):
    return lax.broadcasted_iota(jnp.int32, shape, dim)


def flag(mask):
    return jnp.where(mask, 1.0, 0.0).astype(jnp.bfloat16)


def by_slot(total, square):
    a = (total[0:4] + total[4:8]) + (total[8:12] + total[12:16])
    b = (square[0:4] + square[4:8]) + (square[8:12] + square[12:16])
    return jnp.concatenate([a, b], axis=0)


def slot_vectors(slots, padded):
    padded[...] = jnp.full((1, 128), -1, jnp.int32)
    padded[:, 0:100] = slots[...]
    row = padded[...].astype(jnp.float32)
    wide = jnp.broadcast_to(row, (128, 128))
    diagonal = jnp.where(iota((128, 128), 0) == iota((128, 128), 1), wide, 0.0)
    return row, jnp.sum(diagonal, axis=1, keepdims=True)


def greet_plane(barrier, fr):
    def one(i, carry):
        pl.semaphore_signal(
            barrier, inc=1, device_id={"frames": lax.rem(fr + i, 32)}, device_id_type=MESH
        )
        return carry

    lax.fori_loop(1, 32, one, 0)


def spatial_kernel_body(
    lat,
    gain,
    shift,
    wk,
    bias,
    slots,
    A,
    AX,
    clip,
    G,
    X,
    F,
    R,
    edge_out,
    edge_in,
    RM,
    S,
    EX,
    acc,
    pieces,
    stats,
    scales,
    slot_sums,
    slot_sent,
    slot_all,
    clip_all,
    slot_pad,
    groups_of,
    clip_pick,
    send,
    recv,
    piece_send,
    piece_recv,
    piece_own,
    small_send,
    small_recv,
    lat_sem,
    a2a_send,
    a2a_recv,
    a2a_own,
):
    fr = lax.axis_index("frames")
    y = lax.axis_index("rows")
    core = lax.rem(fr, 2)
    chip = lax.div(fr, 2)
    x = lax.rem(chip, 4)
    z = lax.div(chip, 4)
    u = x + core * (z - x)
    w = z + core * (x - z)
    part = lax.rem(y, 2)

    def wrap(v):
        return lax.rem(v + 4, 4)

    def same_core(u_, w_):
        return (((w_ + core * (u_ - w_)) * 4) + u_ + core * (w_ - u_)) * 2 + core

    u_up = {"frames": same_core(wrap(u + 1), w)}
    u_dn = {"frames": same_core(wrap(u - 1), w)}
    w_up = {"frames": same_core(u, wrap(w + 1))}
    w_dn = {"frames": same_core(u, wrap(w - 1))}
    sib = {"frames": fr + 1 - 2 * core}
    y_up = {"rows": wrap(y + 1)}
    y_dn = {"rows": wrap(y - 1)}
    y_op = {"rows": wrap(y + 2)}
    barrier = pltpu.get_barrier_semaphore()
    for peer in (y_up, y_dn, y_op):
        pl.semaphore_signal(barrier, inc=1, device_id=peer, device_id_type=MESH)
    greet_plane(barrier, fr)
    lat_copy = pltpu.make_async_copy(lat, R, lat_sem)
    lat_copy.start()

    plane_tap = 3 * part

    def piece_cols(s, c):
        return pl.ds(pl.multiple_of(256 * s + 128 * c, 128), 128)

    def piece_copy(s):
        return pltpu.make_async_remote_copy(
            src_ref=wk.at[pl.ds(plane_tap, 6), :, piece_cols(s, 1 - core)],
            dst_ref=pieces.at[s, core],
            send_sem=piece_send.at[s],
            recv_sem=piece_recv.at[s],
            device_id=sib,
            device_id_type=MESH,
        )

    def piece_arrived(s):
        return pltpu.make_async_remote_copy(
            src_ref=pieces.at[s, 1 - core],
            dst_ref=pieces.at[s, 1 - core],
            send_sem=piece_send.at[s],
            recv_sem=piece_recv.at[s],
            device_id=sib,
            device_id_type=MESH,
        )

    def piece_local(s):
        return pltpu.make_async_copy(
            wk.at[pl.ds(plane_tap, 6), :, piece_cols(s, core)], pieces.at[s, core], piece_own.at[s]
        )

    for s in range(STAGES):
        piece_local(s).start()
    pl.semaphore_wait(barrier, 34)
    for s in range(STAGES):
        piece_copy(s).start()

    def small(src, dst, k, target):
        return pltpu.make_async_remote_copy(
            src_ref=src,
            dst_ref=dst,
            send_sem=small_send.at[k],
            recv_sem=small_recv.at[k],
            device_id=target,
            device_id_type=MESH,
        )

    def region(q, row, u0, count, tap, taps):
        return G.at[q, row, pl.ds(u0, count), pl.ds(tap, taps)]

    def mover(k, s, ref, target):
        return pltpu.make_async_remote_copy(
            src_ref=ref,
            dst_ref=ref,
            send_sem=send.at[s, k],
            recv_sem=recv.at[s, k],
            device_id=target,
            device_id_type=MESH,
        )

    rows = [w, wrap(w - 1), wrap(w + 1), wrap(w + 2)]
    sib_rows = [u, wrap(u - 1), wrap(u + 1), wrap(u + 2)]
    out_tap = 6 * part
    in_tap = 6 * (1 - part)
    pending = []

    def go(k, s, ref, target):
        copy = mover(k, s, ref, target)
        copy.start()
        pending.append(copy)

    def arrived(k, s, ref, source):
        mover(k, s, ref, source).wait_recv()

    def spread(i, s):
        q = 2 * s + core
        go(8 + 2 * i, s, region(q, rows[i], 0, 2, out_tap, 3), y_up)
        go(9 + 2 * i, s, region(q, rows[i], 2, 2, out_tap, 3), y_dn)
        go(16 + i, s, region(q, rows[i], 0, 4, plane_tap, 6), sib)

    def event0(s):
        piece_local(s).wait()
        piece_arrived(s).wait_recv()
        q = 2 * s + core

        def one(t, carry):
            both = jnp.concatenate(
                [pieces[s, 0, t].astype(jnp.float32), pieces[s, 1, t].astype(jnp.float32)], axis=0
            )
            G[q, w, u, plane_tap + t] = both.astype(jnp.bfloat16)
            return carry

        lax.fori_loop(0, 6, one, 0)
        unit = region(q, w, u, 1, plane_tap, 6)
        go(0, s, unit, u_up)
        go(1, s, unit, u_dn)

    def event1(s):
        q = 2 * s + core
        um, up = wrap(u - 1), wrap(u + 1)
        arrived(0, s, region(q, w, um, 1, plane_tap, 6), u_dn)
        go(2, s, region(q, w, um, 1, plane_tap, 3), u_up)
        arrived(1, s, region(q, w, up, 1, plane_tap, 6), u_up)
        go(3, s, region(q, w, up, 1, plane_tap + 3, 3), u_dn)

    def event2(s):
        q = 2 * s + core
        uo = wrap(u + 2)
        arrived(2, s, region(q, w, uo, 1, plane_tap, 3), u_dn)
        arrived(3, s, region(q, w, uo, 1, plane_tap + 3, 3), u_up)
        unit = region(q, w, 0, 4, plane_tap, 6)
        go(4, s, unit, w_up)
        go(5, s, unit, w_dn)
        spread(0, s)

    def event3(s):
        q = 2 * s + core
        arrived(4, s, region(q, rows[1], 0, 4, plane_tap, 6), w_dn)
        go(6, s, region(q, rows[1], 0, 2, plane_tap, 6), w_up)
        arrived(5, s, region(q, rows[2], 0, 4, plane_tap, 6), w_up)
        go(7, s, region(q, rows[2], 2, 2, plane_tap, 6), w_dn)
        spread(1, s)
        spread(2, s)

    def event4(s):
        q = 2 * s + core
        arrived(6, s, region(q, rows[3], 0, 2, plane_tap, 6), w_dn)
        arrived(7, s, region(q, rows[3], 2, 2, plane_tap, 6), w_up)
        spread(3, s)
        for i in range(3):
            from_y(i, s)

    def from_y(i, s):
        q = 2 * s + core
        arrived(8 + 2 * i, s, region(q, rows[i], 0, 2, in_tap, 3), y_dn)
        arrived(9 + 2 * i, s, region(q, rows[i], 2, 2, in_tap, 3), y_up)
        go(20 + i, s, region(q, rows[i], 0, 4, in_tap, 3), sib)

    def event5(s):
        from_y(3, s)
        q = 2 * s + 1 - core
        for i in range(4):
            arrived(16 + i, s, region(q, sib_rows[i], 0, 4, plane_tap, 6), sib)

    def event6(s):
        q = 2 * s + 1 - core
        for i in range(4):
            arrived(20 + i, s, region(q, sib_rows[i], 0, 4, in_tap, 3), sib)

    def taps(s, a):
        for b in range(3):
            t = a * 3 + b
            even = G[2 * s, :, :, t].reshape(C, 128)
            odd = jnp.concatenate(
                [G[2 * s + 1, i, j, t] for j in range(4) for i in range(4)], axis=0
            )
            kernel = jnp.concatenate([even, odd], axis=1)
            window = X[a, :, b * 16 : b * 16 + 288, :].reshape(576, C)
            acc[...] += jnp.dot(window, kernel, preferred_element_type=jnp.float32)

    def conv(s):
        def one(i, carry):
            a = 1 + i * (2 * part - 1)
            taps(s, a)
            return carry

        acc[...] = jnp.zeros_like(acc)
        lax.fori_loop(0, 2, one, 0)
        event6(s)
        taps(s, 2 * (1 - part))
        for n in range(2):
            q = 2 * s + n
            base = RM[:, q].reshape(576, 128).astype(jnp.float32)
            value = base + acc[:, 128 * n : 128 * n + 128]
            value = value + bias[q * 128 : q * 128 + 128].reshape(1, 128)
            value = jnp.where(jnp.abs(value) < 3.3e38, value, 0.0).astype(jnp.bfloat16)
            S[:, q] = value.reshape(36, 16, 128)

    def each_peer(start):
        def one(i, carry):
            start(lax.rem(fr + i, 32))
            return carry

        lax.fori_loop(1, 32, one, 0)

    def finish(s):
        span = slice(2 * s, 2 * s + 2)
        each_peer(
            lambda d: pltpu.make_async_remote_copy(
                src_ref=S.at[d, span],
                dst_ref=A.at[fr, span],
                send_sem=a2a_send.at[s],
                recv_sem=a2a_recv.at[s],
                device_id={"frames": d},
                device_id_type=MESH,
            ).start()
        )
        pltpu.make_async_copy(S.at[fr, span], A.at[fr, span], a2a_own.at[s]).start()
        if s in (1, 3, 4):
            send_extra(s // 2)
        for q in range(2 * s, 2 * s + 2):
            value = S[:, q].astype(jnp.float32)
            slot_sums[q] = by_slot(jnp.sum(value, axis=0), jnp.sum(value * value, axis=0))

    def wait_tiles(s):
        span = slice(2 * s, 2 * s + 2)
        pltpu.make_async_copy(S.at[fr, span], A.at[fr, span], a2a_own.at[s]).wait()
        wait_all(S.at[0:31, span], A.at[0:31, span], s)

    def wait_all(src, dst, k):
        both = pltpu.make_async_remote_copy(
            src_ref=src,
            dst_ref=dst,
            send_sem=a2a_send.at[k],
            recv_sem=a2a_recv.at[k],
            device_id=sib,
            device_id_type=MESH,
        )
        both.wait_send()
        both.wait_recv()

    def send_extra(m):
        for t in range(4):
            lanes = [S[32 + t, q].astype(jnp.float32) for q in range(4 * m, min(4 * m + 4, LANES))]
            for r in range(4):
                picked = [v[4 * r : 4 * r + 4] for v in lanes]
                picked += [jnp.zeros((4, 128), jnp.float32)] * (4 - len(lanes))
                EX[4 * t + r, m] = jnp.concatenate(picked, axis=0).astype(jnp.bfloat16)
        each_peer(
            lambda d: pltpu.make_async_remote_copy(
                src_ref=EX.at[lax.div(d, 2), m],
                dst_ref=AX.at[fr, m],
                send_sem=a2a_send.at[5 + m],
                recv_sem=a2a_recv.at[5 + m],
                device_id={"frames": d},
                device_id_type=MESH,
            ).start()
        )
        pltpu.make_async_copy(EX.at[chip, m], AX.at[fr, m], a2a_own.at[5 + m]).start()

    def wait_extra(m):
        pltpu.make_async_copy(EX.at[chip, m], AX.at[fr, m], a2a_own.at[5 + m]).wait()
        wait_all(AX.at[0:31, m], AX.at[0:31, m], 5 + m)

    def send_sums():
        grouped = to_groups([slot_sums[l] for l in range(LANES)], groups_of[...])
        grouped = jnp.minimum(jnp.maximum(grouped, -3e38), 3e38)
        slot_sent[...] = grouped
        slot_all[fr] = grouped

        each_peer(
            lambda d: pltpu.make_async_remote_copy(
                src_ref=slot_sent,
                dst_ref=slot_all.at[fr],
                send_sem=a2a_send.at[8],
                recv_sem=a2a_recv.at[8],
                device_id={"frames": d},
                device_id_type=MESH,
            ).start()
        )

    def prepare():
        groups_of[...] = member((C, 128), 0)
        row, col = slot_vectors(slots, slot_pad)
        kind = lax.shift_right_logical(iota((8, 128), 0), 2)
        video = jnp.bitwise_and(iota((8, 128), 0), 3) * 25
        j = iota((8, 128), 1)
        pick = flag((j >= video) & (j < video + 25))
        entry = iota((128, 256), 1)
        slot_of = lax.shift_right_logical(entry, 3) * 4 + jnp.bitwise_and(entry, 3)
        match = flag(col == slot_of.astype(jnp.float32))
        pick = jnp.dot(pick, match, preferred_element_type=jnp.float32)
        same = jnp.bitwise_and(lax.shift_right_logical(iota((8, 256), 1), 2), 1) == (
            lax.shift_right_logical(iota((8, 256), 0), 2)
        )
        clip_pick[...] = jnp.where(same, pick, 0.0).astype(jnp.bfloat16)

    def clip_sums():
        wait_all(slot_all.at[0:31], slot_all.at[0:31], 8)
        clip_all[y] = exact_pick(clip_pick[...], slot_all[...].reshape(256, 128))
        for k, peer in ((5, y_up), (6, y_dn), (7, y_op)):
            small(clip_all.at[y], clip_all.at[y], k, peer).start()
        for k, o, peer in ((5, 3, y_up), (6, 1, y_dn), (7, 2, y_op)):
            source = clip_all.at[wrap(y + o)]
            small(source, source, k, peer).wait_recv()
        clip[...] = (clip_all[0] + clip_all[1]) + (clip_all[2] + clip_all[3])

    def own_rows():
        lat_copy.wait()

        def fill(c, carry):
            for s in range(4):
                for l in range(LANES):
                    F[l, c, pl.ds(4 + s, 8, stride=4), :] = R[
                        s, c, :, l * 128 : l * 128 + 128
                    ].astype(jnp.float32)
            return carry

        lax.fori_loop(0, 18, fill, 0)

        def edges(l, carry):
            edge_out[0, l] = F[l, :, 32:36, :].astype(jnp.bfloat16)
            edge_out[1, l] = F[l, :, 4:8, :].astype(jnp.bfloat16)
            return carry

        lax.fori_loop(0, LANES, edges, 0)
        small(edge_out.at[0], edge_in.at[0], 0, y_up).start()
        small(edge_out.at[1], edge_in.at[1], 1, y_dn).start()

        def sums(l, carry):
            cols = pl.ds(pl.multiple_of(l * 128, 128), 128)
            total, square = [], []
            for s in range(4):
                a = jnp.zeros((8, 128), jnp.float32)
                b = jnp.zeros((8, 128), jnp.float32)
                for c in range(18):
                    v = R[s, c, :, cols].astype(jnp.float32)
                    a = a + v
                    b = b + v * v
                total.append(jnp.sum(a, axis=0, keepdims=True))
                square.append(jnp.sum(b, axis=0, keepdims=True))
            stats[y, l] = jnp.concatenate(total + square, axis=0)
            return carry

        lax.fori_loop(0, LANES, sums, 0)
        for k, peer in ((2, y_up), (3, y_dn), (4, y_op)):
            small(stats.at[y], stats.at[y], k, peer).start()

    def norm_scales():
        for k, o, peer in ((2, 3, y_up), (3, 1, y_dn), (4, 2, y_op)):
            source = stats.at[wrap(y + o)]
            small(source, source, k, peer).wait_recv()
        grouped = to_groups(
            [(stats[0, l] + stats[1, l]) + (stats[2, l] + stats[3, l]) for l in range(LANES)],
            groups_of[...],
        )
        grouped = grouped * (1.0 / 23040.0)
        mean = grouped[0:4]
        rate = lax.rsqrt(grouped[4:8] - mean * mean + EPS)
        both = jnp.concatenate([rate, mean * rate], axis=0)
        channels = to_channels(both)
        for l in range(LANES):
            wide = channels[:, l * 128 : l * 128 + 128]
            g = gain[l * 128 : l * 128 + 128].reshape(1, 128)
            b = shift[l * 128 : l * 128 + 128].reshape(1, 128)
            up = wide[0:4] * g
            down = b - wide[4:8] * g
            scales[l] = jnp.concatenate([up, up, down, down], axis=0)

    def edge_rows():
        small(edge_out.at[0], edge_in.at[0], 0, y_up).wait_recv()
        small(edge_out.at[1], edge_in.at[1], 1, y_dn).wait_recv()

        def one(l, carry):
            F[l, :, 0:4, :] = edge_in[0, l].astype(jnp.float32)
            F[l, :, 36:40, :] = edge_in[1, l].astype(jnp.float32)
            return carry

        lax.fori_loop(0, LANES, one, 0)

    def window_rows():
        first = jnp.where(y == 0, 4, 0)
        last = jnp.where(y == 3, 36, 40)

        def one(c, carry):
            line = iota((40, 128), 0)
            inside = (line >= first) & (line < last)
            at = pl.ds(pl.multiple_of(c * 16 + 16, 16), 16)
            here_at = pl.ds(pl.multiple_of(c * 16, 16), 16)
            for l in range(LANES):
                raw = F[l, c]
                for h in range(2):
                    RM[h, l, here_at, :] = raw[16 * h + 4 : 16 * h + 20].astype(jnp.bfloat16)
                v = raw.reshape(5, 8, 128) * scales[l, 0:8][None] + scales[l, 8:16][None]
                v = (v * (1.0 / (1.0 + jnp.exp(-v)))).reshape(40, 128)
                v = jnp.where(inside, v, 0.0)
                for h in range(2):
                    for a in range(3):
                        X[a, h, at, l * 128 : l * 128 + 128] = v[
                            16 * h + 4 * a : 16 * h + 4 * a + 16
                        ].astype(jnp.bfloat16)
            return carry

        lax.fori_loop(0, 18, one, 0)

    for s in range(STAGES):
        event0(s)
    zero = jnp.zeros((16, C), jnp.bfloat16)
    for a in range(3):
        for h in range(2):
            X[a, h, 0:16, :] = zero
            X[a, h, 304:320, :] = zero
    event1(0)
    event1(1)
    event2(0)
    own_rows()
    prepare()
    event1(2)
    event2(1)
    event3(0)
    event1(3)
    norm_scales()
    edge_rows()
    event2(2)
    event3(1)
    event4(0)
    event1(4)
    window_rows()
    event2(3)
    event3(2)
    event4(1)
    event5(0)
    conv(0)
    finish(0)
    event2(4)
    event3(3)
    event4(2)
    event5(1)
    conv(1)
    finish(1)
    event3(4)
    event4(3)
    event5(2)
    conv(2)
    finish(2)
    event4(4)
    event5(3)
    conv(3)
    finish(3)
    event5(4)
    conv(4)
    finish(4)
    send_sums()
    clip_sums()
    for s in range(STAGES):
        wait_tiles(s)
    for m in range(3):
        wait_extra(m)
    for copy in pending:
        copy.wait_send()
    for s in range(STAGES):
        piece_copy(s).wait_send()
    small(edge_out.at[0], edge_in.at[0], 0, y_up).wait_send()
    small(edge_out.at[1], edge_in.at[1], 1, y_dn).wait_send()
    for k, peer in ((2, y_up), (3, y_dn), (4, y_op)):
        small(stats.at[y], stats.at[y], k, peer).wait_send()
    for k, peer in ((5, y_up), (6, y_dn), (7, y_op)):
        small(clip_all.at[y], clip_all.at[y], k, peer).wait_send()


def spatial_section(latents, gain, shift, kernel, bias, slots):
    vmem = pl.BlockSpec(memory_space=pltpu.VMEM)
    anywhere = pl.BlockSpec(memory_space=pl.ANY)
    dma = pltpu.SemaphoreType.DMA
    return pl.pallas_call(
        spatial_kernel_body,
        out_shape=(
            jax.ShapeDtypeStruct((32, LANES, 16, 128), jnp.bfloat16),
            jax.ShapeDtypeStruct((32, 3, 16, 128), jnp.bfloat16),
            jax.ShapeDtypeStruct((8, 128), jnp.float32),
        ),
        in_specs=[anywhere, vmem, vmem, anywhere, vmem, vmem],
        out_specs=(vmem, vmem, vmem),
        scratch_shapes=[
            pltpu.VMEM((2 * STAGES, 4, 4, 9, 80, 128), jnp.bfloat16),
            pltpu.VMEM((3, 2, 320, C), jnp.bfloat16),
            pltpu.VMEM((LANES, 18, 40, 128), jnp.float32),
            pltpu.VMEM((4, 18, 8, C), jnp.bfloat16),
            pltpu.VMEM((2, LANES, 18, 4, 128), jnp.bfloat16),
            pltpu.VMEM((2, LANES, 18, 4, 128), jnp.bfloat16),
            pltpu.VMEM((2, LANES, 288, 128), jnp.bfloat16),
            pltpu.VMEM((36, LANES, 16, 128), jnp.bfloat16),
            pltpu.VMEM((16, 3, 16, 128), jnp.bfloat16),
            pltpu.VMEM((576, 256), jnp.float32),
            pltpu.VMEM((STAGES, 2, 6, 40, 128), jnp.bfloat16),
            pltpu.VMEM((4, LANES, 8, 128), jnp.float32),
            pltpu.VMEM((LANES, 16, 128), jnp.float32),
            pltpu.VMEM((LANES, 8, 128), jnp.float32),
            pltpu.VMEM((8, 128), jnp.float32),
            pltpu.VMEM((32, 8, 128), jnp.float32),
            pltpu.VMEM((4, 8, 128), jnp.float32),
            pltpu.VMEM((1, 128), jnp.int32),
            pltpu.VMEM((C, 128), jnp.bfloat16),
            pltpu.VMEM((8, 256), jnp.bfloat16),
            dma((STAGES, KINDS)),
            dma((STAGES, KINDS)),
            dma((STAGES,)),
            dma((STAGES,)),
            dma((STAGES,)),
            dma((8,)),
            dma((8,)),
            dma,
            dma((9,)),
            dma((9,)),
            dma((8,)),
        ],
        compiler_params=pltpu.CompilerParams(
            collective_id=0, has_side_effects=True, vmem_limit_bytes=60 * 1024 * 1024
        ),
        cost_estimate=pl.CostEstimate(
            flops=2 * 576 * 9 * C * C, bytes_accessed=40_000_000, transcendentals=2_000_000
        ),
        name="spatial",
    )(
        latents.transpose(0, 2, 1, 3), gain, shift, kernel.reshape(9, 40, C), bias, slots[None]
    )


def temporal_kernel_body(
    A,
    AX,
    clip,
    slots,
    wt,
    gain,
    shift,
    bias,
    out,
    O,
    turned,
    W,
    H,
    RF,
    HE,
    RE,
    OM,
    OX,
    BX,
    back,
    back_extra,
    scale_rows,
    slot_pad,
    w_sem,
    send,
    recv,
    own,
):
    fr = lax.axis_index("frames")
    core = lax.rem(fr, 2)
    sib = {"frames": fr + 1 - 2 * core}
    loads = [
        pltpu.make_async_copy(
            wt.at[:, :, 256 * n : 256 * n + 256], W.at[:, :, 256 * n : 256 * n + 256], w_sem.at[n]
        )
        for n in range(5)
    ]
    for load in loads:
        load.start()
    barrier = pltpu.get_barrier_semaphore()
    greet_plane(barrier, fr)

    row, col = slot_vectors(slots, slot_pad)

    def entry_slot(entry):
        return lax.shift_right_logical(entry, 4) * 4 + jnp.bitwise_and(entry, 3)

    def entry_pixel(entry):
        return jnp.bitwise_and(lax.shift_right_logical(entry, 2), 3)

    match = flag(col == entry_slot(iota((128, 512), 1)).astype(jnp.float32))
    match_t = flag(entry_slot(iota((512, 128), 0)).astype(jnp.float32) == row)

    def frame_number(line, shift_bits):
        frame = lax.shift_right_logical(line, shift_bits)
        video = jnp.bitwise_and(lax.shift_right_logical(line, shift_bits - 2), 3)
        return video * 25 + frame

    def real(line, count):
        return line < count

    line = iota((400, 128), 0)
    which = flag(frame_number(line, 4) == iota((400, 128), 1))
    pick = jnp.dot(which, match, preferred_element_type=jnp.float32)
    pixel = jnp.bitwise_and(iota((400, 512), 0), 3)
    pick = jnp.where(pixel == entry_pixel(iota((400, 512), 1)), pick, 0.0).astype(jnp.bfloat16)
    line_t = iota((128, 400), 1)
    which_t = flag(frame_number(line_t, 4) == iota((128, 400), 0))
    pick_t = jnp.dot(match_t, which_t, preferred_element_type=jnp.float32)
    pixel_t = jnp.bitwise_and(iota((512, 400), 1), 3)
    back[...] = jnp.where(pixel_t == entry_pixel(iota((512, 400), 0)), pick_t, 0.0).astype(
        jnp.bfloat16
    )
    for n in range(5):
        both = jnp.concatenate(
            [A[:, 2 * n].reshape(512, 128), A[:, 2 * n + 1].reshape(512, 128)], axis=1
        )
        both = jnp.dot(pick, both, preferred_element_type=jnp.float32).astype(jnp.bfloat16)
        RF[:, n * 256 : n * 256 + 256] = both
    grouped = clip[...] * (1.0 / 576000.0)
    mean = grouped[0:4]
    rate = lax.rsqrt(grouped[4:8] - mean * mean + EPS)
    both = jnp.concatenate([rate, mean * rate], axis=0)
    H[0] = jnp.zeros((16, C), jnp.bfloat16)
    H[26] = jnp.zeros((16, C), jnp.bfloat16)
    channels = to_channels(both)
    for l in range(LANES):
        cols = slice(l * 128, l * 128 + 128)
        wide = channels[:, cols]
        a = wide[0:4] * gain[cols].reshape(1, 128)
        b = shift[cols].reshape(1, 128) - wide[4:8] * gain[cols].reshape(1, 128)
        for o, part in ((0, a), (16, b)):
            scale_rows[o : o + 16, cols] = jnp.concatenate(
                [jnp.broadcast_to(part[v : v + 1], (4, 128)) for v in range(4)], axis=0
            )
    def one(f, carry):
        for l in range(LANES):
            cols = slice(l * 128, l * 128 + 128)
            v = RF[pl.ds(pl.multiple_of(f * 16, 16), 16), cols].astype(jnp.float32)
            v = v * scale_rows[0:16, cols] + scale_rows[16:32, cols]
            v = v * (1.0 / (1.0 + jnp.exp(-v)))
            H[f + 1, :, cols] = v.astype(jnp.bfloat16)
        return carry

    lax.fori_loop(0, 25, one, 0)
    pl.semaphore_wait(barrier, 31)

    def spread(src, dst, k):
        def one(i, carry):
            d = lax.rem(fr + i, 32)
            pltpu.make_async_remote_copy(
                src_ref=src(d),
                dst_ref=dst(fr),
                send_sem=send.at[k],
                recv_sem=recv.at[k],
                device_id={"frames": d},
                device_id_type=MESH,
            ).start()
            return carry

        lax.fori_loop(1, 32, one, 0)
        pltpu.make_async_copy(src(fr), dst(fr), own.at[k]).start()

    def collect(src, dst, k):
        pltpu.make_async_copy(src(fr), dst(fr), own.at[k]).wait()
        whole = pltpu.make_async_remote_copy(
            src_ref=src(slice(0, 31)),
            dst_ref=dst(slice(0, 31)),
            send_sem=send.at[k],
            recv_sem=recv.at[k],
            device_id=sib,
            device_id_type=MESH,
        )
        whole.wait_send()
        whole.wait_recv()

    def chunk(n):
        cols = slice(256 * n, 256 * n + 256)
        return (lambda d: OM.at[d, :, cols]), (lambda d: O.at[d, :, cols])

    def mix(n):
        cols = slice(256 * n, 256 * n + 256)
        if n < 3:
            loads[n].wait()
        total = RF[:, cols].astype(jnp.float32) + bias[cols].reshape(1, 256)
        for k in range(3):
            total = total + jnp.dot(
                H[k : k + 25].reshape(400, C), W[k, :, cols], preferred_element_type=jnp.float32
            )
        placed = jnp.dot(back[...], total.astype(jnp.bfloat16), preferred_element_type=jnp.float32)
        OM[:, :, cols] = placed.astype(jnp.bfloat16).reshape(32, 16, 256)
        spread(*chunk(n), n)

    mix(0)
    line = iota((112, 128), 0)
    which = flag((frame_number(line, 2) == iota((112, 128), 1)) & (line < 100))
    extra = jnp.dot(which, match, preferred_element_type=jnp.float32)
    extra_pixel = entry_pixel(iota((112, 512), 1))
    line_t = iota((128, 112), 1)
    which_t = flag((frame_number(line_t, 2) == iota((128, 112), 0)) & (line_t < 100))
    extra_t = jnp.dot(match_t, which_t, preferred_element_type=jnp.float32)
    extra_pixel_t = entry_pixel(iota((512, 112), 0))
    for i in range(4):
        back_extra[i] = jnp.where(extra_pixel_t == i, extra_t, 0.0).astype(jnp.bfloat16)
    for i in range(4):
        picked = jnp.where(extra_pixel == i, extra, 0.0).astype(jnp.bfloat16)
        for m in range(3):
            if 4 * m + i < LANES:
                l = 4 * m + i
                RE[:, l * 128 : l * 128 + 128] = jnp.dot(
                    picked, AX[:, m].reshape(512, 128), preferred_element_type=jnp.float32
                ).astype(jnp.bfloat16)

    HE[0:8, :] = jnp.zeros((8, C), jnp.float32)
    HE[104:128, :] = jnp.zeros((24, C), jnp.float32)
    for l in range(LANES):
        cols = slice(l * 128, l * 128 + 128)
        a8 = jnp.concatenate([scale_rows[4 * v : 4 * v + 1, cols] for v in (0, 1, 2, 3, 0, 1, 2, 3)], axis=0)
        b8 = jnp.concatenate([scale_rows[16 + 4 * v : 17 + 4 * v, cols] for v in (0, 1, 2, 3, 0, 1, 2, 3)], axis=0)
        raw = RE[:, cols].astype(jnp.float32).reshape(14, 8, 128)
        v = raw * a8[None] + b8[None]
        v = (v * (1.0 / (1.0 + jnp.exp(-v)))).reshape(112, 128)
        HE[8:108, cols] = v[0:100]
    mix(1)
    mix(2)
    loads[3].wait()
    loads[4].wait()
    half = pl.multiple_of(core * 640, 128)
    total = RE[:, pl.ds(half, 640)].astype(jnp.float32) + bias[pl.ds(half, 640)].reshape(1, 640)
    for k in range(3):
        window = HE[4 + 4 * k : 116 + 4 * k, :].astype(jnp.bfloat16)
        total = total + jnp.dot(
            window, W[k, :, pl.ds(half, 640)], preferred_element_type=jnp.float32
        )
    mixed = total.astype(jnp.bfloat16)
    for m in range(2):
        placed = jnp.zeros((512, 128), jnp.float32)
        for i in range(4):
            l = 4 * m + i
            if l < 5:
                placed = placed + jnp.dot(
                    back_extra[i],
                    mixed[:, l * 128 : l * 128 + 128],
                    preferred_element_type=jnp.float32,
                )
        OX[:, m] = placed.astype(jnp.bfloat16).reshape(32, 16, 128)
    spread((lambda d: OX.at[d]), (lambda d: BX.at[d]), 5)
    mix(3)
    mix(4)
    collect((lambda d: OX.at[d]), (lambda d: BX.at[d]), 5)
    for t in range(4):
        for l in range(LANES):
            k, m, i = l // 5, (l % 5) // 4, (l % 5) % 4
            part = [
                BX[2 * (4 * t + r) + k, m].astype(jnp.float32)[4 * i : 4 * i + 4] for r in range(4)
            ]
            O[32 + t, :, l * 128 : l * 128 + 128] = jnp.concatenate(part, axis=0).astype(
                jnp.bfloat16
            )

    def turn(n):
        collect(*chunk(n), n)

        def place(c, carry):
            for k in range(2):
                cols = slice(256 * n + 128 * k, 256 * n + 128 * k + 128)
                turned[c, k, 0:16] = O[c, :, cols].astype(jnp.float32)
                turned[c, k, 16:32] = O[c + 18, :, cols].astype(jnp.float32)
            return carry

        def fetch(c, carry):
            for k in range(2):
                cols = slice(256 * n + 128 * k, 256 * n + 128 * k + 128)
                for s in range(4):
                    out[s, c, :, cols] = turned[c, k, pl.ds(s, 8, stride=4), :].astype(jnp.bfloat16)
            return carry

        lax.fori_loop(0, 18, place, 0)
        lax.fori_loop(0, 18, fetch, 0)

    for n in range(5):
        turn(n)


def temporal_section(A, AX, clip, slots, kernel, gain, shift, bias):
    vmem = pl.BlockSpec(memory_space=pltpu.VMEM)
    anywhere = pl.BlockSpec(memory_space=pl.ANY)
    dma = pltpu.SemaphoreType.DMA
    return pl.pallas_call(
        temporal_kernel_body,
        out_shape=jax.ShapeDtypeStruct((4, 18, 8, C), jnp.bfloat16),
        in_specs=[vmem, vmem, vmem, vmem, anywhere, vmem, vmem, vmem],
        out_specs=vmem,
        scratch_shapes=[
            pltpu.VMEM((36, 16, C), jnp.bfloat16),
            pltpu.VMEM((18, 2, 32, 128), jnp.float32),
            pltpu.VMEM((3, C, C), jnp.bfloat16),
            pltpu.VMEM((27, 16, C), jnp.bfloat16),
            pltpu.VMEM((400, C), jnp.bfloat16),
            pltpu.VMEM((128, C), jnp.float32),
            pltpu.VMEM((112, C), jnp.bfloat16),
            pltpu.VMEM((32, 16, C), jnp.bfloat16),
            pltpu.VMEM((32, 2, 16, 128), jnp.bfloat16),
            pltpu.VMEM((32, 2, 16, 128), jnp.bfloat16),
            pltpu.VMEM((512, 400), jnp.bfloat16),
            pltpu.VMEM((4, 512, 112), jnp.bfloat16),
            pltpu.VMEM((32, C), jnp.float32),
            pltpu.VMEM((1, 128), jnp.int32),
            dma((5,)),
            dma((6,)),
            dma((6,)),
            dma((6,)),
        ],
        compiler_params=pltpu.CompilerParams(
            collective_id=1, has_side_effects=True, vmem_limit_bytes=56 * 1024 * 1024
        ),
        cost_estimate=pl.CostEstimate(
            flops=2 * 500 * 3 * C * C, bytes_accessed=14_000_000, transcendentals=1_000_000
        ),
        name="temporal",
    )(A, AX, clip, slots[None], kernel, gain, shift, bias)


def body(
    latents,
    first_gain,
    first_shift,
    spatial_kernel,
    spatial_bias,
    second_gain,
    second_shift,
    temporal_kernel,
    temporal_bias,
    frame_slot,
):
    main, extra, clip = spatial_section(
        latents, first_gain, first_shift, spatial_kernel, spatial_bias, frame_slot
    )
    tiles = temporal_section(
        main, extra, clip, frame_slot, temporal_kernel, second_gain, second_shift, temporal_bias
    )
    return tiles.transpose(0, 2, 1, 3)


def solution(mesh):
    in_specs = (
        P("frames", "rows", None, None),
        P(),
        P(),
        P(None, None, "frames", None),
        P(),
        P(),
        P(),
        P(),
        P(),
        P(),
    )
    out_specs = P("frames", "rows", None, None)
    return jax.shard_map(body, mesh=mesh, in_specs=in_specs, out_specs=out_specs, check_vma=False)
```

```python
import jax
import jax.numpy as jnp
from jax import lax
from jax.experimental import pallas as pl
from jax.experimental.pallas import tpu as pltpu
from jax.sharding import PartitionSpec as P

EPS = 1e-06
MESH = pl.DeviceIdType.MESH
C = 1280
LANES = 10
STAGES = 5
KINDS = 24


def member(shape, channel_dim):
    channel = iota(shape, channel_dim)
    first = iota(shape, 1 - channel_dim) * 40
    return flag((channel >= first) & (channel < first + 40))


def exact_dot(a, b):
    rows = a.shape[0]
    high = a.astype(jnp.bfloat16)
    rest = a - high.astype(jnp.float32)
    middle = rest.astype(jnp.bfloat16)
    low = (rest - middle.astype(jnp.float32)).astype(jnp.bfloat16)
    parts = jnp.concatenate([high.astype(jnp.float32), middle.astype(jnp.float32), low.astype(jnp.float32)], axis=0)
    out = jnp.dot(parts.astype(jnp.bfloat16), b, preferred_element_type=jnp.float32)
    return (out[2 * rows :] + out[rows : 2 * rows]) + out[0:rows]


def exact_pick(pick, b):
    high = b.astype(jnp.bfloat16)
    rest = b - high.astype(jnp.float32)
    middle = rest.astype(jnp.bfloat16)
    low = (rest - middle.astype(jnp.float32)).astype(jnp.bfloat16)
    out = jnp.dot(
        pick, jnp.concatenate([high, middle, low], axis=1), preferred_element_type=jnp.float32
    )
    return (out[:, 256:384] + out[:, 128:256]) + out[:, 0:128]


def to_groups(tiles, groups_of):
    return exact_dot(jnp.concatenate(tiles, axis=1), groups_of)


def to_channels(groups):
    return exact_dot(groups, member((128, C), 1))


def iota(shape, dim):
    return lax.broadcasted_iota(jnp.int32, shape, dim)


def flag(mask):
    return jnp.where(mask, 1.0, 0.0).astype(jnp.bfloat16)


def by_slot(total, square):
    a = (total[0:4] + total[4:8]) + (total[8:12] + total[12:16])
    b = (square[0:4] + square[4:8]) + (square[8:12] + square[12:16])
    return jnp.concatenate([a, b], axis=0)


def slot_vectors(slots, padded):
    padded[...] = jnp.full((1, 128), -1, jnp.int32)
    padded[:, 0:100] = slots[...]
    row = padded[...].astype(jnp.float32)
    wide = jnp.broadcast_to(row, (128, 128))
    diagonal = jnp.where(iota((128, 128), 0) == iota((128, 128), 1), wide, 0.0)
    return row, jnp.sum(diagonal, axis=1, keepdims=True)


def greet_plane(barrier, fr):
    def one(i, carry):
        pl.semaphore_signal(
            barrier, inc=1, device_id={"frames": lax.rem(fr + i, 32)}, device_id_type=MESH
        )
        return carry

    lax.fori_loop(1, 32, one, 0)


def spatial_kernel_body(
    lat,
    gain,
    shift,
    wk,
    bias,
    slots,
    A,
    AX,
    clip,
    G,
    X,
    F,
    R,
    edge_out,
    edge_in,
    RM,
    S,
    EX,
    acc,
    pieces,
    stats,
    scales,
    slot_sums,
    slot_sent,
    slot_all,
    slot_pad,
    groups_of,
    clip_pick,
    send,
    recv,
    piece_send,
    piece_recv,
    piece_own,
    small_send,
    small_recv,
    lat_sem,
    a2a_send,
    a2a_recv,
    a2a_own,
):
    fr = lax.axis_index("frames")
    y = lax.axis_index("rows")
    core = lax.rem(fr, 2)
    chip = lax.div(fr, 2)
    x = lax.rem(chip, 4)
    z = lax.div(chip, 4)
    u = x + core * (z - x)
    w = z + core * (x - z)
    part = lax.rem(y, 2)

    def wrap(v):
        return lax.rem(v + 4, 4)

    def same_core(u_, w_):
        return (((w_ + core * (u_ - w_)) * 4) + u_ + core * (w_ - u_)) * 2 + core

    u_up = {"frames": same_core(wrap(u + 1), w)}
    u_dn = {"frames": same_core(wrap(u - 1), w)}
    w_up = {"frames": same_core(u, wrap(w + 1))}
    w_dn = {"frames": same_core(u, wrap(w - 1))}
    sib = {"frames": fr + 1 - 2 * core}
    y_up = {"rows": wrap(y + 1)}
    y_dn = {"rows": wrap(y - 1)}
    y_op = {"rows": wrap(y + 2)}
    barrier = pltpu.get_barrier_semaphore()
    for peer in (y_up, y_dn, y_op):
        pl.semaphore_signal(barrier, inc=1, device_id=peer, device_id_type=MESH)
    greet_plane(barrier, fr)
    lat_copy = pltpu.make_async_copy(lat, R, lat_sem)
    lat_copy.start()

    plane_tap = 3 * part

    def piece_cols(s, c):
        return pl.ds(pl.multiple_of(256 * s + 128 * c, 128), 128)

    def piece_copy(s):
        return pltpu.make_async_remote_copy(
            src_ref=wk.at[pl.ds(plane_tap, 6), :, piece_cols(s, 1 - core)],
            dst_ref=pieces.at[s, core],
            send_sem=piece_send.at[s],
            recv_sem=piece_recv.at[s],
            device_id=sib,
            device_id_type=MESH,
        )

    def piece_arrived(s):
        return pltpu.make_async_remote_copy(
            src_ref=pieces.at[s, 1 - core],
            dst_ref=pieces.at[s, 1 - core],
            send_sem=piece_send.at[s],
            recv_sem=piece_recv.at[s],
            device_id=sib,
            device_id_type=MESH,
        )

    def piece_local(s):
        return pltpu.make_async_copy(
            wk.at[pl.ds(plane_tap, 6), :, piece_cols(s, core)], pieces.at[s, core], piece_own.at[s]
        )

    for s in range(STAGES):
        piece_local(s).start()
    pl.semaphore_wait(barrier, 34)
    for s in range(STAGES):
        piece_copy(s).start()

    def small(src, dst, k, target):
        return pltpu.make_async_remote_copy(
            src_ref=src,
            dst_ref=dst,
            send_sem=small_send.at[k],
            recv_sem=small_recv.at[k],
            device_id=target,
            device_id_type=MESH,
        )

    def region(q, row, u0, count, tap, taps):
        return G.at[q, row, pl.ds(u0, count), pl.ds(tap, taps)]

    def mover(k, s, ref, target):
        return pltpu.make_async_remote_copy(
            src_ref=ref,
            dst_ref=ref,
            send_sem=send.at[s, k],
            recv_sem=recv.at[s, k],
            device_id=target,
            device_id_type=MESH,
        )

    rows = [w, wrap(w - 1), wrap(w + 1), wrap(w + 2)]
    sib_rows = [u, wrap(u - 1), wrap(u + 1), wrap(u + 2)]
    out_tap = 6 * part
    in_tap = 6 * (1 - part)
    pending = []

    def go(k, s, ref, target):
        copy = mover(k, s, ref, target)
        copy.start()
        pending.append(copy)

    def arrived(k, s, ref, source):
        mover(k, s, ref, source).wait_recv()

    def spread(i, s):
        q = 2 * s + core
        go(8 + 2 * i, s, region(q, rows[i], 0, 2, out_tap, 3), y_up)
        go(9 + 2 * i, s, region(q, rows[i], 2, 2, out_tap, 3), y_dn)
        go(16 + i, s, region(q, rows[i], 0, 4, plane_tap, 6), sib)

    def event0(s):
        piece_local(s).wait()
        piece_arrived(s).wait_recv()
        q = 2 * s + core

        def one(t, carry):
            both = jnp.concatenate(
                [pieces[s, 0, t].astype(jnp.float32), pieces[s, 1, t].astype(jnp.float32)], axis=0
            )
            G[q, w, u, plane_tap + t] = both.astype(jnp.bfloat16)
            return carry

        lax.fori_loop(0, 6, one, 0)
        unit = region(q, w, u, 1, plane_tap, 6)
        go(0, s, unit, u_up)
        go(1, s, unit, u_dn)

    def event1(s):
        q = 2 * s + core
        um, up = wrap(u - 1), wrap(u + 1)
        arrived(0, s, region(q, w, um, 1, plane_tap, 6), u_dn)
        go(2, s, region(q, w, um, 1, plane_tap, 3), u_up)
        arrived(1, s, region(q, w, up, 1, plane_tap, 6), u_up)
        go(3, s, region(q, w, up, 1, plane_tap + 3, 3), u_dn)

    def event2(s):
        q = 2 * s + core
        uo = wrap(u + 2)
        arrived(2, s, region(q, w, uo, 1, plane_tap, 3), u_dn)
        arrived(3, s, region(q, w, uo, 1, plane_tap + 3, 3), u_up)
        unit = region(q, w, 0, 4, plane_tap, 6)
        go(4, s, unit, w_up)
        go(5, s, unit, w_dn)
        spread(0, s)

    def event3(s):
        q = 2 * s + core
        arrived(4, s, region(q, rows[1], 0, 4, plane_tap, 6), w_dn)
        go(6, s, region(q, rows[1], 0, 2, plane_tap, 6), w_up)
        arrived(5, s, region(q, rows[2], 0, 4, plane_tap, 6), w_up)
        go(7, s, region(q, rows[2], 2, 2, plane_tap, 6), w_dn)
        spread(1, s)
        spread(2, s)

    def event4(s):
        q = 2 * s + core
        arrived(6, s, region(q, rows[3], 0, 2, plane_tap, 6), w_dn)
        arrived(7, s, region(q, rows[3], 2, 2, plane_tap, 6), w_up)
        spread(3, s)
        for i in range(3):
            from_y(i, s)

    def from_y(i, s):
        q = 2 * s + core
        arrived(8 + 2 * i, s, region(q, rows[i], 0, 2, in_tap, 3), y_dn)
        arrived(9 + 2 * i, s, region(q, rows[i], 2, 2, in_tap, 3), y_up)
        go(20 + i, s, region(q, rows[i], 0, 4, in_tap, 3), sib)

    def event5(s):
        from_y(3, s)
        q = 2 * s + 1 - core
        for i in range(4):
            arrived(16 + i, s, region(q, sib_rows[i], 0, 4, plane_tap, 6), sib)

    def event6(s):
        q = 2 * s + 1 - core
        for i in range(4):
            arrived(20 + i, s, region(q, sib_rows[i], 0, 4, in_tap, 3), sib)

    def taps(s, a):
        for b in range(3):
            t = a * 3 + b
            even = G[2 * s, :, :, t].reshape(C, 128)
            odd = jnp.concatenate(
                [G[2 * s + 1, i, j, t] for j in range(4) for i in range(4)], axis=0
            )
            kernel = jnp.concatenate([even, odd], axis=1)
            window = X[a, :, b * 16 : b * 16 + 288, :].reshape(576, C)
            acc[...] += jnp.dot(window, kernel, preferred_element_type=jnp.float32)

    def conv(s):
        def one(i, carry):
            a = 1 + i * (2 * part - 1)
            taps(s, a)
            return carry

        acc[...] = jnp.zeros_like(acc)
        lax.fori_loop(0, 2, one, 0)
        event6(s)
        taps(s, 2 * (1 - part))
        for n in range(2):
            q = 2 * s + n
            base = RM[:, q].reshape(576, 128).astype(jnp.float32)
            value = base + acc[:, 128 * n : 128 * n + 128]
            value = value + bias[q * 128 : q * 128 + 128].reshape(1, 128)
            value = jnp.where(jnp.abs(value) < 3.3e38, value, 0.0).astype(jnp.bfloat16)
            S[:, q] = value.reshape(36, 16, 128)

    def each_peer(start):
        def one(i, carry):
            start(lax.rem(fr + i, 32))
            return carry

        lax.fori_loop(1, 32, one, 0)

    def finish(s):
        span = slice(2 * s, 2 * s + 2)
        each_peer(
            lambda d: pltpu.make_async_remote_copy(
                src_ref=S.at[d, span],
                dst_ref=A.at[fr, span],
                send_sem=a2a_send.at[s],
                recv_sem=a2a_recv.at[s],
                device_id={"frames": d},
                device_id_type=MESH,
            ).start()
        )
        pltpu.make_async_copy(S.at[fr, span], A.at[fr, span], a2a_own.at[s]).start()
        if s in (1, 3, 4):
            send_extra(s // 2)
        for q in range(2 * s, 2 * s + 2):
            value = S[:, q].astype(jnp.float32)
            slot_sums[q] = by_slot(jnp.sum(value, axis=0), jnp.sum(value * value, axis=0))

    def wait_tiles(s):
        span = slice(2 * s, 2 * s + 2)
        pltpu.make_async_copy(S.at[fr, span], A.at[fr, span], a2a_own.at[s]).wait()
        wait_all(S.at[0:31, span], A.at[0:31, span], s)

    def wait_all(src, dst, k):
        both = pltpu.make_async_remote_copy(
            src_ref=src,
            dst_ref=dst,
            send_sem=a2a_send.at[k],
            recv_sem=a2a_recv.at[k],
            device_id=sib,
            device_id_type=MESH,
        )
        both.wait_send()
        both.wait_recv()

    def send_extra(m):
        for t in range(4):
            lanes = [S[32 + t, q].astype(jnp.float32) for q in range(4 * m, min(4 * m + 4, LANES))]
            for r in range(4):
                picked = [v[4 * r : 4 * r + 4] for v in lanes]
                picked += [jnp.zeros((4, 128), jnp.float32)] * (4 - len(lanes))
                EX[4 * t + r, m] = jnp.concatenate(picked, axis=0).astype(jnp.bfloat16)
        each_peer(
            lambda d: pltpu.make_async_remote_copy(
                src_ref=EX.at[lax.div(d, 2), m],
                dst_ref=AX.at[fr, m],
                send_sem=a2a_send.at[5 + m],
                recv_sem=a2a_recv.at[5 + m],
                device_id={"frames": d},
                device_id_type=MESH,
            ).start()
        )
        pltpu.make_async_copy(EX.at[chip, m], AX.at[fr, m], a2a_own.at[5 + m]).start()

    def wait_extra(m):
        pltpu.make_async_copy(EX.at[chip, m], AX.at[fr, m], a2a_own.at[5 + m]).wait()
        wait_all(AX.at[0:31, m], AX.at[0:31, m], 5 + m)

    def send_sums():
        grouped = to_groups([slot_sums[l] for l in range(LANES)], groups_of[...])
        grouped = jnp.minimum(jnp.maximum(grouped, -3e38), 3e38)
        slot_sent[...] = grouped
        slot_all[fr] = grouped

        each_peer(
            lambda d: pltpu.make_async_remote_copy(
                src_ref=slot_sent,
                dst_ref=slot_all.at[fr],
                send_sem=a2a_send.at[8],
                recv_sem=a2a_recv.at[8],
                device_id={"frames": d},
                device_id_type=MESH,
            ).start()
        )

    def prepare():
        groups_of[...] = member((C, 128), 0)
        row, col = slot_vectors(slots, slot_pad)
        kind = lax.shift_right_logical(iota((8, 128), 0), 2)
        video = jnp.bitwise_and(iota((8, 128), 0), 3) * 25
        j = iota((8, 128), 1)
        pick = flag((j >= video) & (j < video + 25))
        entry = iota((128, 256), 1)
        slot_of = lax.shift_right_logical(entry, 3) * 4 + jnp.bitwise_and(entry, 3)
        match = flag(col == slot_of.astype(jnp.float32))
        pick = jnp.dot(pick, match, preferred_element_type=jnp.float32)
        same = jnp.bitwise_and(lax.shift_right_logical(iota((8, 256), 1), 2), 1) == (
            lax.shift_right_logical(iota((8, 256), 0), 2)
        )
        clip_pick[...] = jnp.where(same, pick, 0.0).astype(jnp.bfloat16)

    def clip_sums():
        wait_all(slot_all.at[0:31], slot_all.at[0:31], 8)
        clip[...] = exact_pick(clip_pick[...], slot_all[...].reshape(256, 128))

    def own_rows():
        lat_copy.wait()

        def fill(c, carry):
            for s in range(4):
                for l in range(LANES):
                    F[l, c, pl.ds(4 + s, 8, stride=4), :] = R[
                        s, c, :, l * 128 : l * 128 + 128
                    ].astype(jnp.float32)
            return carry

        lax.fori_loop(0, 18, fill, 0)

        def edges(l, carry):
            edge_out[0, l] = F[l, :, 32:36, :].astype(jnp.bfloat16)
            edge_out[1, l] = F[l, :, 4:8, :].astype(jnp.bfloat16)
            return carry

        lax.fori_loop(0, LANES, edges, 0)
        small(edge_out.at[0], edge_in.at[0], 0, y_up).start()
        small(edge_out.at[1], edge_in.at[1], 1, y_dn).start()

        def sums(l, carry):
            cols = pl.ds(pl.multiple_of(l * 128, 128), 128)
            total, square = [], []
            for s in range(4):
                a = jnp.zeros((8, 128), jnp.float32)
                b = jnp.zeros((8, 128), jnp.float32)
                for c in range(18):
                    v = R[s, c, :, cols].astype(jnp.float32)
                    a = a + v
                    b = b + v * v
                total.append(jnp.sum(a, axis=0, keepdims=True))
                square.append(jnp.sum(b, axis=0, keepdims=True))
            stats[y, l] = jnp.concatenate(total + square, axis=0)
            return carry

        lax.fori_loop(0, LANES, sums, 0)
        for k, peer in ((2, y_up), (3, y_dn), (4, y_op)):
            small(stats.at[y], stats.at[y], k, peer).start()

    def norm_scales():
        for k, o, peer in ((2, 3, y_up), (3, 1, y_dn), (4, 2, y_op)):
            source = stats.at[wrap(y + o)]
            small(source, source, k, peer).wait_recv()
        grouped = to_groups(
            [(stats[0, l] + stats[1, l]) + (stats[2, l] + stats[3, l]) for l in range(LANES)],
            groups_of[...],
        )
        grouped = grouped * (1.0 / 23040.0)
        mean = grouped[0:4]
        rate = lax.rsqrt(grouped[4:8] - mean * mean + EPS)
        both = jnp.concatenate([rate, mean * rate], axis=0)
        channels = to_channels(both)
        for l in range(LANES):
            wide = channels[:, l * 128 : l * 128 + 128]
            g = gain[l * 128 : l * 128 + 128].reshape(1, 128)
            b = shift[l * 128 : l * 128 + 128].reshape(1, 128)
            up = wide[0:4] * g
            down = b - wide[4:8] * g
            scales[l] = jnp.concatenate([up, up, down, down], axis=0)

    def edge_rows():
        small(edge_out.at[0], edge_in.at[0], 0, y_up).wait_recv()
        small(edge_out.at[1], edge_in.at[1], 1, y_dn).wait_recv()

        def one(l, carry):
            F[l, :, 0:4, :] = edge_in[0, l].astype(jnp.float32)
            F[l, :, 36:40, :] = edge_in[1, l].astype(jnp.float32)
            return carry

        lax.fori_loop(0, LANES, one, 0)

    def window_rows():
        first = jnp.where(y == 0, 4, 0)
        last = jnp.where(y == 3, 36, 40)

        def one(c, carry):
            line = iota((40, 128), 0)
            inside = (line >= first) & (line < last)
            at = pl.ds(pl.multiple_of(c * 16 + 16, 16), 16)
            here_at = pl.ds(pl.multiple_of(c * 16, 16), 16)
            for l in range(LANES):
                raw = F[l, c]
                for h in range(2):
                    RM[h, l, here_at, :] = raw[16 * h + 4 : 16 * h + 20].astype(jnp.bfloat16)
                v = raw.reshape(5, 8, 128) * scales[l, 0:8][None] + scales[l, 8:16][None]
                v = (v * (1.0 / (1.0 + jnp.exp(-v)))).reshape(40, 128)
                v = jnp.where(inside, v, 0.0)
                for h in range(2):
                    for a in range(3):
                        X[a, h, at, l * 128 : l * 128 + 128] = v[
                            16 * h + 4 * a : 16 * h + 4 * a + 16
                        ].astype(jnp.bfloat16)
            return carry

        lax.fori_loop(0, 18, one, 0)

    for s in range(STAGES):
        event0(s)
    zero = jnp.zeros((16, C), jnp.bfloat16)
    for a in range(3):
        for h in range(2):
            X[a, h, 0:16, :] = zero
            X[a, h, 304:320, :] = zero
    event1(0)
    event1(1)
    event2(0)
    own_rows()
    prepare()
    event1(2)
    event2(1)
    event3(0)
    event1(3)
    norm_scales()
    edge_rows()
    event2(2)
    event3(1)
    event4(0)
    event1(4)
    window_rows()
    event2(3)
    event3(2)
    event4(1)
    event5(0)
    conv(0)
    finish(0)
    event2(4)
    event3(3)
    event4(2)
    event5(1)
    conv(1)
    finish(1)
    event3(4)
    event4(3)
    event5(2)
    conv(2)
    finish(2)
    event4(4)
    event5(3)
    conv(3)
    finish(3)
    event5(4)
    conv(4)
    finish(4)
    send_sums()
    clip_sums()
    for s in range(STAGES):
        wait_tiles(s)
    for m in range(3):
        wait_extra(m)
    for copy in pending:
        copy.wait_send()
    for s in range(STAGES):
        piece_copy(s).wait_send()
    small(edge_out.at[0], edge_in.at[0], 0, y_up).wait_send()
    small(edge_out.at[1], edge_in.at[1], 1, y_dn).wait_send()
    for k, peer in ((2, y_up), (3, y_dn), (4, y_op)):
        small(stats.at[y], stats.at[y], k, peer).wait_send()


def spatial_section(latents, gain, shift, kernel, bias, slots):
    vmem = pl.BlockSpec(memory_space=pltpu.VMEM)
    anywhere = pl.BlockSpec(memory_space=pl.ANY)
    dma = pltpu.SemaphoreType.DMA
    return pl.pallas_call(
        spatial_kernel_body,
        out_shape=(
            jax.ShapeDtypeStruct((32, LANES, 16, 128), jnp.bfloat16),
            jax.ShapeDtypeStruct((32, 3, 16, 128), jnp.bfloat16),
            jax.ShapeDtypeStruct((8, 128), jnp.float32),
        ),
        in_specs=[anywhere, vmem, vmem, anywhere, vmem, vmem],
        out_specs=(vmem, vmem, vmem),
        scratch_shapes=[
            pltpu.VMEM((2 * STAGES, 4, 4, 9, 80, 128), jnp.bfloat16),
            pltpu.VMEM((3, 2, 320, C), jnp.bfloat16),
            pltpu.VMEM((LANES, 18, 40, 128), jnp.float32),
            pltpu.VMEM((4, 18, 8, C), jnp.bfloat16),
            pltpu.VMEM((2, LANES, 18, 4, 128), jnp.bfloat16),
            pltpu.VMEM((2, LANES, 18, 4, 128), jnp.bfloat16),
            pltpu.VMEM((2, LANES, 288, 128), jnp.bfloat16),
            pltpu.VMEM((36, LANES, 16, 128), jnp.bfloat16),
            pltpu.VMEM((16, 3, 16, 128), jnp.bfloat16),
            pltpu.VMEM((576, 256), jnp.float32),
            pltpu.VMEM((STAGES, 2, 6, 40, 128), jnp.bfloat16),
            pltpu.VMEM((4, LANES, 8, 128), jnp.float32),
            pltpu.VMEM((LANES, 16, 128), jnp.float32),
            pltpu.VMEM((LANES, 8, 128), jnp.float32),
            pltpu.VMEM((8, 128), jnp.float32),
            pltpu.VMEM((32, 8, 128), jnp.float32),
            pltpu.VMEM((1, 128), jnp.int32),
            pltpu.VMEM((C, 128), jnp.bfloat16),
            pltpu.VMEM((8, 256), jnp.bfloat16),
            dma((STAGES, KINDS)),
            dma((STAGES, KINDS)),
            dma((STAGES,)),
            dma((STAGES,)),
            dma((STAGES,)),
            dma((5,)),
            dma((5,)),
            dma,
            dma((9,)),
            dma((9,)),
            dma((8,)),
        ],
        compiler_params=pltpu.CompilerParams(
            collective_id=0, has_side_effects=True, vmem_limit_bytes=60 * 1024 * 1024
        ),
        cost_estimate=pl.CostEstimate(
            flops=2 * 576 * 9 * C * C, bytes_accessed=40_000_000, transcendentals=2_000_000
        ),
        name="spatial",
    )(
        latents.transpose(0, 2, 1, 3), gain, shift, kernel.reshape(9, 40, C), bias, slots[None]
    )


def temporal_kernel_body(
    A,
    AX,
    clip,
    slots,
    wt,
    gain,
    shift,
    bias,
    out,
    O,
    turned,
    W,
    H,
    RF,
    HE,
    RE,
    OM,
    OX,
    BX,
    back,
    back_extra,
    scale_rows,
    slot_pad,
    clip_all,
    w_sem,
    send,
    recv,
    own,
    clip_send,
    clip_recv,
):
    fr = lax.axis_index("frames")
    core = lax.rem(fr, 2)
    sib = {"frames": fr + 1 - 2 * core}
    loads = [
        pltpu.make_async_copy(
            wt.at[:, :, 256 * n : 256 * n + 256], W.at[:, :, 256 * n : 256 * n + 256], w_sem.at[n]
        )
        for n in range(5)
    ]
    for load in loads:
        load.start()
    barrier = pltpu.get_barrier_semaphore()
    y = lax.axis_index("rows")
    others = [lax.rem(y + n, 4) for n in (1, 2, 3)]
    for other in others:
        pl.semaphore_signal(
            barrier, inc=1, device_id={"rows": other}, device_id_type=MESH
        )
    greet_plane(barrier, fr)
    clip_all[y] = clip[...]

    def clip_copy(n, ref):
        return pltpu.make_async_remote_copy(
            src_ref=ref,
            dst_ref=ref,
            send_sem=clip_send.at[n],
            recv_sem=clip_recv.at[n],
            device_id={"rows": others[n]},
            device_id_type=MESH,
        )

    row, col = slot_vectors(slots, slot_pad)

    def entry_slot(entry):
        return lax.shift_right_logical(entry, 4) * 4 + jnp.bitwise_and(entry, 3)

    def entry_pixel(entry):
        return jnp.bitwise_and(lax.shift_right_logical(entry, 2), 3)

    match = flag(col == entry_slot(iota((128, 512), 1)).astype(jnp.float32))
    match_t = flag(entry_slot(iota((512, 128), 0)).astype(jnp.float32) == row)

    def frame_number(line, shift_bits):
        frame = lax.shift_right_logical(line, shift_bits)
        video = jnp.bitwise_and(lax.shift_right_logical(line, shift_bits - 2), 3)
        return video * 25 + frame

    def real(line, count):
        return line < count

    line = iota((400, 128), 0)
    which = flag(frame_number(line, 4) == iota((400, 128), 1))
    pick = jnp.dot(which, match, preferred_element_type=jnp.float32)
    pixel = jnp.bitwise_and(iota((400, 512), 0), 3)
    pick = jnp.where(pixel == entry_pixel(iota((400, 512), 1)), pick, 0.0).astype(jnp.bfloat16)
    for n in range(5):
        both = jnp.concatenate(
            [A[:, 2 * n].reshape(512, 128), A[:, 2 * n + 1].reshape(512, 128)], axis=1
        )
        both = jnp.dot(pick, both, preferred_element_type=jnp.float32).astype(jnp.bfloat16)
        RF[:, n * 256 : n * 256 + 256] = both
    pl.semaphore_wait(barrier, 34)
    for n in range(3):
        clip_copy(n, clip_all.at[y]).start()
    line_t = iota((128, 400), 1)
    which_t = flag(frame_number(line_t, 4) == iota((128, 400), 0))
    pick_t = jnp.dot(match_t, which_t, preferred_element_type=jnp.float32)
    pixel_t = jnp.bitwise_and(iota((512, 400), 1), 3)
    back[...] = jnp.where(pixel_t == entry_pixel(iota((512, 400), 0)), pick_t, 0.0).astype(
        jnp.bfloat16
    )
    for n in range(3):
        clip_copy(n, clip_all.at[lax.rem(y + 3 - n, 4)]).wait_recv()
    grouped = ((clip_all[0] + clip_all[1]) + (clip_all[2] + clip_all[3])) * (1.0 / 576000.0)
    mean = grouped[0:4]
    rate = lax.rsqrt(grouped[4:8] - mean * mean + EPS)
    both = jnp.concatenate([rate, mean * rate], axis=0)
    H[0] = jnp.zeros((16, C), jnp.bfloat16)
    H[26] = jnp.zeros((16, C), jnp.bfloat16)
    channels = to_channels(both)
    for l in range(LANES):
        cols = slice(l * 128, l * 128 + 128)
        wide = channels[:, cols]
        a = wide[0:4] * gain[cols].reshape(1, 128)
        b = shift[cols].reshape(1, 128) - wide[4:8] * gain[cols].reshape(1, 128)
        for o, part in ((0, a), (16, b)):
            scale_rows[o : o + 16, cols] = jnp.concatenate(
                [jnp.broadcast_to(part[v : v + 1], (4, 128)) for v in range(4)], axis=0
            )
    def one(f, carry):
        for l in range(LANES):
            cols = slice(l * 128, l * 128 + 128)
            v = RF[pl.ds(pl.multiple_of(f * 16, 16), 16), cols].astype(jnp.float32)
            v = v * scale_rows[0:16, cols] + scale_rows[16:32, cols]
            v = v * (1.0 / (1.0 + jnp.exp(-v)))
            H[f + 1, :, cols] = v.astype(jnp.bfloat16)
        return carry

    lax.fori_loop(0, 25, one, 0)

    def spread(src, dst, k):
        def one(i, carry):
            d = lax.rem(fr + i, 32)
            pltpu.make_async_remote_copy(
                src_ref=src(d),
                dst_ref=dst(fr),
                send_sem=send.at[k],
                recv_sem=recv.at[k],
                device_id={"frames": d},
                device_id_type=MESH,
            ).start()
            return carry

        lax.fori_loop(1, 32, one, 0)
        pltpu.make_async_copy(src(fr), dst(fr), own.at[k]).start()

    def collect(src, dst, k):
        pltpu.make_async_copy(src(fr), dst(fr), own.at[k]).wait()
        whole = pltpu.make_async_remote_copy(
            src_ref=src(slice(0, 31)),
            dst_ref=dst(slice(0, 31)),
            send_sem=send.at[k],
            recv_sem=recv.at[k],
            device_id=sib,
            device_id_type=MESH,
        )
        whole.wait_send()
        whole.wait_recv()

    def chunk(n):
        cols = slice(256 * n, 256 * n + 256)
        return (lambda d: OM.at[d, :, cols]), (lambda d: O.at[d, :, cols])

    def mix(n):
        cols = slice(256 * n, 256 * n + 256)
        if n < 3:
            loads[n].wait()
        total = RF[:, cols].astype(jnp.float32) + bias[cols].reshape(1, 256)
        for k in range(3):
            total = total + jnp.dot(
                H[k : k + 25].reshape(400, C), W[k, :, cols], preferred_element_type=jnp.float32
            )
        placed = jnp.dot(back[...], total.astype(jnp.bfloat16), preferred_element_type=jnp.float32)
        OM[:, :, cols] = placed.astype(jnp.bfloat16).reshape(32, 16, 256)
        spread(*chunk(n), n)

    mix(0)
    line = iota((112, 128), 0)
    which = flag((frame_number(line, 2) == iota((112, 128), 1)) & (line < 100))
    extra = jnp.dot(which, match, preferred_element_type=jnp.float32)
    extra_pixel = entry_pixel(iota((112, 512), 1))
    line_t = iota((128, 112), 1)
    which_t = flag((frame_number(line_t, 2) == iota((128, 112), 0)) & (line_t < 100))
    extra_t = jnp.dot(match_t, which_t, preferred_element_type=jnp.float32)
    extra_pixel_t = entry_pixel(iota((512, 112), 0))
    for i in range(4):
        back_extra[i] = jnp.where(extra_pixel_t == i, extra_t, 0.0).astype(jnp.bfloat16)
    for i in range(4):
        picked = jnp.where(extra_pixel == i, extra, 0.0).astype(jnp.bfloat16)
        for m in range(3):
            if 4 * m + i < LANES:
                l = 4 * m + i
                RE[:, l * 128 : l * 128 + 128] = jnp.dot(
                    picked, AX[:, m].reshape(512, 128), preferred_element_type=jnp.float32
                ).astype(jnp.bfloat16)

    HE[0:8, :] = jnp.zeros((8, C), jnp.float32)
    HE[104:128, :] = jnp.zeros((24, C), jnp.float32)
    for l in range(LANES):
        cols = slice(l * 128, l * 128 + 128)
        a8 = jnp.concatenate([scale_rows[4 * v : 4 * v + 1, cols] for v in (0, 1, 2, 3, 0, 1, 2, 3)], axis=0)
        b8 = jnp.concatenate([scale_rows[16 + 4 * v : 17 + 4 * v, cols] for v in (0, 1, 2, 3, 0, 1, 2, 3)], axis=0)
        raw = RE[:, cols].astype(jnp.float32).reshape(14, 8, 128)
        v = raw * a8[None] + b8[None]
        v = (v * (1.0 / (1.0 + jnp.exp(-v)))).reshape(112, 128)
        HE[8:108, cols] = v[0:100]
    mix(1)
    mix(2)
    loads[3].wait()
    loads[4].wait()
    half = pl.multiple_of(core * 640, 128)
    total = RE[:, pl.ds(half, 640)].astype(jnp.float32) + bias[pl.ds(half, 640)].reshape(1, 640)
    for k in range(3):
        window = HE[4 + 4 * k : 116 + 4 * k, :].astype(jnp.bfloat16)
        total = total + jnp.dot(
            window, W[k, :, pl.ds(half, 640)], preferred_element_type=jnp.float32
        )
    mixed = total.astype(jnp.bfloat16)
    for m in range(2):
        placed = jnp.zeros((512, 128), jnp.float32)
        for i in range(4):
            l = 4 * m + i
            if l < 5:
                placed = placed + jnp.dot(
                    back_extra[i],
                    mixed[:, l * 128 : l * 128 + 128],
                    preferred_element_type=jnp.float32,
                )
        OX[:, m] = placed.astype(jnp.bfloat16).reshape(32, 16, 128)
    spread((lambda d: OX.at[d]), (lambda d: BX.at[d]), 5)
    mix(3)
    mix(4)
    collect((lambda d: OX.at[d]), (lambda d: BX.at[d]), 5)
    for t in range(4):
        for l in range(LANES):
            k, m, i = l // 5, (l % 5) // 4, (l % 5) % 4
            part = [
                BX[2 * (4 * t + r) + k, m].astype(jnp.float32)[4 * i : 4 * i + 4] for r in range(4)
            ]
            O[32 + t, :, l * 128 : l * 128 + 128] = jnp.concatenate(part, axis=0).astype(
                jnp.bfloat16
            )

    def turn(n):
        collect(*chunk(n), n)

        def place(c, carry):
            for k in range(2):
                cols = slice(256 * n + 128 * k, 256 * n + 128 * k + 128)
                turned[c, k, 0:16] = O[c, :, cols].astype(jnp.float32)
                turned[c, k, 16:32] = O[c + 18, :, cols].astype(jnp.float32)
            return carry

        def fetch(c, carry):
            for k in range(2):
                cols = slice(256 * n + 128 * k, 256 * n + 128 * k + 128)
                for s in range(4):
                    out[s, c, :, cols] = turned[c, k, pl.ds(s, 8, stride=4), :].astype(jnp.bfloat16)
            return carry

        lax.fori_loop(0, 18, place, 0)
        lax.fori_loop(0, 18, fetch, 0)

    for n in range(5):
        turn(n)
    for n in range(3):
        clip_copy(n, clip_all.at[y]).wait_send()


def temporal_section(A, AX, clip, slots, kernel, gain, shift, bias):
    vmem = pl.BlockSpec(memory_space=pltpu.VMEM)
    anywhere = pl.BlockSpec(memory_space=pl.ANY)
    dma = pltpu.SemaphoreType.DMA
    return pl.pallas_call(
        temporal_kernel_body,
        out_shape=jax.ShapeDtypeStruct((4, 18, 8, C), jnp.bfloat16),
        in_specs=[vmem, vmem, vmem, vmem, anywhere, vmem, vmem, vmem],
        out_specs=vmem,
        scratch_shapes=[
            pltpu.VMEM((36, 16, C), jnp.bfloat16),
            pltpu.VMEM((18, 2, 32, 128), jnp.float32),
            pltpu.VMEM((3, C, C), jnp.bfloat16),
            pltpu.VMEM((27, 16, C), jnp.bfloat16),
            pltpu.VMEM((400, C), jnp.bfloat16),
            pltpu.VMEM((128, C), jnp.float32),
            pltpu.VMEM((112, C), jnp.bfloat16),
            pltpu.VMEM((32, 16, C), jnp.bfloat16),
            pltpu.VMEM((32, 2, 16, 128), jnp.bfloat16),
            pltpu.VMEM((32, 2, 16, 128), jnp.bfloat16),
            pltpu.VMEM((512, 400), jnp.bfloat16),
            pltpu.VMEM((4, 512, 112), jnp.bfloat16),
            pltpu.VMEM((32, C), jnp.float32),
            pltpu.VMEM((1, 128), jnp.int32),
            pltpu.VMEM((4, 8, 128), jnp.float32),
            dma((5,)),
            dma((6,)),
            dma((6,)),
            dma((6,)),
            dma((3,)),
            dma((3,)),
        ],
        compiler_params=pltpu.CompilerParams(
            collective_id=1, has_side_effects=True, vmem_limit_bytes=56 * 1024 * 1024
        ),
        cost_estimate=pl.CostEstimate(
            flops=2 * 500 * 3 * C * C, bytes_accessed=14_000_000, transcendentals=1_000_000
        ),
        name="temporal",
    )(A, AX, clip, slots[None], kernel, gain, shift, bias)


def body(
    latents,
    first_gain,
    first_shift,
    spatial_kernel,
    spatial_bias,
    second_gain,
    second_shift,
    temporal_kernel,
    temporal_bias,
    frame_slot,
):
    main, extra, clip = spatial_section(
        latents, first_gain, first_shift, spatial_kernel, spatial_bias, frame_slot
    )
    tiles = temporal_section(
        main, extra, clip, frame_slot, temporal_kernel, second_gain, second_shift, temporal_bias
    )
    return tiles.transpose(0, 2, 1, 3)


def solution(mesh):
    in_specs = (
        P("frames", "rows", None, None),
        P(),
        P(),
        P(None, None, "frames", None),
        P(),
        P(),
        P(),
        P(),
        P(),
        P(),
    )
    out_specs = P("frames", "rows", None, None)
    return jax.shard_map(body, mesh=mesh, in_specs=in_specs, out_specs=out_specs, check_vma=False)
```

```python
import jax
import jax.numpy as jnp
from jax import lax
from jax.experimental import pallas as pl
from jax.experimental.pallas import tpu as pltpu
from jax.sharding import PartitionSpec as P

EPS = 1e-06
MESH = pl.DeviceIdType.MESH
C = 1280
LANES = 10
STAGES = 5
KINDS = 24


def member(shape, channel_dim):
    channel = iota(shape, channel_dim)
    first = iota(shape, 1 - channel_dim) * 40
    return flag((channel >= first) & (channel < first + 40))


def exact_dot(a, b):
    rows = a.shape[0]
    high = a.astype(jnp.bfloat16)
    rest = a - high.astype(jnp.float32)
    middle = rest.astype(jnp.bfloat16)
    low = (rest - middle.astype(jnp.float32)).astype(jnp.bfloat16)
    parts = jnp.concatenate([high.astype(jnp.float32), middle.astype(jnp.float32), low.astype(jnp.float32)], axis=0)
    out = jnp.dot(parts.astype(jnp.bfloat16), b, preferred_element_type=jnp.float32)
    return (out[2 * rows :] + out[rows : 2 * rows]) + out[0:rows]


def exact_pick(pick, b):
    high = b.astype(jnp.bfloat16)
    rest = b - high.astype(jnp.float32)
    middle = rest.astype(jnp.bfloat16)
    low = (rest - middle.astype(jnp.float32)).astype(jnp.bfloat16)
    out = jnp.dot(
        pick, jnp.concatenate([high, middle, low], axis=1), preferred_element_type=jnp.float32
    )
    return (out[:, 256:384] + out[:, 128:256]) + out[:, 0:128]


def to_groups(tiles, groups_of):
    return exact_dot(jnp.concatenate(tiles, axis=1), groups_of)


def to_channels(groups):
    return exact_dot(groups, member((128, C), 1))


def iota(shape, dim):
    return lax.broadcasted_iota(jnp.int32, shape, dim)


def flag(mask):
    return jnp.where(mask, 1.0, 0.0).astype(jnp.bfloat16)


def by_slot(total, square):
    a = (total[0:4] + total[4:8]) + (total[8:12] + total[12:16])
    b = (square[0:4] + square[4:8]) + (square[8:12] + square[12:16])
    return jnp.concatenate([a, b], axis=0)


def slot_vectors(slots, padded):
    padded[...] = jnp.full((1, 128), -1, jnp.int32)
    padded[:, 0:100] = slots[...]
    row = padded[...].astype(jnp.float32)
    wide = jnp.broadcast_to(row, (128, 128))
    diagonal = jnp.where(iota((128, 128), 0) == iota((128, 128), 1), wide, 0.0)
    return row, jnp.sum(diagonal, axis=1, keepdims=True)


def greet_plane(barrier, fr):
    def one(i, carry):
        pl.semaphore_signal(
            barrier, inc=1, device_id={"frames": lax.rem(fr + i, 32)}, device_id_type=MESH
        )
        return carry

    lax.fori_loop(1, 32, one, 0)


def spatial_kernel_body(
    lat,
    gain,
    shift,
    wk,
    bias,
    slots,
    A,
    AX,
    clip,
    G,
    X,
    F,
    R,
    edge_out,
    edge_in,
    RM,
    S,
    EX,
    acc,
    pieces,
    stats,
    scales,
    slot_sums,
    slot_sent,
    slot_all,
    clip_all,
    slot_pad,
    groups_of,
    clip_pick,
    send,
    recv,
    piece_send,
    piece_recv,
    piece_own,
    small_send,
    small_recv,
    lat_sem,
    a2a_send,
    a2a_recv,
    a2a_own,
):
    fr = lax.axis_index("frames")
    y = lax.axis_index("rows")
    core = lax.rem(fr, 2)
    chip = lax.div(fr, 2)
    x = lax.rem(chip, 4)
    z = lax.div(chip, 4)
    u = x + core * (z - x)
    w = z + core * (x - z)
    part = lax.rem(y, 2)

    def wrap(v):
        return lax.rem(v + 4, 4)

    def same_core(u_, w_):
        return (((w_ + core * (u_ - w_)) * 4) + u_ + core * (w_ - u_)) * 2 + core

    u_up = {"frames": same_core(wrap(u + 1), w)}
    u_dn = {"frames": same_core(wrap(u - 1), w)}
    w_up = {"frames": same_core(u, wrap(w + 1))}
    w_dn = {"frames": same_core(u, wrap(w - 1))}
    sib = {"frames": fr + 1 - 2 * core}
    y_up = {"rows": wrap(y + 1)}
    y_dn = {"rows": wrap(y - 1)}
    y_op = {"rows": wrap(y + 2)}
    barrier = pltpu.get_barrier_semaphore()
    for peer in (y_up, y_dn, y_op):
        pl.semaphore_signal(barrier, inc=1, device_id=peer, device_id_type=MESH)
    greet_plane(barrier, fr)
    lat_copy = pltpu.make_async_copy(lat, R, lat_sem)
    lat_copy.start()

    plane_tap = 3 * part

    def piece_cols(s, c):
        return pl.ds(pl.multiple_of(256 * s + 128 * c, 128), 128)

    def piece_copy(s):
        return pltpu.make_async_remote_copy(
            src_ref=wk.at[pl.ds(plane_tap, 6), :, piece_cols(s, 1 - core)],
            dst_ref=pieces.at[s, core],
            send_sem=piece_send.at[s],
            recv_sem=piece_recv.at[s],
            device_id=sib,
            device_id_type=MESH,
        )

    def piece_arrived(s):
        return pltpu.make_async_remote_copy(
            src_ref=pieces.at[s, 1 - core],
            dst_ref=pieces.at[s, 1 - core],
            send_sem=piece_send.at[s],
            recv_sem=piece_recv.at[s],
            device_id=sib,
            device_id_type=MESH,
        )

    def piece_local(s):
        return pltpu.make_async_copy(
            wk.at[pl.ds(plane_tap, 6), :, piece_cols(s, core)], pieces.at[s, core], piece_own.at[s]
        )

    for s in range(STAGES):
        piece_local(s).start()
    pl.semaphore_wait(barrier, 34)
    for s in range(STAGES):
        piece_copy(s).start()

    def small(src, dst, k, target):
        return pltpu.make_async_remote_copy(
            src_ref=src,
            dst_ref=dst,
            send_sem=small_send.at[k],
            recv_sem=small_recv.at[k],
            device_id=target,
            device_id_type=MESH,
        )

    def region(q, row, u0, count, tap, taps):
        return G.at[q, row, pl.ds(u0, count), pl.ds(tap, taps)]

    def mover(k, s, ref, target):
        return pltpu.make_async_remote_copy(
            src_ref=ref,
            dst_ref=ref,
            send_sem=send.at[s, k],
            recv_sem=recv.at[s, k],
            device_id=target,
            device_id_type=MESH,
        )

    rows = [w, wrap(w - 1), wrap(w + 1), wrap(w + 2)]
    sib_rows = [u, wrap(u - 1), wrap(u + 1), wrap(u + 2)]
    out_tap = 6 * part
    in_tap = 6 * (1 - part)
    pending = []

    def go(k, s, ref, target):
        copy = mover(k, s, ref, target)
        copy.start()
        pending.append(copy)

    def arrived(k, s, ref, source):
        mover(k, s, ref, source).wait_recv()

    def spread(i, s):
        q = 2 * s + core
        go(8 + 2 * i, s, region(q, rows[i], 0, 2, out_tap, 3), y_up)
        go(9 + 2 * i, s, region(q, rows[i], 2, 2, out_tap, 3), y_dn)
        go(16 + i, s, region(q, rows[i], 0, 4, plane_tap, 6), sib)

    def event0(s):
        piece_local(s).wait()
        piece_arrived(s).wait_recv()
        q = 2 * s + core

        def one(t, carry):
            both = jnp.concatenate(
                [pieces[s, 0, t].astype(jnp.float32), pieces[s, 1, t].astype(jnp.float32)], axis=0
            )
            G[q, w, u, plane_tap + t] = both.astype(jnp.bfloat16)
            return carry

        lax.fori_loop(0, 6, one, 0)
        unit = region(q, w, u, 1, plane_tap, 6)
        go(0, s, unit, u_up)
        go(1, s, unit, u_dn)

    def event1(s):
        q = 2 * s + core
        um, up = wrap(u - 1), wrap(u + 1)
        arrived(0, s, region(q, w, um, 1, plane_tap, 6), u_dn)
        go(2, s, region(q, w, um, 1, plane_tap, 3), u_up)
        arrived(1, s, region(q, w, up, 1, plane_tap, 6), u_up)
        go(3, s, region(q, w, up, 1, plane_tap + 3, 3), u_dn)

    def event2(s):
        q = 2 * s + core
        uo = wrap(u + 2)
        arrived(2, s, region(q, w, uo, 1, plane_tap, 3), u_dn)
        arrived(3, s, region(q, w, uo, 1, plane_tap + 3, 3), u_up)
        unit = region(q, w, 0, 4, plane_tap, 6)
        go(4, s, unit, w_up)
        go(5, s, unit, w_dn)
        spread(0, s)

    def event3(s):
        q = 2 * s + core
        arrived(4, s, region(q, rows[1], 0, 4, plane_tap, 6), w_dn)
        go(6, s, region(q, rows[1], 0, 2, plane_tap, 6), w_up)
        arrived(5, s, region(q, rows[2], 0, 4, plane_tap, 6), w_up)
        go(7, s, region(q, rows[2], 2, 2, plane_tap, 6), w_dn)
        spread(1, s)
        spread(2, s)

    def event4(s):
        q = 2 * s + core
        arrived(6, s, region(q, rows[3], 0, 2, plane_tap, 6), w_dn)
        arrived(7, s, region(q, rows[3], 2, 2, plane_tap, 6), w_up)
        spread(3, s)
        for i in range(3):
            from_y(i, s)

    def from_y(i, s):
        q = 2 * s + core
        arrived(8 + 2 * i, s, region(q, rows[i], 0, 2, in_tap, 3), y_dn)
        arrived(9 + 2 * i, s, region(q, rows[i], 2, 2, in_tap, 3), y_up)
        go(20 + i, s, region(q, rows[i], 0, 4, in_tap, 3), sib)

    def event5(s):
        from_y(3, s)
        q = 2 * s + 1 - core
        for i in range(4):
            arrived(16 + i, s, region(q, sib_rows[i], 0, 4, plane_tap, 6), sib)

    def event6(s):
        q = 2 * s + 1 - core
        for i in range(4):
            arrived(20 + i, s, region(q, sib_rows[i], 0, 4, in_tap, 3), sib)

    def taps(s, a):
        for b in range(3):
            t = a * 3 + b
            even = G[2 * s, :, :, t].reshape(C, 128)
            odd = jnp.concatenate(
                [G[2 * s + 1, i, j, t] for j in range(4) for i in range(4)], axis=0
            )
            kernel = jnp.concatenate([even, odd], axis=1)
            window = X[a, :, b * 16 : b * 16 + 288, :].reshape(576, C)
            acc[...] += jnp.dot(window, kernel, preferred_element_type=jnp.float32)

    def conv(s):
        def one(i, carry):
            a = 1 + i * (2 * part - 1)
            taps(s, a)
            return carry

        acc[...] = jnp.zeros_like(acc)
        lax.fori_loop(0, 2, one, 0)
        event6(s)
        taps(s, 2 * (1 - part))
        for n in range(2):
            q = 2 * s + n
            base = RM[:, q].reshape(576, 128).astype(jnp.float32)
            value = base + acc[:, 128 * n : 128 * n + 128]
            value = value + bias[q * 128 : q * 128 + 128].reshape(1, 128)
            value = jnp.where(jnp.abs(value) < 3.3e38, value, 0.0).astype(jnp.bfloat16)
            S[:, q] = value.reshape(36, 16, 128)

    def each_peer(start):
        def one(i, carry):
            start(lax.rem(fr + i, 32))
            return carry

        lax.fori_loop(1, 32, one, 0)

    def finish(s):
        span = slice(2 * s, 2 * s + 2)
        for q in range(2 * s, 2 * s + 2):
            value = S[:, q].astype(jnp.float32)
            slot_sums[q] = by_slot(jnp.sum(value, axis=0), jnp.sum(value * value, axis=0))
        if s == STAGES - 1:
            send_sums()
        each_peer(
            lambda d: pltpu.make_async_remote_copy(
                src_ref=S.at[d, span],
                dst_ref=A.at[fr, span],
                send_sem=a2a_send.at[s],
                recv_sem=a2a_recv.at[s],
                device_id={"frames": d},
                device_id_type=MESH,
            ).start()
        )
        pltpu.make_async_copy(S.at[fr, span], A.at[fr, span], a2a_own.at[s]).start()
        if s in (1, 3, 4):
            send_extra(s // 2)

    def wait_tiles(s):
        span = slice(2 * s, 2 * s + 2)
        pltpu.make_async_copy(S.at[fr, span], A.at[fr, span], a2a_own.at[s]).wait()
        wait_all(S.at[0:31, span], A.at[0:31, span], s)

    def wait_all(src, dst, k):
        both = pltpu.make_async_remote_copy(
            src_ref=src,
            dst_ref=dst,
            send_sem=a2a_send.at[k],
            recv_sem=a2a_recv.at[k],
            device_id=sib,
            device_id_type=MESH,
        )
        both.wait_send()
        both.wait_recv()

    def send_extra(m):
        for t in range(4):
            lanes = [S[32 + t, q].astype(jnp.float32) for q in range(4 * m, min(4 * m + 4, LANES))]
            for r in range(4):
                picked = [v[4 * r : 4 * r + 4] for v in lanes]
                picked += [jnp.zeros((4, 128), jnp.float32)] * (4 - len(lanes))
                EX[4 * t + r, m] = jnp.concatenate(picked, axis=0).astype(jnp.bfloat16)
        each_peer(
            lambda d: pltpu.make_async_remote_copy(
                src_ref=EX.at[lax.div(d, 2), m],
                dst_ref=AX.at[fr, m],
                send_sem=a2a_send.at[5 + m],
                recv_sem=a2a_recv.at[5 + m],
                device_id={"frames": d},
                device_id_type=MESH,
            ).start()
        )
        pltpu.make_async_copy(EX.at[chip, m], AX.at[fr, m], a2a_own.at[5 + m]).start()

    def wait_extra(m):
        pltpu.make_async_copy(EX.at[chip, m], AX.at[fr, m], a2a_own.at[5 + m]).wait()
        wait_all(AX.at[0:31, m], AX.at[0:31, m], 5 + m)

    def send_sums():
        grouped = to_groups([slot_sums[l] for l in range(LANES)], groups_of[...])
        grouped = jnp.minimum(jnp.maximum(grouped, -3e38), 3e38)
        slot_sent[...] = grouped
        slot_all[fr] = grouped

        each_peer(
            lambda d: pltpu.make_async_remote_copy(
                src_ref=slot_sent,
                dst_ref=slot_all.at[fr],
                send_sem=a2a_send.at[8],
                recv_sem=a2a_recv.at[8],
                device_id={"frames": d},
                device_id_type=MESH,
            ).start()
        )

    def prepare():
        groups_of[...] = member((C, 128), 0)
        row, col = slot_vectors(slots, slot_pad)
        kind = lax.shift_right_logical(iota((8, 128), 0), 2)
        video = jnp.bitwise_and(iota((8, 128), 0), 3) * 25
        j = iota((8, 128), 1)
        pick = flag((j >= video) & (j < video + 25))
        entry = iota((128, 256), 1)
        slot_of = lax.shift_right_logical(entry, 3) * 4 + jnp.bitwise_and(entry, 3)
        match = flag(col == slot_of.astype(jnp.float32))
        pick = jnp.dot(pick, match, preferred_element_type=jnp.float32)
        same = jnp.bitwise_and(lax.shift_right_logical(iota((8, 256), 1), 2), 1) == (
            lax.shift_right_logical(iota((8, 256), 0), 2)
        )
        clip_pick[...] = jnp.where(same, pick, 0.0).astype(jnp.bfloat16)

    def clip_sums():
        wait_all(slot_all.at[0:31], slot_all.at[0:31], 8)
        clip_all[y] = exact_pick(clip_pick[...], slot_all[...].reshape(256, 128))
        for k, peer in ((5, y_up), (6, y_dn), (7, y_op)):
            small(clip_all.at[y], clip_all.at[y], k, peer).start()
        for k, o, peer in ((5, 3, y_up), (6, 1, y_dn), (7, 2, y_op)):
            source = clip_all.at[wrap(y + o)]
            small(source, source, k, peer).wait_recv()
        clip[...] = (clip_all[0] + clip_all[1]) + (clip_all[2] + clip_all[3])

    def own_rows():
        lat_copy.wait()

        def fill(c, carry):
            for s in range(4):
                for l in range(LANES):
                    F[l, c, pl.ds(4 + s, 8, stride=4), :] = R[
                        s, c, :, l * 128 : l * 128 + 128
                    ].astype(jnp.float32)
            return carry

        lax.fori_loop(0, 18, fill, 0)

        def edges(l, carry):
            edge_out[0, l] = F[l, :, 32:36, :].astype(jnp.bfloat16)
            edge_out[1, l] = F[l, :, 4:8, :].astype(jnp.bfloat16)
            return carry

        lax.fori_loop(0, LANES, edges, 0)
        small(edge_out.at[0], edge_in.at[0], 0, y_up).start()
        small(edge_out.at[1], edge_in.at[1], 1, y_dn).start()

        def sums(l, carry):
            cols = pl.ds(pl.multiple_of(l * 128, 128), 128)
            total, square = [], []
            for s in range(4):
                a = jnp.zeros((8, 128), jnp.float32)
                b = jnp.zeros((8, 128), jnp.float32)
                for c in range(18):
                    v = R[s, c, :, cols].astype(jnp.float32)
                    a = a + v
                    b = b + v * v
                total.append(jnp.sum(a, axis=0, keepdims=True))
                square.append(jnp.sum(b, axis=0, keepdims=True))
            stats[y, l] = jnp.concatenate(total + square, axis=0)
            return carry

        lax.fori_loop(0, LANES, sums, 0)
        for k, peer in ((2, y_up), (3, y_dn), (4, y_op)):
            small(stats.at[y], stats.at[y], k, peer).start()

    def norm_scales():
        for k, o, peer in ((2, 3, y_up), (3, 1, y_dn), (4, 2, y_op)):
            source = stats.at[wrap(y + o)]
            small(source, source, k, peer).wait_recv()
        grouped = to_groups(
            [(stats[0, l] + stats[1, l]) + (stats[2, l] + stats[3, l]) for l in range(LANES)],
            groups_of[...],
        )
        grouped = grouped * (1.0 / 23040.0)
        mean = grouped[0:4]
        rate = lax.rsqrt(grouped[4:8] - mean * mean + EPS)
        both = jnp.concatenate([rate, mean * rate], axis=0)
        channels = to_channels(both)
        for l in range(LANES):
            wide = channels[:, l * 128 : l * 128 + 128]
            g = gain[l * 128 : l * 128 + 128].reshape(1, 128)
            b = shift[l * 128 : l * 128 + 128].reshape(1, 128)
            up = wide[0:4] * g
            down = b - wide[4:8] * g
            scales[l] = jnp.concatenate([up, up, down, down], axis=0)

    def edge_rows():
        small(edge_out.at[0], edge_in.at[0], 0, y_up).wait_recv()
        small(edge_out.at[1], edge_in.at[1], 1, y_dn).wait_recv()

        def one(l, carry):
            F[l, :, 0:4, :] = edge_in[0, l].astype(jnp.float32)
            F[l, :, 36:40, :] = edge_in[1, l].astype(jnp.float32)
            return carry

        lax.fori_loop(0, LANES, one, 0)

    def window_rows():
        first = jnp.where(y == 0, 4, 0)
        last = jnp.where(y == 3, 36, 40)

        def one(c, carry):
            line = iota((40, 128), 0)
            inside = (line >= first) & (line < last)
            at = pl.ds(pl.multiple_of(c * 16 + 16, 16), 16)
            here_at = pl.ds(pl.multiple_of(c * 16, 16), 16)
            for l in range(LANES):
                raw = F[l, c]
                for h in range(2):
                    RM[h, l, here_at, :] = raw[16 * h + 4 : 16 * h + 20].astype(jnp.bfloat16)
                v = raw.reshape(5, 8, 128) * scales[l, 0:8][None] + scales[l, 8:16][None]
                v = (v * (1.0 / (1.0 + jnp.exp(-v)))).reshape(40, 128)
                v = jnp.where(inside, v, 0.0)
                for h in range(2):
                    for a in range(3):
                        X[a, h, at, l * 128 : l * 128 + 128] = v[
                            16 * h + 4 * a : 16 * h + 4 * a + 16
                        ].astype(jnp.bfloat16)
            return carry

        lax.fori_loop(0, 18, one, 0)

    for s in range(STAGES):
        event0(s)
    zero = jnp.zeros((16, C), jnp.bfloat16)
    for a in range(3):
        for h in range(2):
            X[a, h, 0:16, :] = zero
            X[a, h, 304:320, :] = zero
    event1(0)
    event1(1)
    event2(0)
    own_rows()
    prepare()
    event1(2)
    event2(1)
    event3(0)
    event1(3)
    norm_scales()
    edge_rows()
    event2(2)
    event3(1)
    event4(0)
    event1(4)
    window_rows()
    event2(3)
    event3(2)
    event4(1)
    event5(0)
    conv(0)
    finish(0)
    event2(4)
    event3(3)
    event4(2)
    event5(1)
    conv(1)
    finish(1)
    event3(4)
    event4(3)
    event5(2)
    conv(2)
    finish(2)
    event4(4)
    event5(3)
    conv(3)
    finish(3)
    event5(4)
    conv(4)
    finish(4)
    clip_sums()
    for s in range(STAGES):
        wait_tiles(s)
    for m in range(3):
        wait_extra(m)
    for copy in pending:
        copy.wait_send()
    for s in range(STAGES):
        piece_copy(s).wait_send()
    small(edge_out.at[0], edge_in.at[0], 0, y_up).wait_send()
    small(edge_out.at[1], edge_in.at[1], 1, y_dn).wait_send()
    for k, peer in ((2, y_up), (3, y_dn), (4, y_op)):
        small(stats.at[y], stats.at[y], k, peer).wait_send()
    for k, peer in ((5, y_up), (6, y_dn), (7, y_op)):
        small(clip_all.at[y], clip_all.at[y], k, peer).wait_send()


def spatial_section(latents, gain, shift, kernel, bias, slots):
    vmem = pl.BlockSpec(memory_space=pltpu.VMEM)
    anywhere = pl.BlockSpec(memory_space=pl.ANY)
    dma = pltpu.SemaphoreType.DMA
    return pl.pallas_call(
        spatial_kernel_body,
        out_shape=(
            jax.ShapeDtypeStruct((32, LANES, 16, 128), jnp.bfloat16),
            jax.ShapeDtypeStruct((32, 3, 16, 128), jnp.bfloat16),
            jax.ShapeDtypeStruct((8, 128), jnp.float32),
        ),
        in_specs=[anywhere, vmem, vmem, anywhere, vmem, vmem],
        out_specs=(vmem, vmem, vmem),
        scratch_shapes=[
            pltpu.VMEM((2 * STAGES, 4, 4, 9, 80, 128), jnp.bfloat16),
            pltpu.VMEM((3, 2, 320, C), jnp.bfloat16),
            pltpu.VMEM((LANES, 18, 40, 128), jnp.float32),
            pltpu.VMEM((4, 18, 8, C), jnp.bfloat16),
            pltpu.VMEM((2, LANES, 18, 4, 128), jnp.bfloat16),
            pltpu.VMEM((2, LANES, 18, 4, 128), jnp.bfloat16),
            pltpu.VMEM((2, LANES, 288, 128), jnp.bfloat16),
            pltpu.VMEM((36, LANES, 16, 128), jnp.bfloat16),
            pltpu.VMEM((16, 3, 16, 128), jnp.bfloat16),
            pltpu.VMEM((576, 256), jnp.float32),
            pltpu.VMEM((STAGES, 2, 6, 40, 128), jnp.bfloat16),
            pltpu.VMEM((4, LANES, 8, 128), jnp.float32),
            pltpu.VMEM((LANES, 16, 128), jnp.float32),
            pltpu.VMEM((LANES, 8, 128), jnp.float32),
            pltpu.VMEM((8, 128), jnp.float32),
            pltpu.VMEM((32, 8, 128), jnp.float32),
            pltpu.VMEM((4, 8, 128), jnp.float32),
            pltpu.VMEM((1, 128), jnp.int32),
            pltpu.VMEM((C, 128), jnp.bfloat16),
            pltpu.VMEM((8, 256), jnp.bfloat16),
            dma((STAGES, KINDS)),
            dma((STAGES, KINDS)),
            dma((STAGES,)),
            dma((STAGES,)),
            dma((STAGES,)),
            dma((8,)),
            dma((8,)),
            dma,
            dma((9,)),
            dma((9,)),
            dma((8,)),
        ],
        compiler_params=pltpu.CompilerParams(
            collective_id=0, has_side_effects=True, vmem_limit_bytes=60 * 1024 * 1024
        ),
        cost_estimate=pl.CostEstimate(
            flops=2 * 576 * 9 * C * C, bytes_accessed=40_000_000, transcendentals=2_000_000
        ),
        name="spatial",
    )(
        latents.transpose(0, 2, 1, 3), gain, shift, kernel.reshape(9, 40, C), bias, slots[None]
    )


def temporal_kernel_body(
    A,
    AX,
    clip,
    slots,
    wt,
    gain,
    shift,
    bias,
    out,
    O,
    turned,
    W,
    H,
    RF,
    HE,
    RE,
    OM,
    OX,
    BX,
    back,
    back_extra,
    scale_rows,
    slot_pad,
    w_sem,
    send,
    recv,
    own,
):
    fr = lax.axis_index("frames")
    core = lax.rem(fr, 2)
    sib = {"frames": fr + 1 - 2 * core}
    loads = [
        pltpu.make_async_copy(
            wt.at[:, :, 256 * n : 256 * n + 256], W.at[:, :, 256 * n : 256 * n + 256], w_sem.at[n]
        )
        for n in range(5)
    ]
    for load in loads:
        load.start()
    barrier = pltpu.get_barrier_semaphore()
    greet_plane(barrier, fr)

    row, col = slot_vectors(slots, slot_pad)

    def entry_slot(entry):
        return lax.shift_right_logical(entry, 4) * 4 + jnp.bitwise_and(entry, 3)

    def entry_pixel(entry):
        return jnp.bitwise_and(lax.shift_right_logical(entry, 2), 3)

    match = flag(col == entry_slot(iota((128, 512), 1)).astype(jnp.float32))
    match_t = flag(entry_slot(iota((512, 128), 0)).astype(jnp.float32) == row)

    def frame_number(line, shift_bits):
        frame = lax.shift_right_logical(line, shift_bits)
        video = jnp.bitwise_and(lax.shift_right_logical(line, shift_bits - 2), 3)
        return video * 25 + frame

    def real(line, count):
        return line < count

    line = iota((400, 128), 0)
    which = flag(frame_number(line, 4) == iota((400, 128), 1))
    pick = jnp.dot(which, match, preferred_element_type=jnp.float32)
    pixel = jnp.bitwise_and(iota((400, 512), 0), 3)
    pick = jnp.where(pixel == entry_pixel(iota((400, 512), 1)), pick, 0.0).astype(jnp.bfloat16)
    line_t = iota((128, 400), 1)
    which_t = flag(frame_number(line_t, 4) == iota((128, 400), 0))
    pick_t = jnp.dot(match_t, which_t, preferred_element_type=jnp.float32)
    pixel_t = jnp.bitwise_and(iota((512, 400), 1), 3)
    back[...] = jnp.where(pixel_t == entry_pixel(iota((512, 400), 0)), pick_t, 0.0).astype(
        jnp.bfloat16
    )
    for n in range(5):
        both = jnp.concatenate(
            [A[:, 2 * n].reshape(512, 128), A[:, 2 * n + 1].reshape(512, 128)], axis=1
        )
        both = jnp.dot(pick, both, preferred_element_type=jnp.float32).astype(jnp.bfloat16)
        RF[:, n * 256 : n * 256 + 256] = both
    grouped = clip[...] * (1.0 / 576000.0)
    mean = grouped[0:4]
    rate = lax.rsqrt(grouped[4:8] - mean * mean + EPS)
    both = jnp.concatenate([rate, mean * rate], axis=0)
    H[0] = jnp.zeros((16, C), jnp.bfloat16)
    H[26] = jnp.zeros((16, C), jnp.bfloat16)
    channels = to_channels(both)
    for l in range(LANES):
        cols = slice(l * 128, l * 128 + 128)
        wide = channels[:, cols]
        a = wide[0:4] * gain[cols].reshape(1, 128)
        b = shift[cols].reshape(1, 128) - wide[4:8] * gain[cols].reshape(1, 128)
        for o, part in ((0, a), (16, b)):
            scale_rows[o : o + 16, cols] = jnp.concatenate(
                [jnp.broadcast_to(part[v : v + 1], (4, 128)) for v in range(4)], axis=0
            )
    def one(f, carry):
        for l in range(LANES):
            cols = slice(l * 128, l * 128 + 128)
            v = RF[pl.ds(pl.multiple_of(f * 16, 16), 16), cols].astype(jnp.float32)
            v = v * scale_rows[0:16, cols] + scale_rows[16:32, cols]
            v = v * (1.0 / (1.0 + jnp.exp(-v)))
            H[f + 1, :, cols] = v.astype(jnp.bfloat16)
        return carry

    lax.fori_loop(0, 25, one, 0)
    pl.semaphore_wait(barrier, 31)

    def spread(src, dst, k):
        def one(i, carry):
            d = lax.rem(fr + i, 32)
            pltpu.make_async_remote_copy(
                src_ref=src(d),
                dst_ref=dst(fr),
                send_sem=send.at[k],
                recv_sem=recv.at[k],
                device_id={"frames": d},
                device_id_type=MESH,
            ).start()
            return carry

        lax.fori_loop(1, 32, one, 0)
        pltpu.make_async_copy(src(fr), dst(fr), own.at[k]).start()

    def collect(src, dst, k):
        pltpu.make_async_copy(src(fr), dst(fr), own.at[k]).wait()
        whole = pltpu.make_async_remote_copy(
            src_ref=src(slice(0, 31)),
            dst_ref=dst(slice(0, 31)),
            send_sem=send.at[k],
            recv_sem=recv.at[k],
            device_id=sib,
            device_id_type=MESH,
        )
        whole.wait_send()
        whole.wait_recv()

    def chunk(n):
        cols = slice(256 * n, 256 * n + 256)
        return (lambda d: OM.at[d, :, cols]), (lambda d: O.at[d, :, cols])

    def mix(n):
        cols = slice(256 * n, 256 * n + 256)
        if n < 3:
            loads[n].wait()
        total = RF[:, cols].astype(jnp.float32) + bias[cols].reshape(1, 256)
        for k in range(3):
            total = total + jnp.dot(
                H[k : k + 25].reshape(400, C), W[k, :, cols], preferred_element_type=jnp.float32
            )
        placed = jnp.dot(back[...], total.astype(jnp.bfloat16), preferred_element_type=jnp.float32)
        OM[:, :, cols] = placed.astype(jnp.bfloat16).reshape(32, 16, 256)
        spread(*chunk(n), n)

    mix(0)
    line = iota((112, 128), 0)
    which = flag((frame_number(line, 2) == iota((112, 128), 1)) & (line < 100))
    extra = jnp.dot(which, match, preferred_element_type=jnp.float32)
    extra_pixel = entry_pixel(iota((112, 512), 1))
    line_t = iota((128, 112), 1)
    which_t = flag((frame_number(line_t, 2) == iota((128, 112), 0)) & (line_t < 100))
    extra_t = jnp.dot(match_t, which_t, preferred_element_type=jnp.float32)
    extra_pixel_t = entry_pixel(iota((512, 112), 0))
    for i in range(4):
        back_extra[i] = jnp.where(extra_pixel_t == i, extra_t, 0.0).astype(jnp.bfloat16)
    for i in range(4):
        picked = jnp.where(extra_pixel == i, extra, 0.0).astype(jnp.bfloat16)
        for m in range(3):
            if 4 * m + i < LANES:
                l = 4 * m + i
                RE[:, l * 128 : l * 128 + 128] = jnp.dot(
                    picked, AX[:, m].reshape(512, 128), preferred_element_type=jnp.float32
                ).astype(jnp.bfloat16)

    HE[0:8, :] = jnp.zeros((8, C), jnp.float32)
    HE[104:128, :] = jnp.zeros((24, C), jnp.float32)
    for l in range(LANES):
        cols = slice(l * 128, l * 128 + 128)
        a8 = jnp.concatenate([scale_rows[4 * v : 4 * v + 1, cols] for v in (0, 1, 2, 3, 0, 1, 2, 3)], axis=0)
        b8 = jnp.concatenate([scale_rows[16 + 4 * v : 17 + 4 * v, cols] for v in (0, 1, 2, 3, 0, 1, 2, 3)], axis=0)
        raw = RE[:, cols].astype(jnp.float32).reshape(14, 8, 128)
        v = raw * a8[None] + b8[None]
        v = (v * (1.0 / (1.0 + jnp.exp(-v)))).reshape(112, 128)
        HE[8:108, cols] = v[0:100]
    mix(1)
    mix(2)
    loads[3].wait()
    loads[4].wait()
    half = pl.multiple_of(core * 640, 128)
    total = RE[:, pl.ds(half, 640)].astype(jnp.float32) + bias[pl.ds(half, 640)].reshape(1, 640)
    for k in range(3):
        window = HE[4 + 4 * k : 116 + 4 * k, :].astype(jnp.bfloat16)
        total = total + jnp.dot(
            window, W[k, :, pl.ds(half, 640)], preferred_element_type=jnp.float32
        )
    mixed = total.astype(jnp.bfloat16)
    for m in range(2):
        placed = jnp.zeros((512, 128), jnp.float32)
        for i in range(4):
            l = 4 * m + i
            if l < 5:
                placed = placed + jnp.dot(
                    back_extra[i],
                    mixed[:, l * 128 : l * 128 + 128],
                    preferred_element_type=jnp.float32,
                )
        OX[:, m] = placed.astype(jnp.bfloat16).reshape(32, 16, 128)
    spread((lambda d: OX.at[d]), (lambda d: BX.at[d]), 5)
    mix(3)
    mix(4)
    collect((lambda d: OX.at[d]), (lambda d: BX.at[d]), 5)
    for t in range(4):
        for l in range(LANES):
            k, m, i = l // 5, (l % 5) // 4, (l % 5) % 4
            part = [
                BX[2 * (4 * t + r) + k, m].astype(jnp.float32)[4 * i : 4 * i + 4] for r in range(4)
            ]
            O[32 + t, :, l * 128 : l * 128 + 128] = jnp.concatenate(part, axis=0).astype(
                jnp.bfloat16
            )

    def turn(n):
        collect(*chunk(n), n)

        def place(c, carry):
            for k in range(2):
                cols = slice(256 * n + 128 * k, 256 * n + 128 * k + 128)
                turned[c, k, 0:16] = O[c, :, cols].astype(jnp.float32)
                turned[c, k, 16:32] = O[c + 18, :, cols].astype(jnp.float32)
            return carry

        def fetch(c, carry):
            for k in range(2):
                cols = slice(256 * n + 128 * k, 256 * n + 128 * k + 128)
                for s in range(4):
                    out[s, c, :, cols] = turned[c, k, pl.ds(s, 8, stride=4), :].astype(jnp.bfloat16)
            return carry

        lax.fori_loop(0, 18, place, 0)
        lax.fori_loop(0, 18, fetch, 0)

    for n in range(5):
        turn(n)


def temporal_section(A, AX, clip, slots, kernel, gain, shift, bias):
    vmem = pl.BlockSpec(memory_space=pltpu.VMEM)
    anywhere = pl.BlockSpec(memory_space=pl.ANY)
    dma = pltpu.SemaphoreType.DMA
    return pl.pallas_call(
        temporal_kernel_body,
        out_shape=jax.ShapeDtypeStruct((4, 18, 8, C), jnp.bfloat16),
        in_specs=[vmem, vmem, vmem, vmem, anywhere, vmem, vmem, vmem],
        out_specs=vmem,
        scratch_shapes=[
            pltpu.VMEM((36, 16, C), jnp.bfloat16),
            pltpu.VMEM((18, 2, 32, 128), jnp.float32),
            pltpu.VMEM((3, C, C), jnp.bfloat16),
            pltpu.VMEM((27, 16, C), jnp.bfloat16),
            pltpu.VMEM((400, C), jnp.bfloat16),
            pltpu.VMEM((128, C), jnp.float32),
            pltpu.VMEM((112, C), jnp.bfloat16),
            pltpu.VMEM((32, 16, C), jnp.bfloat16),
            pltpu.VMEM((32, 2, 16, 128), jnp.bfloat16),
            pltpu.VMEM((32, 2, 16, 128), jnp.bfloat16),
            pltpu.VMEM((512, 400), jnp.bfloat16),
            pltpu.VMEM((4, 512, 112), jnp.bfloat16),
            pltpu.VMEM((32, C), jnp.float32),
            pltpu.VMEM((1, 128), jnp.int32),
            dma((5,)),
            dma((6,)),
            dma((6,)),
            dma((6,)),
        ],
        compiler_params=pltpu.CompilerParams(
            collective_id=1, has_side_effects=True, vmem_limit_bytes=56 * 1024 * 1024
        ),
        cost_estimate=pl.CostEstimate(
            flops=2 * 500 * 3 * C * C, bytes_accessed=14_000_000, transcendentals=1_000_000
        ),
        name="temporal",
    )(A, AX, clip, slots[None], kernel, gain, shift, bias)


def body(
    latents,
    first_gain,
    first_shift,
    spatial_kernel,
    spatial_bias,
    second_gain,
    second_shift,
    temporal_kernel,
    temporal_bias,
    frame_slot,
):
    main, extra, clip = spatial_section(
        latents, first_gain, first_shift, spatial_kernel, spatial_bias, frame_slot
    )
    tiles = temporal_section(
        main, extra, clip, frame_slot, temporal_kernel, second_gain, second_shift, temporal_bias
    )
    return tiles.transpose(0, 2, 1, 3)


def solution(mesh):
    in_specs = (
        P("frames", "rows", None, None),
        P(),
        P(),
        P(None, None, "frames", None),
        P(),
        P(),
        P(),
        P(),
        P(),
        P(),
    )
    out_specs = P("frames", "rows", None, None)
    return jax.shard_map(body, mesh=mesh, in_specs=in_specs, out_specs=out_specs, check_vma=False)
```
